32 devices in a mesh: dp: 16 (over z, y, x), tensor: 2 (over core).
Axes of the slice: x: 2, y: 2, z: 4, core: 2. Of those that a mesh axis runs over, the one named last changes fastest.
Arguments:
- tokens: bfloat16 [8192, 1536], P('dp'), may hold values from -6 to 6
- cotangent: bfloat16 [8192, 1536], P('dp'), may hold values from -6 to 6
- seq_offsets: int32 [6], replicated, may hold values from 0 to 5736, as said below
- block_offsets: int32 [17], replicated, may hold values from 0 to 5736, as said below
- image_mod: float32 [5, 6, 1536], replicated, may hold values from -4 to 4
- text_mod: float32 [5, 6, 1536], replicated, may hold values from -4 to 4
- image_qkv: bfloat16 [1536, 3, 1536], P('dp', None, 'tensor'), may hold values from -0.15625 to 0.15625
- text_qkv: bfloat16 [1536, 3, 1536], P('dp', None, 'tensor'), may hold values from -0.15625 to 0.15625
- image_out: bfloat16 [1536, 1536], P('tensor', 'dp'), may hold values from -0.4375 to 0.4375
- text_out: bfloat16 [1536, 1536], P('tensor', 'dp'), may hold values from -0.4375 to 0.4375
- image_fc1: bfloat16 [1536, 6144], P('dp', 'tensor'), may hold values from -0.15625 to 0.15625
- text_fc1: bfloat16 [1536, 6144], P('dp', 'tensor'), may hold values from -0.15625 to 0.15625
- image_fc2: bfloat16 [6144, 1536], P('tensor', 'dp'), may hold values from -0.109375 to 0.109375
- text_fc2: bfloat16 [6144, 1536], P('tensor', 'dp'), may hold values from -0.109375 to 0.109375
- clip_limits: float32 [24], P('tensor'), may hold values from 2 to 20
Outputs:
- mixed: bfloat16 [8192, 1536], P('dp')
- tokens_grad: float32 [8192, 1536], P('dp')
- image_mod_grad: float32 [5, 6, 1536], P(None, None, 'dp')
- text_mod_grad: float32 [5, 6, 1536], P(None, None, 'dp')
- image_qkv_grad: float32 [1536, 3, 1536], P('dp', None, 'tensor')
- text_qkv_grad: float32 [1536, 3, 1536], P('dp', None, 'tensor')
- image_out_grad: float32 [1536, 1536], P('tensor', 'dp')
- text_out_grad: float32 [1536, 1536], P('tensor', 'dp')
- image_fc1_grad: float32 [1536, 6144], P('dp', 'tensor')
- text_fc1_grad: float32 [1536, 6144], P('dp', 'tensor')
- image_fc2_grad: float32 [6144, 1536], P('tensor', 'dp')
- text_fc2_grad: float32 [6144, 1536], P('tensor', 'dp')
- head_max: float32 [24], P('tensor')
- image_clipped: bfloat16 [1536, 2, 1536], P('dp', None, 'tensor')
- text_clipped: bfloat16 [1536, 2, 1536], P('dp', None, 'tensor')
The draws below stay inside these ranges and needn't reach their ends.
Inputs may be any that keep to these rules, and one draw needn't show every extreme that they name: seq_offsets[0] = 0 and rises; each sequence has 1024 image tokens followed by 77 to 154 text tokens, and some sequence has exactly 154; the last entry, the stream's length, is always 5 * 1101 + 462 // 2 and equals the last entry of block_offsets. block_offsets[0] = 0 and rises; every block of dp holds 256 to 512 live rows, its first ones, and some block holds exactly 512; the last entry is the stream's length.
All inputs are finite; a program needn't handle non-finite values.
Results may differ from the reference program's by a relative error of at most 0.014.
Values may be sent and summed in bfloat16 or wider, within the bound.
No kernel may reach another device: no remote copies, remote signals or barrier semaphores. Data moves between devices by JAX's collectives and lax.ppermute only.
A program may use at most 448 MiB of HBM per device.

```python
import math
import jax
import jax.numpy as jnp
from jax import lax

D = 1536
HEADS = 24
HEAD = 64
FF = 6144
HD = 1536
IMG = 1024
TXT = 154
CAP = 512
SEQS = 5
ROWS = 8192
N_DP = 16


def offsets_pair(key):
    key_lengths, key_longest, key_full, key_order = jax.random.split(key, 4)
    half_text = TXT - TXT // 2
    longest = jax.random.randint(key_longest, (), 0, SEQS)
    extra_text = (SEQS - 1) * half_text // 2
    text_order = jax.random.permutation(key_lengths, max((SEQS - 1) * half_text, 1))[:(SEQS - 1) * half_text]
    text_chosen = (text_order < extra_text).astype(jnp.int32).reshape(SEQS - 1, half_text)
    text_others = TXT // 2 + jnp.sum(text_chosen, axis=1)
    seq_ids = jnp.arange(SEQS)
    text_source = jnp.minimum(jnp.where(seq_ids > longest, seq_ids - 1, seq_ids), max(SEQS - 2, 0))
    padded_others = jnp.concatenate([text_others, jnp.full((1,), TXT // 2, jnp.int32)])
    text_len = jnp.where(seq_ids == longest, TXT, padded_others[text_source])
    seq_lengths = (IMG + text_len).astype(jnp.int32)
    stream_total = jnp.sum(seq_lengths)
    half_cap = CAP // 2
    full_device = jax.random.randint(key_full, (), 0, N_DP)
    extra_rows = stream_total - (N_DP + 1) * half_cap
    slot_order = jax.random.permutation(key_order, (N_DP - 1) * half_cap)
    chosen = (slot_order < extra_rows).astype(jnp.int32).reshape(N_DP - 1, half_cap)
    others = half_cap + jnp.sum(chosen, axis=1)
    device_ids = jnp.arange(N_DP)
    source = jnp.minimum(jnp.where(device_ids > full_device, device_ids - 1, device_ids), N_DP - 2)
    counts = jnp.where(device_ids == full_device, CAP, others[source]).astype(jnp.int32)
    zero_head = jnp.zeros((1,), jnp.int32)
    seq_offsets = jnp.concatenate([zero_head, jnp.cumsum(seq_lengths).astype(jnp.int32)])
    block_offsets = jnp.concatenate([zero_head, jnp.cumsum(counts).astype(jnp.int32)])
    return (seq_offsets, block_offsets)


def draw_seq_offsets(key, part):
    return offsets_pair(key)[0]


def draw_block_offsets(key, part):
    return offsets_pair(key)[1]


def level_of(key, shape, cuts, low, largest):
    level = 1.0
    for dim, parts in cuts:
        draws = jax.random.uniform(jax.random.fold_in(jax.random.fold_in(key, 6), dim), (parts,), jnp.float32, low / len(cuts), largest / len(cuts))
        level = level * jnp.repeat(jnp.exp(draws), shape[dim] // parts).reshape((-1,) + (1,) * (len(shape) - 1 - dim))
    return level


def noise(own_key, extent, scale, most, cuts=(), kind=jnp.bfloat16):
    array = scale * jax.random.normal(own_key, extent, jnp.float32)
    if cuts:
        array = array * level_of(own_key, extent, cuts, -0.22, 0.18)
    return jnp.clip(array, -most, most).astype(kind)


def setup_inputs(seed: int = 0) -> dict:
    seeds = jax.random.split(jax.random.key(seed), 16)
    return {
        "tokens": noise(seeds[0], (ROWS, D), 1.0, 6.0, ((0, 16),)),
        "cotangent": noise(seeds[1], (ROWS, D), 1.0, 6.0, ((0, 16),)),
        "seq_offsets": draw_seq_offsets(jax.random.fold_in(seeds[15], 71), 0),
        "block_offsets": draw_block_offsets(jax.random.fold_in(seeds[15], 71), 0),
        "image_mod": noise(seeds[4], (SEQS, 6, D), 0.7, 4.0, (), jnp.float32),
        "text_mod": noise(seeds[5], (SEQS, 6, D), 0.7, 4.0, (), jnp.float32),
        "image_qkv": noise(seeds[6], (D, 3, HD), D ** -0.5, 0.15625, ((0, 16), (2, 2))),
        "text_qkv": noise(seeds[7], (D, 3, HD), D ** -0.5, 0.15625, ((0, 16), (2, 2))),
        "image_out": noise(seeds[8], (HD, D), (HD // 8) ** -0.5, 0.4375, ((0, 2), (1, 16))),
        "text_out": noise(seeds[9], (HD, D), (HD // 8) ** -0.5, 0.4375, ((0, 2), (1, 16))),
        "image_fc1": noise(seeds[10], (D, FF), D ** -0.5, 0.15625, ((0, 16), (1, 2))),
        "text_fc1": noise(seeds[11], (D, FF), D ** -0.5, 0.15625, ((0, 16), (1, 2))),
        "image_fc2": noise(seeds[12], (FF, D), (FF // 2) ** -0.5, 0.109375, ((0, 2), (1, 16))),
        "text_fc2": noise(seeds[13], (FF, D), (FF // 2) ** -0.5, 0.109375, ((0, 2), (1, 16))),
        "clip_limits": jnp.clip(jnp.exp(math.log(20.0) - 2.3025851 * jax.random.uniform(seeds[14], (HEADS,), jnp.float32) ** level_of(seeds[14], (HEADS,), ((0, 2),), -0.2, 0.2)), 2.0, 20.0),
    }


EPSILON = 1e-06
NEGATIVE = -1e+30
HIGHEST_PRECISION = lax.Precision.HIGHEST

@jax.custom_vjp
def low(v):
    return lax.optimization_barrier(v.astype(jnp.bfloat16)).astype(jnp.float32)

@jax.custom_vjp
def low_back(v):
    return v

def low_keep(v):
    return (low(v), None)

def low_pass(kept, grad):
    return (grad,)

def back_keep(v):
    return (v, None)

def back_low(kept, grad):
    return (low(grad),)
low.defvjp(low_keep, low_pass)
low_back.defvjp(back_keep, back_low)

def stream_layout(seq_offsets, block_offsets):
    slot_ids = jnp.arange(IMG + TXT, dtype=jnp.int32)
    position = seq_offsets[:SEQS, None] + slot_ids[None, :]
    is_live = position < seq_offsets[1:, None]
    is_text = (slot_ids[None, :] >= IMG) & is_live
    device_ids = lax.optimization_barrier(jnp.sum((position[:, :, None] >= block_offsets[None, None, 1:N_DP]).astype(jnp.int32), axis=2))
    row_index = device_ids * CAP + position - block_offsets[device_ids]
    row_index = jnp.where(is_live, row_index, 0).astype(jnp.int32)
    return (row_index, is_live, is_text)

def attend(operands):
    queries, keys, values, is_live = operands
    logits = low_back(jnp.einsum('qhd,khd->hqk', queries, keys, precision=HIGHEST_PRECISION) * HEAD ** (-0.5))
    pair_live = is_live[:, None] & is_live[None, :]
    head_top = lax.optimization_barrier(jnp.max(jnp.where(pair_live[None], logits, NEGATIVE), axis=(1, 2)))
    probs = low(jax.nn.softmax(jnp.where(is_live[None, None, :], logits, NEGATIVE), axis=-1))
    attended = jnp.einsum('hqk,khd->qhd', probs, values, precision=HIGHEST_PRECISION)
    return (attended, head_top)

def by_kind(inputs, image_weight, text_weight, text_flag):
    image_part = jnp.einsum('sli,io->slo', inputs, image_weight, precision=HIGHEST_PRECISION)
    text_part = jnp.einsum('sli,io->slo', inputs, text_weight, precision=HIGHEST_PRECISION)
    return jnp.where(text_flag, text_part, image_part)

def norm_rows(inputs):
    centered = inputs - lax.optimization_barrier(jnp.mean(inputs, axis=-1, keepdims=True))
    return centered * lax.rsqrt(lax.optimization_barrier(jnp.mean(centered * centered, axis=-1, keepdims=True)) + EPSILON)

def forward(stream, image_mod, text_mod, image_qkv, text_qkv, image_out, text_out, image_fc1, text_fc1, image_fc2, text_fc2, row_index, is_live, is_text):
    rows = stream[row_index]
    text_flag = is_text[:, :, None]
    modulation = jnp.where(is_text[:, :, None, None], text_mod[:, None], image_mod[:, None])
    modulated = low(norm_rows(rows) * (1.0 + modulation[:, :, 1]) + modulation[:, :, 0])
    qkv = low_back(low(by_kind(modulated, image_qkv.reshape(D, 3 * HD), text_qkv.reshape(D, 3 * HD), text_flag)))
    seq_count, seq_len = is_live.shape
    queries = qkv[:, :, :HD].reshape(seq_count, seq_len, HEADS, HEAD)
    keys = qkv[:, :, HD:2 * HD].reshape(seq_count, seq_len, HEADS, HEAD)
    values = qkv[:, :, 2 * HD:].reshape(seq_count, seq_len, HEADS, HEAD)
    attended, tops = lax.map(jax.checkpoint(attend), (queries, keys, values, is_live))
    attended = low_back(low(attended.reshape(seq_count, seq_len, HD)))
    branch = low_back(by_kind(attended, image_out, text_out, text_flag))
    first = rows + modulation[:, :, 2] * branch
    modulated_mlp = low(norm_rows(first) * (1.0 + modulation[:, :, 4]) + modulation[:, :, 3])
    before_act = low_back(by_kind(modulated_mlp, image_fc1, text_fc1, text_flag))
    hidden = low_back(low(jax.nn.gelu(before_act, approximate=True)))
    mlp_branch = low_back(by_kind(hidden, image_fc2, text_fc2, text_flag))
    mixed = first + modulation[:, :, 5] * mlp_branch
    placed = jnp.zeros(stream.shape, jnp.float32).at[row_index].add(jnp.where(is_live[:, :, None], mixed, 0.0))
    return (placed, lax.optimization_barrier(jnp.max(tops, axis=0)))

def reference(tokens, cotangent, seq_offsets, block_offsets, image_mod, text_mod, image_qkv, text_qkv, image_out, text_out, image_fc1, text_fc1, image_fc2, text_fc2, clip_limits):
    row_index, is_live, is_text = stream_layout(seq_offsets, block_offsets)

    def run(stream, image_m, text_m, image_w, text_w, image_o, text_o, image_u, text_u, image_d, text_d):
        return forward(stream, image_m, text_m, image_w, text_w, image_o, text_o, image_u, text_u, image_d, text_d, row_index, is_live, is_text)
    inputs = (tokens.astype(jnp.float32), image_mod, text_mod, image_qkv.astype(jnp.float32), text_qkv.astype(jnp.float32), image_out.astype(jnp.float32), text_out.astype(jnp.float32), image_fc1.astype(jnp.float32), text_fc1.astype(jnp.float32), image_fc2.astype(jnp.float32), text_fc2.astype(jnp.float32))
    mixed, pull, head_max = jax.vjp(run, *inputs, has_aux=True)
    grads = pull(cotangent.astype(jnp.float32))
    root_factor = jnp.sqrt(clip_limits / jnp.maximum(head_max, clip_limits))
    column_scale = jnp.repeat(root_factor, HEAD)[None, None, :]
    image_clipped = (image_qkv[:, :2, :].astype(jnp.float32) * column_scale).astype(jnp.bfloat16)
    text_clipped = (text_qkv[:, :2, :].astype(jnp.float32) * column_scale).astype(jnp.bfloat16)
    return (mixed.astype(jnp.bfloat16), grads[0], grads[1], grads[2], grads[3], grads[4], grads[5], grads[6], grads[7], grads[8], grads[9], grads[10], head_max, image_clipped, text_clipped)
```

```python
import jax
import jax.numpy as jnp
from jax import lax
from jax.experimental import pallas as pl
from jax.experimental.pallas import tpu as pltpu
from jax.sharding import Mesh, PartitionSpec as P

HEAD = 64
IMG = 1024
TXT = 154
EPSILON = 1e-06
NEGATIVE = -1e30
BLOCKS = 4
SUB = 128
TAIL = 1184
TAIL_PAD = 1280
EDGE = 160
CHUNK = 256
ALIGN = 16
BF = jnp.bfloat16
F32 = jnp.float32
SWAP = [(0, 1), (1, 0)]
VMEM_LIMIT = 60 * 1024 * 1024

VMEM = pl.BlockSpec(memory_space=pltpu.VMEM)
SMEM = pl.BlockSpec(memory_space=pltpu.SMEM)

COUNT, OFFSET, TEXT_FROM, TEXT_TO = 0, 4, 8, 12
CORE, TAIL_FROM, EDGE_FROM = 16, 17, 18


def dot(a, b):
    return jnp.dot(a, b, preferred_element_type=F32)


def dot_back(a, b):
    return lax.dot_general(a, b, (((1,), (1,)), ((), ())), preferred_element_type=F32)


def dot_rows(a, b):
    return lax.dot_general(a, b, (((0,), (0,)), ((), ())), preferred_element_type=F32)


def call(body, out_shape, n_in, scratch=(), flops=0, moved=0):
    return pl.pallas_call(
        body,
        out_shape=out_shape,
        in_specs=[SMEM] + [VMEM] * (n_in - 1),
        out_specs=jax.tree.map(lambda _: VMEM, out_shape),
        scratch_shapes=list(scratch),
        compiler_params=pltpu.CompilerParams(vmem_limit_bytes=VMEM_LIMIT),
        cost_estimate=pl.CostEstimate(flops=flops, bytes_accessed=moved, transcendentals=0),
    )


def for_tiles(info, half, body, empty=None):
    def step(j, carry):
        for side in (0, 1):
            base = (info[CORE] if side == 0 else 1 - info[CORE]) * half
            live = info[COUNT + j] - base

            @pl.when(live > SUB)
            def _():
                body(j, side, base, half)

            @pl.when((live > 0) & (live <= SUB))
            def _():
                body(j, side, base, SUB)

            if empty is not None:

                @pl.when(live <= 0)
                def _():
                    empty(j, side)

        return carry

    lax.fori_loop(0, BLOCKS, step, 0)


def row_ids(base, rows):
    return base + lax.broadcasted_iota(jnp.int32, (rows, 1), 0)


def for_text(info, j, base, rows, body):
    for u in range(rows // SUB):
        low = base + u * SUB

        @pl.when((info[TEXT_FROM + j] < low + SUB) & (info[TEXT_TO + j] > low))
        def _():
            ids = row_ids(low, SUB)
            body(u, (ids >= info[TEXT_FROM + j]) & (ids < info[TEXT_TO + j]))


def window(start, rows, total):
    base = jnp.minimum(lax.shift_right_logical(start, 4) * ALIGN, total - rows - ALIGN)
    return pl.ds(pl.multiple_of(base, ALIGN), rows + ALIGN), start - base


def moved(part, skip):
    rows = part.shape[0]
    shape = (rows + ALIGN, rows)
    there = lax.broadcasted_iota(jnp.int32, shape, 0) - skip
    return dot((there == lax.broadcasted_iota(jnp.int32, shape, 1)).astype(F32).astype(BF), part)


def read_rows(ref, start, rows):
    place, skip = window(start, rows, ref.shape[0])
    shape = (rows, rows + ALIGN)
    here = lax.broadcasted_iota(jnp.int32, shape, 1) - skip
    pick = (here == lax.broadcasted_iota(jnp.int32, shape, 0)).astype(F32).astype(BF)
    return dot(pick, ref[place, :]).astype(BF)


def slots_to_rows(info, own, oth, w_image, w_text, out, tile):
    half = own.shape[1]
    out[...] = jnp.zeros_like(out)

    def body(j, side, base, rows):
        x = (own, oth)[side]
        tile[:rows, :] = dot(x[j, :rows, :], w_image[...])

        def text(u, is_text):
            part = slice(u * SUB, (u + 1) * SUB)
            tile[part, :] = jnp.where(is_text, dot(x[j, part, :], w_text[...]), tile[part, :])

        for_text(info, j, base, rows, text)
        place, skip = window(info[OFFSET + j] + base, rows, out.shape[0])
        part = moved(tile[:rows, :].astype(BF), skip)
        ids = row_ids(base - skip, rows + ALIGN)
        stop = jnp.minimum(info[COUNT + j], base + rows)
        out[place, :] = jnp.where((ids >= base) & (ids < stop), part, out[place, :].astype(F32)).astype(BF)

    for_tiles(info, half, body)


def rows_to_slots(info, rows_ref, w_image, w_text, own, oth):
    half = own.shape[1]

    def body(j, side, base, rows):
        out = (own, oth)[side]
        x = read_rows(rows_ref, info[OFFSET + j] + base, rows)
        out[j, :rows, :] = dot_back(x, w_image[...]).astype(BF)
        if rows < half:
            out[j, rows:, :] = jnp.zeros((half - rows, out.shape[2]), BF)

        def text(u, is_text):
            part = slice(u * SUB, (u + 1) * SUB)
            out[j, part, :] = jnp.where(
                is_text, dot_back(x[part], w_text[...]).astype(BF), out[j, part, :]
            )

        for_text(info, j, base, rows, text)

    def empty(j, side):
        out = (own, oth)[side]
        out[j] = jnp.zeros(out.shape[1:], BF)

    for_tiles(info, half, body, empty)


def slots_to_slots(info, x_own, x_oth, w, own, oth):
    half = own.shape[1]
    cut = w.shape[1] // 2

    def body(j, side, base, rows):
        x, out = (x_own, x_oth)[side], (own, oth)[side]
        out[j, :rows, :] = dot_back(x[j, :rows, :], w[:, :cut]).astype(BF)
        if rows < half:
            out[j, rows:, :] = jnp.zeros((half - rows, out.shape[2]), BF)

        def text(u, is_text):
            part = slice(u * SUB, (u + 1) * SUB)
            out[j, part, :] = jnp.where(
                is_text, dot_back(x[j, part, :], w[:, cut:]).astype(BF), out[j, part, :]
            )

        for_text(info, j, base, rows, text)

    def empty(j, side):
        out = (own, oth)[side]
        out[j] = jnp.zeros(out.shape[1:], BF)

    for_tiles(info, half, body, empty)


def gelu_parts(v):
    k = 0.7978845608028654
    square = v * v
    t = jnp.tanh(k * v * (1.0 + 0.044715 * square))
    value = 0.5 * v * (1.0 + t)
    slope = 0.5 * (1.0 + t) + 0.5 * v * (1.0 - t * t) * k * (1.0 + 3 * 0.044715 * square)
    return value, slope


def mlp_core(
    info, x_own, x_oth, g_own, g_oth, upper, lower,
    gm_own, gm_oth, hid_own, hid_oth, gb_own, gb_oth,
    before, back,
):
    half = x_own.shape[1]
    cut = upper.shape[1] // 2

    def body(j, side, base, rows):
        x, g = (x_own, x_oth)[side], (g_own, g_oth)[side]
        gm, hid, gb = (gm_own, gm_oth)[side], (hid_own, hid_oth)[side], (gb_own, gb_oth)[side]
        before[:rows, :] = dot(x[j, :rows, :], upper[:, :cut])
        back[:rows, :] = dot(g[j, :rows, :], lower[:, :cut])

        def text(u, is_text):
            part = slice(u * SUB, (u + 1) * SUB)
            before[part, :] = jnp.where(is_text, dot(x[j, part, :], upper[:, cut:]), before[part, :])
            back[part, :] = jnp.where(is_text, dot(g[j, part, :], lower[:, cut:]), back[part, :])

        for_text(info, j, base, rows, text)
        value, slope = gelu_parts(before[:rows, :])
        hid[j, :rows, :] = value.astype(BF)
        gb[j, :rows, :] = (back[:rows, :].astype(BF).astype(F32) * slope).astype(BF)
        gm[j, :rows, :] = dot_back(gb[j, :rows, :], upper[:, :cut]).astype(BF)

        def text_back(u, is_text):
            part = slice(u * SUB, (u + 1) * SUB)
            gm[j, part, :] = jnp.where(
                is_text, dot_back(gb[j, part, :], upper[:, cut:]).astype(BF), gm[j, part, :]
            )

        for_text(info, j, base, rows, text_back)
        if rows < half:
            for ref in (gm, hid, gb):
                ref[j, rows:, :] = jnp.zeros((half - rows, ref.shape[2]), BF)

    def empty(j, side):
        for ref in ((gm_own, gm_oth)[side], (hid_own, hid_oth)[side], (gb_own, gb_oth)[side]):
            ref[j] = jnp.zeros(ref.shape[1:], BF)

    for_tiles(info, half, body, empty)


def weight_sums(info, half, left_of, right_of, acc_image, acc_text):
    acc_image[...] = jnp.zeros_like(acc_image)
    acc_text[...] = jnp.zeros_like(acc_text)

    def body(j, side, base, rows):
        left, right = left_of(j, side, base, rows), right_of(j, side, base, rows)
        ids = row_ids(base, rows)
        is_text = (ids >= info[TEXT_FROM + j]) & (ids < info[TEXT_TO + j])
        is_image = (ids < info[COUNT + j]) & jnp.logical_not(is_text)
        acc_image[...] += dot_rows(left, jnp.where(is_image, right, 0).astype(BF))

        def text(u, hit):
            part = slice(u * SUB, (u + 1) * SUB)
            acc_text[...] += dot_rows(left[part], jnp.where(hit, right[part], 0).astype(BF))

        for_text(info, j, base, rows, text)

    for_tiles(info, half, body)


def sums_of_slots(info, l_own, l_oth, r_own, r_oth, out, acc_image, acc_text):
    cut = acc_image.shape[1]
    weight_sums(
        info,
        l_own.shape[1],
        lambda j, side, base, rows: (l_own, l_oth)[side][j, :rows, :],
        lambda j, side, base, rows: (r_own, r_oth)[side][j, :rows, :].astype(F32),
        acc_image,
        acc_text,
    )
    out[:, :cut] = acc_image[...].astype(BF)
    out[:, cut:] = acc_text[...].astype(BF)


def sums_of_rows(info, l_own, l_oth, right, image, text, acc_image, acc_text):
    weight_sums(
        info,
        l_own.shape[1],
        lambda j, side, base, rows: (l_own, l_oth)[side][j, :rows, :],
        lambda j, side, base, rows: read_rows(right, info[OFFSET + j] + base, rows).astype(F32),
        acc_image,
        acc_text,
    )
    image[...] = acc_image[...].astype(BF)
    text[...] = acc_text[...].astype(BF)


def head_rows(turned, h):
    ids = lax.broadcasted_iota(jnp.int32, turned.shape, 0)
    return jnp.where((ids >= h * HEAD) & (ids < (h + 1) * HEAD), turned, 0)


def head_columns(plain, h):
    ids = lax.broadcasted_iota(jnp.int32, plain.shape, 1)
    return jnp.where((ids >= h * HEAD) & (ids < (h + 1) * HEAD), plain, 0)


def chunk_mask(chunks, i, n_chunks, q_from, q_to):
    position = chunks[i] + lax.broadcasted_iota(jnp.int32, (CHUNK, 1), 0)
    valid = (position >= chunks[n_chunks + i]) & (position < chunks[2 * n_chunks + i])
    position = jnp.where(valid, position, -1)
    return (position >= q_from) & (position < q_to)


def for_chunks(chunks, n_chunks, t, body):
    low, high = chunks[3 * n_chunks + 2 * t], chunks[3 * n_chunks + 2 * t + 1]

    def step(i, carry):
        start = jnp.maximum(chunks[i], chunks[n_chunks + i])
        stop = jnp.minimum(chunks[i] + CHUNK, chunks[2 * n_chunks + i])

        @pl.when((start < high) & (stop > low) & (start < stop))
        def _():
            body(i)

        return carry

    lax.fori_loop(0, n_chunks, step, 0)


def attend_kernel(chunks, q, k, v, q_from, q_to, out, exact, lse, top, v_turned, logits, total, high):
    t = pl.program_id(0)
    n_chunks = k.shape[0] // CHUNK
    heads = q.shape[1] // HEAD

    @pl.when(t == 0)
    def _():
        for i in range(n_chunks):
            part = slice(i * CHUNK, (i + 1) * CHUNK)
            v_turned[:, part] = v[part, :].T
        top[...] = jnp.full_like(top, NEGATIVE)

    live = chunks[3 * n_chunks + 2 * t + 1] > 0

    @pl.when(live)
    def _():
        turned = (q[...].astype(F32) * HEAD**-0.5).T
        per_head = [head_rows(turned, h).astype(BF) for h in range(heads)]
        lanes_from, lanes_to = q_from[0], q_to[0]
        total[...] = jnp.zeros_like(total)
        high[...] = jnp.full_like(high, NEGATIVE)

        def first(i):
            keys = k[pl.ds(pl.multiple_of(i * CHUNK, CHUNK), CHUNK), :]
            mask = chunk_mask(chunks, i, n_chunks, lanes_from, lanes_to)
            for h in range(heads):
                part = jnp.where(mask, dot(keys, per_head[h]), NEGATIVE)
                logits[h, i] = part
                high[h : h + 1, :] = jnp.maximum(high[h : h + 1, :], jnp.max(part, axis=0, keepdims=True))

        for_chunks(chunks, n_chunks, t, first)
        tops = [high[h : h + 1, :] for h in range(heads)]

        def second(i):
            for h in range(heads):
                part = jnp.exp(logits[h, i] - tops[h])
                high[8 + h : 9 + h, :] += jnp.sum(part, axis=0, keepdims=True)
                rows = slice(h * HEAD, (h + 1) * HEAD)
                values = v_turned[rows, pl.ds(pl.multiple_of(i * CHUNK, CHUNK), CHUNK)]
                total[rows, :] += dot(values, part.astype(BF))

        high[8:, :] = jnp.zeros((8, high.shape[1]), F32)
        for_chunks(chunks, n_chunks, t, second)
        for h in range(heads):
            rows = slice(h * HEAD, (h + 1) * HEAD)
            sums = high[8 + h : 9 + h, :]
            total[rows, :] = total[rows, :] / sums
            lse[0, h : h + 1, :] = tops[h] + jnp.log(sums)
            seen = jnp.where(lanes_to > lanes_from, tops[h], NEGATIVE)
            top[h : h + 1, :] = jnp.maximum(top[h : h + 1, :], seen)
        result = total[...].T
        exact[...] = result
        out[...] = result.astype(BF)

    @pl.when(jnp.logical_not(live))
    def _():
        exact[...] = jnp.zeros_like(exact)
        out[...] = jnp.zeros_like(out)
        lse[...] = jnp.zeros_like(lse)


def attend_back_kernel(
    chunks, q, g, attended, k, v, lse, q_from, q_to, dq, dk, dv, k_turned, q_stack, g_stack, total
):
    t = pl.program_id(0)
    n_chunks = k.shape[0] // CHUNK
    heads = q.shape[1] // HEAD
    wide = q.shape[0]

    @pl.when(t == 0)
    def _():
        for i in range(n_chunks):
            part = slice(i * CHUNK, (i + 1) * CHUNK)
            k_turned[:, part] = k[part, :].T
        dk[...] = jnp.zeros_like(dk)
        dv[...] = jnp.zeros_like(dv)

    live = chunks[3 * n_chunks + 2 * t + 1] > 0

    @pl.when(live)
    def _():
        scaled = q[...].astype(F32) * HEAD**-0.5
        grads = g[...].astype(F32)
        q_turned, g_turned = scaled.T, grads.T
        product = g_turned * attended[...].T
        q_heads, g_heads, delta, logs = [], [], [], []
        for h in range(heads):
            rows = slice(h * wide, (h + 1) * wide)
            q_stack[rows, :] = head_columns(scaled, h).astype(BF)
            g_stack[rows, :] = head_columns(grads, h).astype(BF)
            q_heads.append(head_rows(q_turned, h).astype(BF))
            g_heads.append(head_rows(g_turned, h).astype(BF))
            delta.append(jnp.sum(product[h * HEAD : (h + 1) * HEAD, :], axis=0, keepdims=True))
            logs.append(lse[0, h : h + 1, :])
        lanes_from, lanes_to = q_from[0], q_to[0]
        total[...] = jnp.zeros_like(total)

        def body(i):
            place = pl.ds(pl.multiple_of(i * CHUNK, CHUNK), CHUNK)
            keys, values = k[place, :], v[place, :]
            mask = chunk_mask(chunks, i, n_chunks, lanes_from, lanes_to)
            probs, grad_logits = [], []
            for h in range(heads):
                part = jnp.where(mask, jnp.exp(dot(keys, q_heads[h]) - logs[h]), 0.0)
                back = (part * (dot(values, g_heads[h]) - delta[h])).astype(BF)
                probs.append(part.astype(BF))
                grad_logits.append(back)
                rows = slice(h * HEAD, (h + 1) * HEAD)
                total[rows, :] += dot(k_turned[rows, place], back)
            dv[place, :] += dot(jnp.concatenate(probs, axis=1), g_stack[...])
            dk[place, :] += dot(jnp.concatenate(grad_logits, axis=1), q_stack[...])

        for_chunks(chunks, n_chunks, t, body)
        dq[...] = total[...].T * HEAD**-0.5

    @pl.when(jnp.logical_not(live))
    def _():
        dq[...] = jnp.zeros_like(dq)


def gather_grads_kernel(info, dq, dk, dv, near_back, near_on, far_back, far_on, out, keys, values):
    width = dq.shape[1]
    keys[...] = dk[...]
    values[...] = dv[...]

    def add(place, part):
        keys[place, :] += part[:, :width]
        values[place, :] += part[:, width:]

    for start, part in ((info[TAIL_FROM], near_back), (info[EDGE_FROM], far_back)):
        place, skip = window(start, part.shape[0], keys.shape[0])
        add(place, moved(part[...], skip))
    add(pl.ds(0, TAIL), near_on[...].astype(F32))
    add(pl.ds(0, EDGE), far_on[...].astype(F32))
    out[...] = jnp.concatenate([dq[...], keys[...], values[...]], axis=1).astype(BF)


def shift(value, steps):
    count = lax.axis_size("g")
    pairs = [(i, i + steps) for i in range(count) if 0 <= i + steps < count]
    if not pairs:
        return jnp.zeros_like(value)
    return lax.ppermute(value, "g", pairs)


def over_x(value):
    return lax.ppermute(value, "x", SWAP)


def over_y(value):
    return lax.ppermute(value, "y", SWAP)


def over_core(value):
    return lax.ppermute(value, "c", SWAP)


def over_xy(value):
    return lax.ppermute(value, ("y", "x"), [(0, 3), (1, 2), (2, 1), (3, 0)])


def spread(value):
    cut = value.shape[0] // 2
    from_x, from_y = over_x(value), over_y(value)
    far = jnp.concatenate([over_y(from_x[:cut]), over_x(from_y[cut:])], axis=0)
    own = jnp.stack([value, from_x, from_y, far])
    return own, over_core(own)


def add16(*parts):
    total = parts[0].astype(F32)
    for part in parts[1:]:
        total = total + part.astype(F32)
    return total


def collect(own, oth):
    cut = own.shape[1] // 2
    part = add16(own, over_core(oth)).astype(BF)
    to_x, to_y, far = part[1], part[2], part[3]
    from_x, from_y = over_x(far[:cut]), over_y(far[cut:])
    first_x = over_x(to_x[:cut])
    first_y = over_y(to_y[cut:])
    last_x = over_x(add16(to_x[cut:], from_y).astype(BF))
    last_y = over_y(add16(to_y[:cut], from_x).astype(BF))
    low = add16(part[0, :cut], first_x, last_y)
    high = add16(part[0, cut:], last_x, first_y)
    return jnp.concatenate([low, high], axis=0)


def layer_norm(inputs):
    centered = inputs - jnp.mean(inputs, axis=1, keepdims=True)
    inverse_std = lax.rsqrt(jnp.mean(centered * centered, axis=1, keepdims=True) + EPSILON)
    return (centered * inverse_std, inverse_std)


def norm_back(grad_normed, normed, inverse_std):
    return inverse_std * (
        grad_normed
        - jnp.mean(grad_normed, axis=1, keepdims=True)
        - normed * jnp.mean(grad_normed * normed, axis=1, keepdims=True)
    )


def exchange_pieces(pieces, q):
    pick = lambda j: lax.dynamic_index_in_dim(pieces, q ^ j, 0, keepdims=False)
    got = jnp.stack([pick(0), over_x(pick(1)), over_y(pick(2)), over_xy(pick(3))])
    return jnp.stack([lax.dynamic_index_in_dim(got, q ^ b, 0, keepdims=False) for b in range(BLOCKS)])


def local(
    tokens,
    cotangent,
    seq_offsets,
    block_offsets,
    image_mod,
    text_mod,
    image_qkv,
    text_qkv,
    image_out,
    text_out,
    image_fc1,
    text_fc1,
    image_fc2,
    text_fc2,
    clip_limits,
):
    rows_cap, width = tokens.shape
    half = rows_cap // 2
    share = image_qkv.shape[0]
    columns = image_qkv.shape[2]
    group_rows = BLOCKS * rows_cap
    mine = columns // BLOCKS
    heads = mine // HEAD
    seq_count = seq_offsets.shape[0] - 1
    n_groups = lax.axis_size("g")
    g, c = lax.axis_index("g"), lax.axis_index("c")
    q = 2 * lax.axis_index("y") + lax.axis_index("x")
    device = g * BLOCKS + q

    def quarter(inputs):
        return jnp.moveaxis(inputs.reshape(share, -1, BLOCKS, mine), 2, 0).reshape(BLOCKS, share, -1)

    def quarter_turned(inputs):
        return jnp.swapaxes(inputs.reshape(BLOCKS, -1, share), 1, 2)

    def quarter_wide(inputs):
        return jnp.swapaxes(inputs.reshape(share, BLOCKS, -1), 0, 1)

    pack_qkv = jnp.concatenate([quarter(image_qkv), quarter(text_qkv)], axis=2)
    pack_rest = jnp.concatenate(
        [
            quarter_wide(image_fc1),
            quarter_wide(text_fc1),
            quarter_turned(image_fc2),
            quarter_turned(text_fc2),
            quarter_turned(image_out),
            quarter_turned(text_out),
        ],
        axis=2,
    )
    fc = image_fc1.shape[1] // BLOCKS
    plane_qkv = exchange_pieces(pack_qkv, q).reshape(BLOCKS * share, -1)
    plane_rest = exchange_pieces(pack_rest, q).reshape(BLOCKS * share, -1)
    whole_qkv = lax.all_gather(plane_qkv, "g", axis=0, tiled=True)
    whole_out = lax.all_gather(plane_rest[:, 4 * fc :], "g", axis=0, tiled=True)
    whole_fc1 = lax.all_gather(plane_rest[:, : 2 * fc], "g", axis=0, tiled=True)
    whole_fc2 = lax.all_gather(plane_rest[:, 2 * fc : 4 * fc], "g", axis=0, tiled=True)
    qkv_image, qkv_text = whole_qkv[:, : 3 * mine], whole_qkv[:, 3 * mine :]
    out_image, out_text = whole_out[:, :mine], whole_out[:, mine:]

    group_from = block_offsets[:: BLOCKS]
    own_from, own_to = block_offsets[device], block_offsets[device + 1]
    start, stop = group_from[g], group_from[g + 1]
    live_rows = stop - start
    members = g * BLOCKS + (q ^ jnp.arange(BLOCKS, dtype=jnp.int32))
    member_from, member_to = block_offsets[members], block_offsets[members + 1]
    text_low = jnp.maximum(seq_offsets[None, :-1] + IMG, member_from[:, None])
    text_high = jnp.minimum(seq_offsets[None, 1:], member_to[:, None])
    has_text = text_low < text_high
    text_from = jnp.sum(jnp.where(has_text, text_low - member_from[:, None], 0), axis=1)
    text_to = jnp.sum(jnp.where(has_text, text_high - member_from[:, None], 0), axis=1)
    tail_from = jnp.maximum(live_rows - TAIL, 0)
    edge_from = jnp.maximum(live_rows - EDGE, 0)
    info = jnp.concatenate(
        [
            member_to - member_from,
            member_from - start,
            text_from,
            text_to,
            jnp.stack([c, tail_from, edge_from]),
        ]
    ).astype(jnp.int32)

    def group_span(steps):
        there = (g + steps >= 0) & (g + steps < n_groups)
        at = jnp.clip(g + steps, 0, n_groups - 1)
        return jnp.where(there, group_from[at], 0), jnp.where(there, group_from[at + 1], 0)

    def region(base, low, high, rows):
        n = rows // CHUNK
        steps = jnp.arange(n, dtype=jnp.int32) * CHUNK
        return base + steps, jnp.full((n,), 0, jnp.int32) + low, jnp.full((n,), 0, jnp.int32) + high

    spans = {steps: group_span(steps) for steps in (-2, -1, 1, 2)}
    regions = [
        region(jnp.maximum(spans[-2][1] - EDGE, spans[-2][0]), *spans[-2], CHUNK),
        region(jnp.maximum(spans[-1][1] - TAIL, spans[-1][0]), *spans[-1], TAIL_PAD),
        region(start, start, stop, group_rows),
        region(spans[1][0], spans[1][0], jnp.minimum(spans[1][1], spans[1][0] + TAIL), TAIL_PAD),
        region(spans[2][0], spans[2][0], jnp.minimum(spans[2][1], spans[2][0] + EDGE), CHUNK),
    ]
    n_tiles = group_rows // CHUNK
    position = start + jnp.arange(group_rows, dtype=jnp.int32)
    row_seq = jnp.sum((position[:, None] >= seq_offsets[None, 1:-1]).astype(jnp.int32), axis=1)
    seq_hit = row_seq[:, None] == jnp.arange(seq_count)[None, :]
    row_live = position < stop
    rows_from = jnp.where(row_live, jnp.sum(jnp.where(seq_hit, seq_offsets[None, :-1], 0), axis=1), 0)
    rows_to = jnp.where(row_live, jnp.sum(jnp.where(seq_hit, seq_offsets[None, 1:], 0), axis=1), 0)
    rows_from = rows_from.reshape(n_tiles, 1, CHUNK).astype(jnp.int32)
    rows_to = rows_to.reshape(n_tiles, 1, CHUNK).astype(jnp.int32)
    tile_span = jnp.stack([rows_from[:, 0, 0], jnp.max(rows_to[:, 0, :], axis=1)], axis=1).reshape(-1)
    chunks = jnp.concatenate([part for field in zip(*regions) for part in field] + [tile_span]).astype(jnp.int32)

    my_rows = lambda inputs: lax.dynamic_slice_in_dim(inputs, c * half, half, 0)
    ids = c * half + jnp.arange(half, dtype=jnp.int32)
    is_live = (ids < own_to - own_from)[:, None]
    my_seq = jnp.sum((own_from >= seq_offsets[1:-1]).astype(jnp.int32))
    next_seq = jnp.minimum(my_seq + 1, seq_count - 1)
    is_text = (is_live[:, 0] & (ids >= text_from[0]) & (ids < text_to[0]))[:, None]
    is_next = is_live & (own_from + ids >= seq_offsets[my_seq + 1])[:, None]
    vectors = (image_mod[my_seq], text_mod[my_seq], image_mod[next_seq])

    def modulation(which):
        return jnp.where(
            is_text, vectors[1][which][None], jnp.where(is_next, vectors[2][which][None], vectors[0][which][None])
        )

    shift_rows, scale_rows, gate_rows, shift_mlp, scale_mlp, gate_mlp = (modulation(i) for i in range(6))
    stream = my_rows(tokens).astype(F32)
    grad_stream = jnp.where(is_live, my_rows(cotangent).astype(F32), 0.0)
    normed, inverse_std = layer_norm(stream)
    modulated = (normed * (1.0 + scale_rows) + shift_rows).astype(BF)
    grad_mlp = (gate_mlp * grad_stream).astype(BF)

    slot = lambda n: jax.ShapeDtypeStruct((BLOCKS, half, n), BF)
    rows_of = lambda n, kind: jax.ShapeDtypeStruct((group_rows, n), kind)
    work = lambda n, k: 2 * (group_rows * 3 // 4) * n * k
    mod_own, mod_oth = spread(modulated)
    qkv = call(
        slots_to_rows,
        rows_of(3 * mine, BF),
        5,
        [pltpu.VMEM((half, 3 * mine), F32)],
        work(width, 3 * mine),
        12_000_000,
    )(info, mod_own, mod_oth, qkv_image, qkv_text)

    queries = qkv[:, :mine]
    pairs = qkv[:, mine:]
    tail = lax.dynamic_slice_in_dim(pairs, tail_from, TAIL, 0)
    edge = lax.dynamic_slice_in_dim(pairs, edge_from, EDGE, 0)
    near_back, near_on = shift(tail, 1), shift(pairs[:TAIL], -1)
    far_back, far_on = shift(edge, 2), shift(pairs[:EDGE], -2)
    blank = lambda n: jnp.zeros((n, 2 * mine), BF)
    around = jnp.concatenate(
        [
            far_back,
            blank(CHUNK - EDGE),
            near_back,
            blank(TAIL_PAD - TAIL),
            pairs,
            near_on,
            blank(TAIL_PAD - TAIL),
            far_on,
            blank(CHUNK - EDGE),
        ],
        axis=0,
    )
    keys, values = around[:, :mine], around[:, mine:]
    reach = keys.shape[0]
    n_chunks = reach // CHUNK

    tile_spec = pl.BlockSpec((CHUNK, mine), lambda t: (t, 0))
    all_spec = pl.BlockSpec((reach, mine), lambda t: (0, 0))
    lane_spec = pl.BlockSpec((1, 1, CHUNK), lambda t: (t, 0, 0))
    log_spec = pl.BlockSpec((1, 8, CHUNK), lambda t: (t, 0, 0))
    pair_work = 2 * heads * group_rows * 3 // 4 * 1280 * 256
    attended, attended_exact, logs, tops = pl.pallas_call(
        attend_kernel,
        grid=(n_tiles,),
        out_shape=(
            rows_of(mine, BF),
            rows_of(mine, F32),
            jax.ShapeDtypeStruct((n_tiles, 8, CHUNK), F32),
            jax.ShapeDtypeStruct((8, CHUNK), F32),
        ),
        in_specs=[SMEM, tile_spec, all_spec, all_spec, lane_spec, lane_spec],
        out_specs=(tile_spec, tile_spec, log_spec, pl.BlockSpec((8, CHUNK), lambda t: (0, 0))),
        scratch_shapes=[
            pltpu.VMEM((mine, reach), BF),
            pltpu.VMEM((heads, n_chunks, CHUNK, CHUNK), F32),
            pltpu.VMEM((mine, CHUNK), F32),
            pltpu.VMEM((16, CHUNK), F32),
        ],
        compiler_params=pltpu.CompilerParams(vmem_limit_bytes=VMEM_LIMIT),
        cost_estimate=pl.CostEstimate(flops=2 * pair_work, bytes_accessed=8_000_000, transcendentals=8_000_000),
    )(chunks, queries, keys, values, rows_from, rows_to)

    head_top = jnp.max(tops[:heads], axis=1)
    spot = jnp.arange(BLOCKS)[:, None] == q
    head_max = lax.pmax(jnp.where(spot, head_top[None, :], NEGATIVE).reshape(-1), ("g", "y", "x"))

    sent = call(rows_to_slots, (slot(width), slot(width)), 4, (), work(width, mine), 9_000_000)(
        info, attended, out_image, out_text
    )
    branch = collect(*sent)
    first = stream + gate_rows * branch
    normed_mlp, inverse_mlp = layer_norm(first)
    modulated_mlp = (normed_mlp * (1.0 + scale_mlp) + shift_mlp).astype(BF)

    gmlp_own, gmlp_oth = spread(grad_mlp)
    mm_own, mm_oth = spread(modulated_mlp)
    gm_own, gm_oth, hid_own, hid_oth, gb_own, gb_oth = call(
        mlp_core,
        (slot(width), slot(width), slot(fc), slot(fc), slot(fc), slot(fc)),
        7,
        [pltpu.VMEM((half, fc), F32), pltpu.VMEM((half, fc), F32)],
        work(width, 3 * fc),
        35_000_000,
    )(info, mm_own, mm_oth, gmlp_own, gmlp_oth, whole_fc1, whole_fc2)
    grad_mod_mlp = collect(gm_own, gm_oth)

    def slot_sums(left, right):
        return call(
            sums_of_slots,
            jax.ShapeDtypeStruct((width, 2 * fc), BF),
            5,
            [pltpu.VMEM((width, fc), F32), pltpu.VMEM((width, fc), F32)],
            work(width, fc),
            15_000_000,
        )(info, *left, *right)

    def row_sums(left, right):
        n = right.shape[1]
        return jnp.concatenate(
            call(
                sums_of_rows,
                (jax.ShapeDtypeStruct((width, n), BF), jax.ShapeDtypeStruct((width, n), BF)),
                4,
                [pltpu.VMEM((width, n), F32), pltpu.VMEM((width, n), F32)],
                work(width, n),
                12_000_000,
            )(info, *left, right),
            axis=1,
        )

    fc2_sums = slot_sums((gmlp_own, gmlp_oth), (hid_own, hid_oth))
    fc1_sums = slot_sums((mm_own, mm_oth), (gb_own, gb_oth))
    mlp_sent = call(slots_to_slots, (slot(width), slot(width)), 4, (), work(width, fc), 12_000_000)(
        info, hid_own, hid_oth, whole_fc2
    )
    mlp_branch = collect(*mlp_sent)
    mixed_rows = jnp.where(is_live, first + gate_mlp * mlp_branch, 0.0).astype(BF)

    grad_first = jnp.where(
        is_live,
        grad_stream + norm_back(grad_mod_mlp * (1.0 + scale_mlp), normed_mlp, inverse_mlp),
        0.0,
    )
    grad_branch = (gate_rows * grad_first).astype(BF)
    gbr_own, gbr_oth = spread(grad_branch)
    grad_attended = call(
        slots_to_rows,
        rows_of(mine, BF),
        5,
        [pltpu.VMEM((half, mine), F32)],
        work(width, mine),
        8_000_000,
    )(info, gbr_own, gbr_oth, out_image, out_text)
    out_sums = row_sums((gbr_own, gbr_oth), attended)

    dq, dk, dv = pl.pallas_call(
        attend_back_kernel,
        grid=(n_tiles,),
        out_shape=(
            rows_of(mine, F32),
            jax.ShapeDtypeStruct((reach, mine), F32),
            jax.ShapeDtypeStruct((reach, mine), F32),
        ),
        in_specs=[SMEM, tile_spec, tile_spec, tile_spec, all_spec, all_spec, log_spec, lane_spec, lane_spec],
        out_specs=(tile_spec, all_spec, all_spec),
        scratch_shapes=[
            pltpu.VMEM((mine, reach), BF),
            pltpu.VMEM((heads * CHUNK, mine), BF),
            pltpu.VMEM((heads * CHUNK, mine), BF),
            pltpu.VMEM((mine, CHUNK), F32),
        ],
        compiler_params=pltpu.CompilerParams(vmem_limit_bytes=VMEM_LIMIT),
        cost_estimate=pl.CostEstimate(flops=5 * pair_work, bytes_accessed=20_000_000, transcendentals=8_000_000),
    )(chunks, queries, grad_attended, attended_exact, keys, values, logs, rows_from, rows_to)

    both = lambda a, n: jnp.concatenate([dk[a : a + n], dv[a : a + n]], axis=1).astype(BF)
    at_own = CHUNK + TAIL_PAD
    at_next = at_own + group_rows
    back_near = shift(both(CHUNK, TAIL), -1)
    on_near = shift(both(at_next, TAIL), 1)
    back_far = shift(both(0, EDGE), -2)
    on_far = shift(both(at_next + TAIL_PAD, EDGE), 2)
    grad_qkv = call(
        gather_grads_kernel,
        rows_of(3 * mine, BF),
        8,
        [pltpu.VMEM((group_rows, mine), F32), pltpu.VMEM((group_rows, mine), F32)],
        0,
        20_000_000,
    )(
        info,
        dq,
        dk[at_own:at_next],
        dv[at_own:at_next],
        back_near,
        on_near,
        back_far,
        on_far,
    )
    mod_sent = call(
        rows_to_slots, (slot(width), slot(width)), 4, (), work(width, 3 * mine), 12_000_000
    )(info, grad_qkv, qkv_image, qkv_text)
    grad_modulated = collect(*mod_sent)
    qkv_sums = row_sums((mod_own, mod_oth), grad_qkv)

    tokens_grad_rows = jnp.where(
        is_live,
        grad_first + norm_back(grad_modulated * (1.0 + scale_rows), normed, inverse_std),
        0.0,
    )

    def scattered(sums):
        part = lax.psum_scatter(sums, "g", scatter_dimension=0, tiled=True)
        return exchange_pieces(part.reshape(BLOCKS, share, -1), q)

    fc2_back, fc1_back = scattered(fc2_sums), scattered(fc1_sums)
    out_back, qkv_back = scattered(out_sums), scattered(qkv_sums)

    def qkv_out(part):
        return jnp.transpose(part.reshape(BLOCKS, share, 3, mine), (1, 2, 0, 3)).reshape(share, 3, columns).astype(F32)

    def turned_out(part):
        return jnp.swapaxes(part, 1, 2).reshape(-1, share).astype(F32)

    def wide_out(part):
        return jnp.swapaxes(part, 0, 1).reshape(share, -1).astype(F32)

    picks = jnp.concatenate(
        [is_live & ~is_text & ~is_next, is_text, is_next & ~is_text, jnp.zeros((half, 5), bool)], axis=1
    ).astype(F32)
    terms = (
        grad_modulated,
        grad_modulated * normed,
        grad_first * branch,
        grad_mod_mlp,
        grad_mod_mlp * normed_mlp,
        grad_stream * mlp_branch,
    )
    sums = jnp.stack(
        [
            lax.dot_general(
                picks,
                jnp.where(is_live, term, 0.0),
                (((0,), (0,)), ((), ())),
                precision=lax.Precision.HIGHEST,
                preferred_element_type=F32,
            )
            for term in terms
        ],
        axis=1,
    )
    seq_ids = jnp.arange(seq_count)[:, None, None]
    image_part = jnp.where(seq_ids == my_seq, sums[0][None], 0.0) + jnp.where(
        (seq_ids == next_seq) & (next_seq > my_seq), sums[2][None], 0.0
    )
    text_part = jnp.where(seq_ids == my_seq, sums[1][None], 0.0)
    mod_part = jnp.concatenate([image_part, text_part], axis=0).reshape(2 * seq_count * 6, -1, share)
    mod_part = jnp.swapaxes(mod_part, 0, 1)
    mod_part = mod_part + over_core(mod_part)
    mod_sum = lax.psum_scatter(mod_part, ("g", "y", "x"), scatter_dimension=0, tiled=True)
    mod_sum = mod_sum.reshape(2, seq_count, 6, share)

    def both_halves(rows):
        other = over_core(rows)
        return jnp.where(c == 0, jnp.concatenate([rows, other], axis=0), jnp.concatenate([other, rows], axis=0))

    root_factor = jnp.sqrt(clip_limits / jnp.maximum(head_max, clip_limits))
    column_scale = jnp.repeat(root_factor, HEAD)[None, None, :]
    image_clipped = (image_qkv[:, :2, :].astype(F32) * column_scale).astype(BF)
    text_clipped = (text_qkv[:, :2, :].astype(F32) * column_scale).astype(BF)
    return (
        both_halves(mixed_rows),
        both_halves(tokens_grad_rows),
        mod_sum[0],
        mod_sum[1],
        qkv_out(qkv_back[:, :, : 3 * mine]),
        qkv_out(qkv_back[:, :, 3 * mine :]),
        turned_out(out_back[:, :, :mine]),
        turned_out(out_back[:, :, mine:]),
        wide_out(fc1_back[:, :, :fc]),
        wide_out(fc1_back[:, :, fc:]),
        turned_out(fc2_back[:, :, :fc]),
        turned_out(fc2_back[:, :, fc:]),
        head_max,
        image_clipped,
        text_clipped,
    )


def solution(mesh):
    devices = mesh.devices
    split = Mesh(devices.reshape(devices.shape[0] // BLOCKS, 2, 2, devices.shape[1]), ("g", "y", "x", "c"))
    dp = ("g", "y", "x")
    placed = (
        P(dp, None),
        P(dp, None),
        P(),
        P(),
        P(),
        P(),
        P(dp, None, "c"),
        P(dp, None, "c"),
        P("c", dp),
        P("c", dp),
        P(dp, "c"),
        P(dp, "c"),
        P("c", dp),
        P("c", dp),
        P("c"),
    )
    return jax.shard_map(
        local,
        mesh=split,
        in_specs=placed,
        out_specs=(
            P(dp, None),
            P(dp, None),
            P(None, None, dp),
            P(None, None, dp),
            P(dp, None, "c"),
            P(dp, None, "c"),
            P("c", dp),
            P("c", dp),
            P(dp, "c"),
            P(dp, "c"),
            P("c", dp),
            P("c", dp),
            P("c"),
            P(dp, None, "c"),
            P(dp, None, "c"),
        ),
        check_vma=False,
    )
```

```python
import functools

import jax
import jax.numpy as jnp
from jax import lax
from jax.experimental import pallas as pl
from jax.experimental.pallas import tpu as pltpu
from jax.sharding import Mesh, PartitionSpec as P

HEAD = 64
IMG = 1024
TXT = 154
EPSILON = 1e-06
NEGATIVE = -1e30
BLOCKS = 4
SUB = 128
TAIL = 1184
TAIL_PAD = 1536
EDGE = 160
CHUNK = 256
KEYS = 512
SLAB = 64
ALIGN = 16
TEXT_ROWS = 176
BF = jnp.bfloat16
F32 = jnp.float32
SWAP = [(0, 1), (1, 0)]
VMEM_LIMIT = 60 * 1024 * 1024

VMEM = pl.BlockSpec(memory_space=pltpu.VMEM)
SMEM = pl.BlockSpec(memory_space=pltpu.SMEM)
ANY = pl.BlockSpec(memory_space=pl.ANY)

COUNT, OFFSET, TEXT_FROM, TEXT_TO = 0, 4, 8, 12
CORE, TAIL_FROM, EDGE_FROM, OWN_FROM, OWN_SEQ, NEXT_FROM, INFO = 16, 17, 18, 19, 20, 21, 22


def dot(a, b):
    return jnp.dot(a, b, preferred_element_type=F32)


def dot_back(a, b):
    return lax.dot_general(a, b, (((1,), (1,)), ((), ())), preferred_element_type=F32)


def dot_rows(a, b):
    return lax.dot_general(a, b, (((0,), (0,)), ((), ())), preferred_element_type=F32)


def took_us(time):
    return pl.CostEstimate(flops=int(time * 1.15e9), bytes_accessed=int(time * 1e6), transcendentals=0)


def after(body, n_in, n_deps):
    return lambda *refs: body(*refs[:n_in], *refs[n_in + n_deps :])


def whole(shape):
    return pl.BlockSpec(shape, lambda j: (0,) * len(shape), pipeline_mode=pl.Buffered(1))


def kept(shape):
    return pl.BlockSpec(shape, lambda j: (0,) * len(shape))


def block(shape):
    return pl.BlockSpec((1,) + shape, lambda j: (j,) + (0,) * len(shape))


def columns_from(rows, n, at):
    return pl.BlockSpec((rows, n), lambda j: (0, at), pipeline_mode=pl.Buffered(1))


def stepped(body, steps, in_specs, out_specs, out_shape, scratch, time, deps=()):
    run = pl.pallas_call(
        after(body, len(in_specs), len(deps)),
        grid=(steps,),
        out_shape=out_shape,
        in_specs=list(in_specs) + [ANY] * len(deps),
        out_specs=out_specs,
        scratch_shapes=list(scratch),
        compiler_params=pltpu.CompilerParams(vmem_limit_bytes=VMEM_LIMIT),
        cost_estimate=took_us(time),
    )
    return lambda *args: run(*args, *deps)


def sum_after(parts, kind, deps, time=1):
    n = len(parts)

    def body(*refs):
        total = refs[0][...].astype(F32)
        for part in refs[1:n]:
            total = total + part[...].astype(F32)
        refs[n][...] = total.astype(kind)

    return pl.pallas_call(
        after(body, n, len(deps)),
        out_shape=jax.ShapeDtypeStruct(parts[0].shape, kind),
        in_specs=[VMEM] * n + [ANY] * len(deps),
        out_specs=VMEM,
        compiler_params=pltpu.CompilerParams(vmem_limit_bytes=VMEM_LIMIT),
        cost_estimate=took_us(time),
    )(*parts, *deps)


def window(start, rows, total):
    base = jnp.minimum(lax.shift_right_logical(start, 4) * ALIGN, total - rows - ALIGN)
    return pl.ds(pl.multiple_of(base, ALIGN), rows + ALIGN), start - base


def moved(part, skip):
    rows = part.shape[0]
    shape = (rows + ALIGN, rows)
    there = lax.broadcasted_iota(jnp.int32, shape, 0) - skip
    return dot((there == lax.broadcasted_iota(jnp.int32, shape, 1)).astype(F32).astype(BF), part)


def read_rows(ref, start, rows):
    place, skip = window(start, rows, ref.shape[0])
    shape = (rows, rows + ALIGN)
    here = lax.broadcasted_iota(jnp.int32, shape, 1) - skip
    pick = (here == lax.broadcasted_iota(jnp.int32, shape, 0)).astype(F32).astype(BF)
    return dot(pick, ref[place, :]).astype(BF)


def layout_kernel(group_rows, seq, blocks, place, info, chunks):
    g, q = place[0], place[1]
    n_groups, n_seq = (blocks.shape[0] - 1) // BLOCKS, seq.shape[0] - 1
    start, stop = blocks[g * BLOCKS], blocks[g * BLOCKS + BLOCKS]

    def seq_of(position, shift):
        found = jnp.int32(0)
        for s in range(n_seq):
            found = jnp.where(position >= seq[s], s + shift, found)
        return found

    for j in range(BLOCKS):
        b = g * BLOCKS + (q ^ j)
        low, high = blocks[b], blocks[b + 1]
        text_from, text_to = jnp.int32(0), jnp.int32(0)
        for s in range(n_seq):
            first, last = jnp.maximum(seq[s] + IMG, low), jnp.minimum(seq[s + 1], high)
            text_from = jnp.where(first < last, first - low, text_from)
            text_to = jnp.where(first < last, last - low, text_to)
        info[COUNT + j] = high - low
        info[OFFSET + j] = low - start
        info[TEXT_FROM + j] = text_from
        info[TEXT_TO + j] = text_to
    own = blocks[g * BLOCKS + q]
    info[CORE] = place[2]
    info[TAIL_FROM] = jnp.maximum(stop - start - TAIL, 0)
    info[EDGE_FROM] = jnp.maximum(stop - start - EDGE, 0)
    info[OWN_FROM] = own
    info[OWN_SEQ] = seq_of(own, 0)
    info[NEXT_FROM] = seq[seq_of(own, 0) + 1]

    def span(steps):
        there = (g + steps >= 0) & (g + steps < n_groups)
        at = jnp.clip(g + steps, 0, n_groups - 1) * BLOCKS
        return jnp.where(there, blocks[at], 0), jnp.where(there, blocks[at + BLOCKS], 0)

    before, behind, ahead, beyond = span(-2), span(-1), span(1), span(2)
    n_chunks = (2 * KEYS + 2 * TAIL_PAD + group_rows) // KEYS
    i = 0
    for base, low, high, rows in (
        (jnp.maximum(before[1] - EDGE, before[0]) - (KEYS - EDGE), jnp.maximum(before[1] - EDGE, before[0]), before[1], KEYS),
        (
            jnp.maximum(behind[1] - TAIL, behind[0]) - (TAIL_PAD - TAIL),
            jnp.maximum(behind[1] - TAIL, behind[0]),
            behind[1],
            TAIL_PAD,
        ),
        (start, start, stop, group_rows),
        (ahead[0], ahead[0], jnp.minimum(ahead[1], ahead[0] + TAIL), TAIL_PAD),
        (beyond[0], beyond[0], jnp.minimum(beyond[1], beyond[0] + EDGE), KEYS),
    ):
        for step in range(rows // KEYS):
            chunks[i] = base + step * KEYS
            chunks[n_chunks + i] = low
            chunks[2 * n_chunks + i] = high
            i += 1
    n_tiles = group_rows // CHUNK
    for t in range(n_tiles):
        first = start + t * CHUNK
        last = jnp.minimum(first + CHUNK, stop) - 1
        chunks[3 * n_chunks + 2 * t] = jnp.where(first < stop, seq[seq_of(first, 0)], 0)
        chunks[3 * n_chunks + 2 * t + 1] = jnp.where(first < stop, seq[seq_of(last, 1)], 0)
        one = (first + CHUNK <= stop) & (seq_of(first, 0) == seq_of(last, 0))
        chunks[3 * n_chunks + 2 * n_tiles + 2 + t] = jnp.where(one, 1, 0)
    chunks[3 * n_chunks + 3 * n_tiles + 2] = seq[seq_of(start, 0)]
    chunks[3 * n_chunks + 3 * n_tiles + 3] = seq[seq_of(stop - 1, 1)]
    chunks[3 * n_chunks + 2 * n_tiles] = start
    chunks[3 * n_chunks + 2 * n_tiles + 1] = stop


def lane_spans(chunks, seq, n_chunks, n_tiles, t):
    start, stop = chunks[3 * n_chunks + 2 * n_tiles], chunks[3 * n_chunks + 2 * n_tiles + 1]
    position = start + t * CHUNK + lax.broadcasted_iota(jnp.int32, (1, CHUNK), 1)
    low, high = jnp.zeros_like(position), jnp.zeros_like(position)
    for s in range(seq.shape[0] - 1):
        hit = (position >= seq[s]) & (position < seq[s + 1]) & (position < stop)
        low, high = jnp.where(hit, seq[s], low), jnp.where(hit, seq[s + 1], high)
    return low, high


def enter_kernel(info, tokens, cotangent, image_mod, text_mod, modulated, grad_mlp):
    half = modulated.shape[0]
    n_seq = image_mod.shape[0]
    place = pl.ds(pl.multiple_of(info[CORE] * half, half), half)
    s = info[OWN_SEQ]
    after_s = jnp.minimum(s + 1, n_seq - 1)
    ids = row_ids(info[CORE] * half, half)
    live = ids < info[COUNT]
    is_text = live & (ids >= info[TEXT_FROM]) & (ids < info[TEXT_TO])
    is_next = live & (info[OWN_FROM] + ids >= info[NEXT_FROM])

    def pick(i):
        row = pl.ds(i, 1)
        own, text, following = image_mod[s][i : i + 1], text_mod[s][i : i + 1], image_mod[after_s][i : i + 1]
        return jnp.where(is_text, text, jnp.where(is_next, following, own))

    rows = tokens[place, :].astype(F32)
    centered = rows - jnp.mean(rows, axis=1, keepdims=True)
    normed = centered * lax.rsqrt(jnp.mean(centered * centered, axis=1, keepdims=True) + EPSILON)
    modulated[...] = (normed * (1.0 + pick(1)) + pick(0)).astype(BF)
    grad_mlp[...] = (pick(5) * jnp.where(live, cotangent[place, :].astype(F32), 0.0)).astype(BF)


def leave_kernel(
    info, grad_modulated, grad_first, branch, grad_mod_mlp, mlp_branch, tokens, cotangent, image_mod, text_mod,
    tokens_grad, sums,
):
    step = tokens_grad.shape[0]
    half = step * pl.num_programs(0)
    n_seq = image_mod.shape[0]
    s = info[OWN_SEQ]
    after_s = jnp.minimum(s + 1, n_seq - 1)
    ids = row_ids(info[CORE] * half + pl.program_id(0) * step, step)
    live = ids < info[COUNT]
    is_text = live & (ids >= info[TEXT_FROM]) & (ids < info[TEXT_TO])
    is_next = live & (info[OWN_FROM] + ids >= info[NEXT_FROM])
    is_own = live & jnp.logical_not(is_text | is_next)

    def pick(i):
        own, text, following = image_mod[s][i : i + 1], text_mod[s][i : i + 1], image_mod[after_s][i : i + 1]
        return jnp.where(is_text, text, jnp.where(is_next, following, own))

    def normal(rows):
        centered = rows - jnp.mean(rows, axis=1, keepdims=True)
        inverse = lax.rsqrt(jnp.mean(centered * centered, axis=1, keepdims=True) + EPSILON)
        return centered * inverse, inverse

    rows = tokens[...].astype(F32)
    normed, inverse = normal(rows)
    normed_mlp, _ = normal(rows + pick(2) * branch[...])

    @pl.when(pl.program_id(0) == 0)
    def _():
        sums[...] = jnp.zeros_like(sums)

    def add(i, term):
        for kept_rows, at in ((is_own, s), (is_next, after_s), (is_text, n_seq + s)):
            row = jnp.sum(jnp.where(kept_rows, term, 0.0), axis=0, keepdims=True)
            sums[at, i : i + 1, :] += row

    add(0, grad_modulated[...])
    add(1, grad_modulated[...] * normed)
    add(2, grad_first[...] * branch[...])
    add(3, grad_mod_mlp[...])
    add(4, grad_mod_mlp[...] * normed_mlp)
    add(5, cotangent[...].astype(F32) * mlp_branch[...])
    h = grad_modulated[...] * (1.0 + pick(1))
    back = h - jnp.mean(h, axis=1, keepdims=True) - normed * jnp.mean(h * normed, axis=1, keepdims=True)
    tokens_grad[...] = jnp.where(live, grad_first[...] + inverse * back, 0.0)


def row_ids(base, rows):
    return base + lax.broadcasted_iota(jnp.int32, (rows, 1), 0)


def for_rows(info, cap, body):
    count = info[COUNT + pl.program_id(0)]
    low = 0
    for rows in range(cap // 2, cap + 1, SUB):

        @pl.when((count > low) & (count <= rows))
        def _():
            body(rows)

        low = rows


def for_text(info, cap, body):
    j = pl.program_id(0)
    low, high = info[TEXT_FROM + j], info[TEXT_TO + j]

    @pl.when(high > low)
    def _():
        base = jnp.minimum(lax.shift_right_logical(low, 4) * ALIGN, cap - TEXT_ROWS)
        base = pl.multiple_of(base, ALIGN)
        ids = row_ids(base, TEXT_ROWS)
        body(pl.ds(base, TEXT_ROWS), (ids >= low) & (ids < high))


def half_places(info, half):
    mine = pl.multiple_of(info[CORE] * half, half)
    return pl.ds(mine, half), pl.ds(pl.multiple_of(half - mine, half), half)


def join(info, own, oth, out):
    half = own.shape[1]
    at_own, at_oth = half_places(info, half)
    out[at_own, :] = own[0]
    out[at_oth, :] = oth[0]


def part_ways(info, rows_ref, own, oth):
    half = own.shape[1]
    at_own, at_oth = half_places(info, half)
    own[0] = rows_ref[at_own, :]
    oth[0] = rows_ref[at_oth, :]


def split_columns(w, first, image, text):
    n = image.shape[1]
    image[...] = w[:, first : first + n]
    text[...] = w[:, first + n : first + 2 * n]


def to_group_rows(info, own, oth, w_image, w_text, out, joined, tile):
    cap = joined.shape[0]
    join(info, own, oth, joined)

    @pl.when(pl.program_id(0) == 0)
    def _():
        out[...] = jnp.zeros_like(out)

    def body(rows):
        tile[:rows, :] = dot(joined[:rows, :], w_image[...]).astype(BF)

        def text(place, is_text):
            tile[place, :] = jnp.where(is_text, dot(joined[place, :], w_text[...]).astype(BF), tile[place, :])

        for_text(info, cap, text)
        j = pl.program_id(0)
        place, skip = window(info[OFFSET + j], rows, out.shape[0])
        part = moved(tile[:rows, :], skip).astype(BF)
        ids = row_ids(-skip, rows + ALIGN)
        out[place, :] = jnp.where((ids >= 0) & (ids < info[COUNT + j]), part, out[place, :])

    for_rows(info, cap, body)


def project_kernel(info, own, oth, w, q, kv, tail, edge, head, head_edge, w_image, w_text, out, joined, tile):
    @pl.when(pl.program_id(0) == 0)
    def _():
        split_columns(w, 0, w_image, w_text)

    to_group_rows(info, own, oth, w_image, w_text, out, joined, tile)

    @pl.when(pl.program_id(0) == BLOCKS - 1)
    def _():
        n = q.shape[1]
        q[...] = out[:, :n]
        kv[...] = out[:, n:]
        tail[...] = read_rows(kv, info[TAIL_FROM], TAIL)
        edge[...] = read_rows(kv, info[EDGE_FROM], EDGE)
        head[...] = kv[:TAIL, :]
        head_edge[...] = kv[:EDGE, :]


def back_project_kernel(first, info, own, oth, w, out, w_image, w_text, joined, tile):
    @pl.when(pl.program_id(0) == 0)
    def _():
        split_columns(w, first, w_image, w_text)

    to_group_rows(info, own, oth, w_image, w_text, out, joined, tile)


def times_turned(info, x, w_image, w_text, result):
    cap = result.shape[0]

    def body(rows):
        result[:rows, :] = dot_back(x[:rows, :], w_image[...]).astype(BF)
        if rows < cap:
            result[rows:, :] = jnp.zeros((cap - rows, result.shape[1]), BF)

        def text(place, is_text):
            part = dot_back(x[place, :], w_text[...]).astype(BF)
            result[place, :] = jnp.where(is_text, part, result[place, :])

        for_text(info, cap, text)

    for_rows(info, cap, body)


def rows_to_slots_kernel(first, info, rows_ref, w, own, oth, w_image, w_text, x, result):
    j = pl.program_id(0)

    @pl.when(j == 0)
    def _():
        split_columns(w, first, w_image, w_text)

    def take(rows):
        x[:rows, :] = read_rows(rows_ref, info[OFFSET + j], rows)

    for_rows(info, x.shape[0], take)
    times_turned(info, x, w_image, w_text, result)
    part_ways(info, result, own, oth)


def slots_to_slots_kernel(info, x, w_image, w_text, own, oth, result):
    times_turned(info, x.at[0], w_image, w_text, result)
    part_ways(info, result, own, oth)


def gelu_parts(v):
    k = 0.7978845608028654
    square = v * v
    t = jnp.tanh(k * v * (1.0 + 0.044715 * square))
    half = 0.5 * (1.0 + t)
    return v * half, half + 0.5 * v * (1.0 - t * t) * (k + 3 * 0.044715 * k * square)


def mlp_up_kernel(info, x_own, x_oth, w_image, w_text, hid, slope, x, before):
    cap = x.shape[0]
    join(info, x_own, x_oth, x)

    def body(rows):
        before[:rows, :] = dot(x[:rows, :], w_image[...])

        def text(place, is_text):
            before[place, :] = jnp.where(is_text, dot(x[place, :], w_text[...]), before[place, :])

        for_text(info, cap, text)
        value, steep = gelu_parts(before[:rows, :])
        hid[0, :rows, :] = value.astype(BF)
        slope[0, :rows, :] = steep.astype(BF)
        if rows < cap:
            for ref in (hid, slope):
                ref[0, rows:, :] = jnp.zeros((cap - rows, ref.shape[2]), BF)

    for_rows(info, cap, body)


def mlp_back_kernel(
    info, g_own, g_oth, slope, upper_image, upper_text, lower_image, lower_text, gm_own, gm_oth, gb, g, back, result
):
    cap = g.shape[0]
    join(info, g_own, g_oth, g)

    def body(rows):
        back[:rows, :] = dot(g[:rows, :], lower_image[...]).astype(BF)

        def text(place, is_text):
            back[place, :] = jnp.where(is_text, dot(g[place, :], lower_text[...]).astype(BF), back[place, :])

        for_text(info, cap, text)
        gb[0, :rows, :] = (back[:rows, :].astype(F32) * slope[0, :rows, :].astype(F32)).astype(BF)
        if rows < cap:
            gb[0, rows:, :] = jnp.zeros((cap - rows, gb.shape[2]), BF)

    for_rows(info, cap, body)
    times_turned(info, gb.at[0], upper_image, upper_text, result)
    part_ways(info, result, gm_own, gm_oth)


def add_sums(info, left, right, acc_image, acc_text):
    cap = left.shape[0]
    j = pl.program_id(0)

    @pl.when(j == 0)
    def _():
        acc_image[...] = jnp.zeros_like(acc_image)
        acc_text[...] = jnp.zeros_like(acc_text)

    def body(rows):
        ids = row_ids(0, rows)
        is_text = (ids >= info[TEXT_FROM + j]) & (ids < info[TEXT_TO + j])
        is_image = (ids < info[COUNT + j]) & jnp.logical_not(is_text)
        acc_image[...] += dot_rows(left[:rows, :], jnp.where(is_image, right[:rows, :], jnp.zeros((), BF)))

    for_rows(info, cap, body)

    def text(place, is_text):
        acc_text[...] += dot_rows(left[place, :], jnp.where(is_text, right[place, :], jnp.zeros((), BF)))

    for_text(info, cap, text)


def give_sums(out, acc_image, acc_text):
    cut = acc_image.shape[1]

    @pl.when(pl.program_id(0) == BLOCKS - 1)
    def _():
        out[:, :cut] = acc_image[...].astype(BF)
        out[:, cut:] = acc_text[...].astype(BF)


def slot_sums_kernel(info, l_own, l_oth, right, out, acc_image, acc_text, left):
    join(info, l_own, l_oth, left)
    add_sums(info, left, right.at[0], acc_image, acc_text)
    give_sums(out, acc_image, acc_text)


def row_sums_kernel(info, l_own, l_oth, rows_ref, out, acc_image, acc_text, left, right):
    join(info, l_own, l_oth, left)

    def take(rows):
        right[:rows, :] = read_rows(rows_ref, info[OFFSET + pl.program_id(0)], rows)

    for_rows(info, left.shape[0], take)
    add_sums(info, left, right, acc_image, acc_text)
    give_sums(out, acc_image, acc_text)


def head_rows(turned, h):
    ids = lax.broadcasted_iota(jnp.int32, turned.shape, 0)
    return jnp.where((ids >= h * HEAD) & (ids < (h + 1) * HEAD), turned, 0)


def head_columns(plain, h):
    ids = lax.broadcasted_iota(jnp.int32, plain.shape, 1)
    return jnp.where((ids >= h * HEAD) & (ids < (h + 1) * HEAD), plain, 0)


def fold(combine, rows):
    parts = [rows[at : at + 8, :] for at in range(0, rows.shape[0], 8)]
    while len(parts) > 1:
        parts = [combine(a, b) for a, b in zip(parts[::2], parts[1::2])]
    return parts[0]


def slab_mask(chunks, i, n_chunks, low, q_from, q_to):
    position = chunks[i] + low + lax.broadcasted_iota(jnp.int32, (SLAB, 1), 0)
    valid = (position >= chunks[n_chunks + i]) & (position < chunks[2 * n_chunks + i])
    position = jnp.where(valid, position, -1)
    return (position >= q_from) & (position < q_to)


def for_chunks(chunks, n_chunks, t, body):
    low, high = chunks[3 * n_chunks + 2 * t], chunks[3 * n_chunks + 2 * t + 1]
    one = chunks[3 * n_chunks + 2 * pl.num_programs(0) + 2 + t] > 0

    def step(i, carry):
        base = chunks[i]
        start = jnp.maximum(base, chunks[n_chunks + i])
        stop = jnp.minimum(base + KEYS, chunks[2 * n_chunks + i])
        reached = (start < high) & (stop > low) & (start < stop)
        inside = one & (start == base) & (stop == base + KEYS) & (base >= low) & (stop <= high)

        @pl.when(reached & inside)
        def _():
            body(i, True)

        @pl.when(reached & jnp.logical_not(inside))
        def _():
            body(i, False)

        return carry

    lax.fori_loop(0, n_chunks, step, 0)


def sources_at(far_back, near_back, kv, near_on, far_on):
    chunk = 0
    for source, size, last in (
        (far_back, KEYS, True),
        (near_back, TAIL_PAD, True),
        (kv, kv.shape[0], False),
        (near_on, TAIL_PAD, False),
        (far_on, KEYS, False),
    ):
        rows = source.shape[0]
        skip = size - rows if last else 0
        for low in range(0, size, KEYS):
            first, stop = max(low, skip), min(low + KEYS, skip + rows)
            yield chunk, source, slice(first - skip, stop - skip), first - low, stop - low
            chunk += 1


def if_reached(chunks, n_chunks, i, body, otherwise=None):
    last = 3 * n_chunks + 3 * pl.num_programs(0) + 2
    start = jnp.maximum(chunks[i], chunks[n_chunks + i])
    stop = jnp.minimum(chunks[i] + KEYS, chunks[2 * n_chunks + i])
    reached = (start < chunks[last + 1]) & (stop > chunks[last]) & (start < stop)
    pl.when(reached)(body)
    if otherwise:
        pl.when(jnp.logical_not(reached))(otherwise)


def gather_keys(chunks, sources, k, v, plain, turned):
    n = k.shape[1]
    n_chunks = k.shape[0] // KEYS
    for i, source, rows, first, stop in sources_at(*sources):

        def take():
            at = i * KEYS
            for ref, columns in ((k, slice(0, n)), (v, slice(n, 2 * n))):
                ref[at + first : at + stop, :] = source[rows, columns]
                for low, high in ((0, first), (stop, KEYS)):
                    if low < high:
                        ref[at + low : at + high, :] = jnp.zeros((high - low, n), BF)
            part = slice(at, at + KEYS)
            turned[:, part] = plain[part, :].T

        if_reached(chunks, n_chunks, i, take)


def attend_kernel(
    chunks, seq, q, far_back, near_back, kv, near_on, far_on,
    out, exact, lse, top,
    k, v, v_turned, q_turn, logits, probs, total, high,
):
    t = pl.program_id(0)
    n_chunks = k.shape[0] // KEYS
    heads = q.shape[1] // HEAD
    wide = q.shape[0]

    @pl.when(t == 0)
    def _():
        gather_keys(chunks, (far_back, near_back, kv, near_on, far_on), k, v, v, v_turned)
        top[...] = jnp.full_like(top, NEGATIVE)

    live = chunks[3 * n_chunks + 2 * t + 1] > 0

    @pl.when(live)
    def _():
        turned = (q[...].astype(F32) * HEAD**-0.5).T
        for h in range(heads):
            q_turn[h] = head_rows(turned, h).astype(BF)
        lanes_from, lanes_to = lane_spans(chunks, seq, n_chunks, pl.num_programs(0), t)
        total[...] = jnp.zeros_like(total)
        high[...] = jnp.full_like(high, NEGATIVE)

        def first(i, whole_chunk):
            place = pl.ds(pl.multiple_of(i * KEYS, KEYS), KEYS)
            for h in range(heads):
                logits[h, i] = dot(k[place, :], q_turn[h])
            for low in range(0, KEYS, SLAB):
                part = slice(low, low + SLAB)
                if not whole_chunk:
                    mask = slab_mask(chunks, i, n_chunks, low, lanes_from, lanes_to)
                for h in range(heads):
                    values = logits[h, i, part, :]
                    if not whole_chunk:
                        values = jnp.where(mask, values, NEGATIVE)
                        logits[h, i, part, :] = values
                    rows = slice(8 * h, 8 * h + 8)
                    high[rows, :] = jnp.maximum(high[rows, :], fold(jnp.maximum, values))

        for_chunks(chunks, n_chunks, t, first)
        tops = [jnp.max(high[8 * h : 8 * h + 8, :], axis=0, keepdims=True) for h in range(heads)]
        high[...] = jnp.zeros_like(high)

        def second(i, whole_chunk):
            place = pl.ds(pl.multiple_of(i * KEYS, KEYS), KEYS)
            for low in range(0, KEYS, SLAB):
                part = slice(low, low + SLAB)
                for h in range(heads):
                    p = jnp.exp(logits[h, i, part, :] - tops[h])
                    rows = slice(8 * h, 8 * h + 8)
                    high[rows, :] += fold(jnp.add, p)
                    probs[part, h * wide : (h + 1) * wide] = p.astype(BF)
            for h in range(heads):
                rows = slice(h * HEAD, (h + 1) * HEAD)
                total[rows, :] += dot(v_turned[rows, place], probs[:, h * wide : (h + 1) * wide])

        for_chunks(chunks, n_chunks, t, second)
        for h in range(heads):
            rows = slice(h * HEAD, (h + 1) * HEAD)
            sums = jnp.sum(high[8 * h : 8 * h + 8, :], axis=0, keepdims=True)
            total[rows, :] = total[rows, :] / sums
            lse[0, h : h + 1, :] = tops[h] + jnp.log(sums)
            seen = jnp.where(lanes_to > lanes_from, tops[h], NEGATIVE)
            top[h : h + 1, :] = jnp.maximum(top[h : h + 1, :], seen)
        result = total[...].T
        exact[...] = result
        out[...] = result.astype(BF)

    @pl.when(jnp.logical_not(live))
    def _():
        exact[...] = jnp.zeros_like(exact)
        out[...] = jnp.zeros_like(out)
        lse[...] = jnp.zeros_like(lse)


def attend_back_kernel(
    chunks, seq, q, g, attended, far_back, near_back, kv, near_on, far_on, lse,
    dq, d_far_back, d_near_back, d_kv, d_near_on, d_far_on,
    k, v, k_turned, q_stack, g_stack, q_turn, g_turn, logits, grads_of, probs, grad_logits, total, dk, dv,
):
    t = pl.program_id(0)
    n_chunks = k.shape[0] // KEYS
    heads = q.shape[1] // HEAD
    wide = q.shape[0]

    @pl.when(t == 0)
    def _():
        gather_keys(chunks, (far_back, near_back, kv, near_on, far_on), k, v, k, k_turned)
        for i in range(n_chunks):

            def clear():
                dk[i * KEYS : (i + 1) * KEYS, :] = jnp.zeros((KEYS, dk.shape[1]), F32)
                dv[i * KEYS : (i + 1) * KEYS, :] = jnp.zeros((KEYS, dk.shape[1]), F32)

            if_reached(chunks, n_chunks, i, clear)

    live = chunks[3 * n_chunks + 2 * t + 1] > 0

    @pl.when(live)
    def _():
        scaled = q[...].astype(F32) * HEAD**-0.5
        grads = g[...].astype(F32)
        q_turned, g_turned = scaled.T, grads.T
        product = g_turned * attended[...].T
        delta, logs = [], []
        for h in range(heads):
            rows = slice(h * wide, (h + 1) * wide)
            q_stack[rows, :] = head_columns(scaled, h).astype(BF)
            g_stack[rows, :] = head_columns(grads, h).astype(BF)
            q_turn[h] = head_rows(q_turned, h).astype(BF)
            g_turn[h] = head_rows(g_turned, h).astype(BF)
            delta.append(jnp.sum(product[h * HEAD : (h + 1) * HEAD, :], axis=0, keepdims=True))
            logs.append(lse[0, h : h + 1, :])
        lanes_from, lanes_to = lane_spans(chunks, seq, n_chunks, pl.num_programs(0), t)
        total[...] = jnp.zeros_like(total)

        def body(i, whole_chunk):
            place = pl.ds(pl.multiple_of(i * KEYS, KEYS), KEYS)
            for h in range(heads):
                logits[h] = dot(k[place, :], q_turn[h])
                grads_of[h] = dot(v[place, :], g_turn[h])
            for low in range(0, KEYS, SLAB):
                part = slice(low, low + SLAB)
                if not whole_chunk:
                    mask = slab_mask(chunks, i, n_chunks, low, lanes_from, lanes_to)
                for h in range(heads):
                    lanes = slice(h * wide, (h + 1) * wide)
                    p = jnp.exp(logits[h, part, :] - logs[h])
                    if not whole_chunk:
                        p = jnp.where(mask, p, 0.0)
                    probs[part, lanes] = p.astype(BF)
                    grad_logits[part, lanes] = (p * (grads_of[h, part, :] - delta[h])).astype(BF)
            for h in range(heads):
                rows = slice(h * HEAD, (h + 1) * HEAD)
                total[rows, :] += dot(k_turned[rows, place], grad_logits[:, h * wide : (h + 1) * wide])
            dv[place, :] += dot(probs[...], g_stack[...])
            dk[place, :] += dot(grad_logits[...], q_stack[...])

        for_chunks(chunks, n_chunks, t, body)
        dq[...] = (total[...].T * HEAD**-0.5).astype(BF)

    @pl.when(jnp.logical_not(live))
    def _():
        dq[...] = jnp.zeros_like(dq)

    @pl.when(t == pl.num_programs(0) - 1)
    def _():
        n = dk.shape[1]
        for i, out, rows, first, stop in sources_at(d_far_back, d_near_back, d_kv, d_near_on, d_far_on):

            def give():
                place = slice(i * KEYS + first, i * KEYS + stop)
                out[rows, :n] = dk[place, :].astype(out.dtype)
                out[rows, n:] = dv[place, :].astype(out.dtype)

            def blank():
                out[rows, :] = jnp.zeros((stop - first, 2 * n), out.dtype)

            if_reached(chunks, n_chunks, i, give, blank)


def gather_grads_kernel(info, dq, d_kv, near_back, near_on, far_back, far_on, out, total):
    total[...] = d_kv[...]
    for start, part in ((info[TAIL_FROM], near_back), (info[EDGE_FROM], far_back)):
        place, skip = window(start, part.shape[0], total.shape[0])
        total[place, :] += moved(part[...], skip)
    for part in (near_on, far_on):
        total[: part.shape[0], :] += part[...].astype(F32)
    n = dq.shape[1]
    out[:, :n] = dq[...]
    out[:, n:] = total[...].astype(BF)


def copy_after(source, deps):
    return sum_after([source], source.dtype, deps)


def shift(value, steps):
    count = lax.axis_size("g")
    pairs = [(i, i + steps) for i in range(count) if 0 <= i + steps < count]
    if not pairs:
        return jnp.zeros_like(value)
    return lax.ppermute(value, "g", pairs)


def if_needed(predicate, run, *values):
    return lax.cond(predicate, run, lambda *v: tuple(jnp.zeros_like(a) for a in v), *values)


def max_over_groups(value):
    groups = lax.axis_size("g")
    top = value
    for step in range(1, groups):
        top = jnp.maximum(top, lax.ppermute(value, "g", [(i, (i + step) % groups) for i in range(groups)]))
    return top


def max_over_plane(value):
    return jnp.maximum(jnp.maximum(value, over_x(value)), jnp.maximum(over_y(value), over_xy(value)))


def over_x(value):
    return lax.ppermute(value, "x", SWAP)


def over_y(value):
    return lax.ppermute(value, "y", SWAP)


def over_core(value):
    return lax.ppermute(value, "c", SWAP)


def over_xy(value):
    return lax.ppermute(value, ("y", "x"), [(0, 3), (1, 2), (2, 1), (3, 0)])


def over_groups(sums):
    return lax.psum_scatter(sums, "g", scatter_dimension=0, tiled=True)


def spread_begin(value):
    return value, over_x(value), over_y(value)


def spread_next(begun, deps=()):
    value, from_x, from_y = begun
    cut = value.shape[0] // 2
    on_y, on_x = from_x[:cut], from_y[cut:]
    if deps:
        on_y, on_x = sum_after([on_y], BF, deps), sum_after([on_x], BF, deps)
    return value, from_x, from_y, on_y, on_x, over_y(on_y), over_x(on_x)


def spread_end(state):
    value, from_x, from_y, _, _, low, high = state
    own = jnp.stack([value, from_x, from_y, jnp.concatenate([low, high], axis=0)])
    return own, over_core(own)


def spread(value, deps=()):
    return spread_end(spread_next(spread_begin(value), deps))


def add16(*parts):
    total = parts[0].astype(F32)
    for part in parts[1:]:
        total = total + part.astype(F32)
    return total


def core_sum(own, oth, deps=()):
    other = over_core(oth)
    half, width = own.shape[1:]
    cut = half // 2
    cuts = ((0, 0, half), (3, 0, cut), (3, cut, half), (1, 0, cut), (1, cut, half), (2, 0, cut), (2, cut, half))

    def body(*refs):
        for out, (j, low, high) in zip(refs[2:], cuts):
            out[...] = (refs[0][j, low:high, :].astype(F32) + refs[1][j, low:high, :].astype(F32)).astype(BF)

    return pl.pallas_call(
        after(body, 2, len(deps)),
        out_shape=tuple(jax.ShapeDtypeStruct((high - low, width), BF) for _, low, high in cuts),
        in_specs=[VMEM] * 2 + [ANY] * len(deps),
        out_specs=(VMEM,) * len(cuts),
        compiler_params=pltpu.CompilerParams(vmem_limit_bytes=VMEM_LIMIT),
        cost_estimate=took_us(3),
    )(own, other, *deps)


def collect_begin(pieces):
    mine, far_x, far_y, x_low, x_high, y_low, y_high = pieces
    from_x, from_y = over_x(far_x), over_y(far_y)
    return mine, x_high, y_low, from_x, from_y, over_x(x_low), over_y(y_high)


def collect_next(begun, deps=()):
    mine, x_high, y_low, from_x, from_y, first_x, first_y = begun
    on_x, on_y = sum_after((x_high, from_y), BF, deps), sum_after((y_low, from_x), BF, deps)
    return mine, first_x, first_y, on_x, on_y, over_x(on_x), over_y(on_y)


def collect_end(state, deps=()):
    own, first_x, first_y, _, _, last_x, last_y = state
    cut = own.shape[0] // 2
    n = 5

    def body(mine, first_x, first_y, last_x, last_y, out):
        out[:cut, :] = mine[:cut, :].astype(F32) + first_x[...].astype(F32) + last_y[...].astype(F32)
        out[cut:, :] = mine[cut:, :].astype(F32) + last_x[...].astype(F32) + first_y[...].astype(F32)

    return pl.pallas_call(
        after(body, n, len(deps)),
        out_shape=jax.ShapeDtypeStruct(own.shape, F32),
        in_specs=[VMEM] * n + [ANY] * len(deps),
        out_specs=VMEM,
        compiler_params=pltpu.CompilerParams(vmem_limit_bytes=VMEM_LIMIT),
        cost_estimate=took_us(2),
    )(own, first_x, first_y, last_x, last_y, *deps)


def sums_of_shares(shares, g, q, deps):
    groups = lax.axis_size("g")
    pick = lambda values, at: lax.dynamic_index_in_dim(values, at, 0, keepdims=False)
    shares = jnp.moveaxis(shares.reshape((groups, BLOCKS) + shares.shape[1:]), 1, 0)
    shares = (
        pick(shares, q)
        + over_x(pick(shares, q ^ 1))
        + over_y(pick(shares, q ^ 2))
        + over_xy(pick(shares, q ^ 3))
    )
    shares = sum_after([shares], F32, deps)
    total = pick(shares, g)
    for step in range(1, groups):
        pairs = [(i, (i + step) % groups) for i in range(groups)]
        total = total + lax.ppermute(pick(shares, lax.rem(g + step, groups)), "g", pairs)
    return total


def layer_norm(inputs):
    centered = inputs - jnp.mean(inputs, axis=1, keepdims=True)
    inverse_std = lax.rsqrt(jnp.mean(centered * centered, axis=1, keepdims=True) + EPSILON)
    return (centered * inverse_std, inverse_std)


def norm_back(grad_normed, normed, inverse_std):
    return inverse_std * (
        grad_normed
        - jnp.mean(grad_normed, axis=1, keepdims=True)
        - normed * jnp.mean(grad_normed * normed, axis=1, keepdims=True)
    )


def pick_pieces(pieces, place, deps=()):
    shape = pieces.shape[1:]

    def body(place_ref, source, *outs):
        for j, out in enumerate(outs):
            out[...] = source[place_ref[1] ^ j]

    return pl.pallas_call(
        after(body, 2, len(deps)),
        out_shape=(jax.ShapeDtypeStruct(shape, pieces.dtype),) * BLOCKS,
        in_specs=[SMEM, VMEM] + [ANY] * len(deps),
        out_specs=(VMEM,) * BLOCKS,
        compiler_params=pltpu.CompilerParams(vmem_limit_bytes=VMEM_LIMIT),
        cost_estimate=took_us(2),
    )(place, pieces, *deps)


def swap_pieces(picked):
    own, to_x, to_y, to_xy = picked
    return own, over_x(to_x), over_y(to_y), over_xy(to_xy)


def exchange(pieces, place):
    return swap_pieces(pick_pieces(pieces, place))


def arrange(got, place, body, out_shape, deps=()):
    n = len(got)

    def kernel(place_ref, *refs):
        for j in range(n):
            body(place_ref[1] ^ j, refs[j], refs[n:])

    return pl.pallas_call(
        after(kernel, 1 + n, len(deps)),
        out_shape=out_shape,
        in_specs=[SMEM] + [VMEM] * n + [ANY] * len(deps),
        out_specs=(VMEM,) * len(out_shape),
        compiler_params=pltpu.CompilerParams(vmem_limit_bytes=VMEM_LIMIT),
        cost_estimate=took_us(2),
    )(place, *got, *deps)


def stack_rows(b, piece, outs):
    rows = piece.shape[0]
    outs[0][pl.ds(pl.multiple_of(b * rows, ALIGN), rows), :] = piece[...]


def give_wide(b, piece, outs):
    n = piece.shape[1] // 2
    for k, out in enumerate(outs):
        out[:, pl.ds(pl.multiple_of(b * n, SUB), n)] = piece[:, k * n : (k + 1) * n].astype(F32)


def give_turned(b, piece, outs):
    n = piece.shape[1] // 2
    for k, out in enumerate(outs):
        out[pl.ds(pl.multiple_of(b * n, ALIGN), n), :] = piece[:, k * n : (k + 1) * n].astype(F32).T


def give_qkv(b, piece, outs):
    n = piece.shape[1] // 6
    for at in range(BLOCKS):

        @pl.when(b == at)
        def _():
            for k, out in enumerate(outs):
                for p in range(3):
                    part = piece[:, (3 * k + p) * n : (3 * k + p + 1) * n].astype(F32)
                    out[:, p, at * n : (at + 1) * n] = part


def local(
    tokens,
    cotangent,
    seq_offsets,
    block_offsets,
    image_mod,
    text_mod,
    image_qkv,
    text_qkv,
    image_out,
    text_out,
    image_fc1,
    text_fc1,
    image_fc2,
    text_fc2,
    clip_limits,
):
    rows_cap, width = tokens.shape
    half = rows_cap // 2
    share = image_qkv.shape[0]
    columns = image_qkv.shape[2]
    group_rows = BLOCKS * rows_cap
    mine = columns // BLOCKS
    fc = image_fc1.shape[1] // BLOCKS
    heads = mine // HEAD
    seq_count = seq_offsets.shape[0] - 1
    n_groups = lax.axis_size("g")
    g, c = lax.axis_index("g"), lax.axis_index("c")
    q = 2 * lax.axis_index("y") + lax.axis_index("x")

    def both_halves(rows):
        other = over_core(rows)
        return jnp.where(c == 0, jnp.concatenate([rows, other], axis=0), jnp.concatenate([other, rows], axis=0))

    def quarter(inputs):
        return jnp.moveaxis(inputs.reshape(share, -1, BLOCKS, mine), 2, 0).reshape(BLOCKS, share, -1)

    def quarter_turned(inputs):
        return jnp.swapaxes(inputs.reshape(BLOCKS, -1, share), 1, 2)

    def quarter_wide(inputs):
        return jnp.swapaxes(inputs.reshape(share, BLOCKS, -1), 0, 1)

    pack_qkv = jnp.concatenate([quarter(image_qkv), quarter(text_qkv)], axis=2)
    place = jnp.stack([g, q, c]).astype(jnp.int32)
    plane_of = lambda n: (jax.ShapeDtypeStruct((BLOCKS * share, n), BF),)
    (plane_qkv,) = arrange(exchange(pack_qkv, place), place, stack_rows, plane_of(6 * mine))

    n_tiles = group_rows // CHUNK
    reach = 2 * KEYS + 2 * TAIL_PAD + group_rows
    n_chunks = reach // KEYS
    info, chunks = pl.pallas_call(
        functools.partial(layout_kernel, group_rows),
        out_shape=(
            jax.ShapeDtypeStruct((INFO,), jnp.int32),
            jax.ShapeDtypeStruct((3 * n_chunks + 3 * n_tiles + 4,), jnp.int32),
        ),
        in_specs=[SMEM] * 3,
        out_specs=(SMEM, SMEM),
        cost_estimate=took_us(1),
    )(seq_offsets, block_offsets, place)

    my_rows = lambda inputs: lax.dynamic_slice_in_dim(inputs, c * half, half, 0)
    ids = c * half + jnp.arange(half, dtype=jnp.int32)
    my_seq = info[OWN_SEQ]
    next_seq = jnp.minimum(my_seq + 1, seq_count - 1)
    is_live = (ids < info[COUNT])[:, None]
    is_text = is_live & ((ids >= info[TEXT_FROM]) & (ids < info[TEXT_TO]))[:, None]
    is_next = is_live & (info[OWN_FROM] + ids >= info[NEXT_FROM])[:, None]
    vectors = (image_mod[my_seq], text_mod[my_seq], image_mod[next_seq])

    def modulation(which):
        return jnp.where(
            is_text, vectors[1][which][None], jnp.where(is_next, vectors[2][which][None], vectors[0][which][None])
        )

    shift_rows, scale_rows, gate_rows, shift_mlp, scale_mlp, gate_mlp = (modulation(i) for i in range(6))
    stream = my_rows(tokens).astype(F32)
    grad_stream = jnp.where(is_live, my_rows(cotangent).astype(F32), 0.0)
    normed, inverse_std = layer_norm(stream)
    modulated, grad_mlp = pl.pallas_call(
        enter_kernel,
        out_shape=(jax.ShapeDtypeStruct((half, width), BF),) * 2,
        in_specs=[SMEM] + [VMEM] * 4,
        out_specs=(VMEM, VMEM),
        compiler_params=pltpu.CompilerParams(vmem_limit_bytes=VMEM_LIMIT),
        cost_estimate=took_us(4),
    )(info, tokens, cotangent, image_mod, text_mod)

    slot = lambda n: jax.ShapeDtypeStruct((BLOCKS, half, n), BF)
    full = lambda n: jax.ShapeDtypeStruct((BLOCKS, rows_cap, n), BF)
    rows_of = lambda n, kind: jax.ShapeDtypeStruct((group_rows, n), kind)
    slot_block = block((half, width))
    scratch = lambda rows, n, kind=BF: pltpu.VMEM((rows, n), kind)
    weight_pair = lambda n: [scratch(width, n), scratch(width, n)]

    whole_qkv = lax.all_gather(plane_qkv, "g", axis=0, tiled=True)
    mod_begun = spread_begin(modulated)
    pack_rest = jnp.concatenate(
        [
            quarter_wide(image_fc1),
            quarter_wide(text_fc1),
            quarter_turned(image_fc2),
            quarter_turned(text_fc2),
            quarter_turned(image_out),
            quarter_turned(text_out),
        ],
        axis=2,
    )
    rest_picked = pick_pieces(pack_rest, place)
    mod_own, mod_oth = spread_end(spread_next(mod_begun, rest_picked[:1]))
    (plane_rest,) = arrange(swap_pieces(rest_picked), place, stack_rows, plane_of(4 * fc + 2 * mine))
    whole_out = lax.all_gather(plane_rest[:, 4 * fc :], "g", axis=0, tiled=True)
    whole_fc2 = lax.all_gather(plane_rest[:, 2 * fc : 4 * fc], "g", axis=0, tiled=True)

    pair = lambda rows: jax.ShapeDtypeStruct((rows, 2 * mine), BF)
    queries, pairs, tail, edge, head, head_edge = stepped(
        project_kernel,
        BLOCKS,
        [SMEM, slot_block, slot_block, whole(whole_qkv.shape)],
        [kept(s) for s in ((group_rows, mine), (group_rows, 2 * mine), (TAIL, 2 * mine), (EDGE, 2 * mine), (TAIL, 2 * mine), (EDGE, 2 * mine))],
        (rows_of(mine, BF), pair(group_rows), pair(TAIL), pair(EDGE), pair(TAIL), pair(EDGE)),
        weight_pair(3 * mine) + [scratch(group_rows, 3 * mine), scratch(rows_cap, width), scratch(rows_cap, 3 * mine)],
        1,
    )(info, mod_own, mod_oth, whole_qkv)

    near_back, near_on = shift(tail, 1), shift(head, -1)
    gmlp_begun = spread_begin(copy_after(grad_mlp, (queries,)))
    fc1_piece = copy_after(plane_rest[:, : 2 * fc], (near_back, near_on, *gmlp_begun[1:]))
    whole_fc1 = lax.all_gather(fc1_piece, "g", axis=0, tiled=True)
    gmlp_state = spread_next(gmlp_begun, (near_back, near_on, whole_out))
    gmlp_own, gmlp_oth = spread_end(gmlp_state)
    need_far = jnp.min(block_offsets[BLOCKS::BLOCKS] - block_offsets[:-1:BLOCKS]) < IMG + TXT
    far_back, far_on = if_needed(need_far, lambda a, b: (shift(a, 2), shift(b, -2)), edge, head_edge)
    sources = (far_back, near_back, pairs, near_on, far_on)
    source_specs = [whole(s.shape) for s in sources]

    tile_spec = pl.BlockSpec((CHUNK, mine), lambda t: (t, 0))
    log_spec = block((8, CHUNK))
    attended, attended_exact, logs, tops = stepped(
        attend_kernel,
        n_tiles,
        [SMEM, SMEM, tile_spec, *source_specs],
        (tile_spec, tile_spec, log_spec, kept((8, CHUNK))),
        (
            rows_of(mine, BF),
            rows_of(mine, F32),
            jax.ShapeDtypeStruct((n_tiles, 8, CHUNK), F32),
            jax.ShapeDtypeStruct((8, CHUNK), F32),
        ),
        [
            scratch(reach, mine),
            scratch(reach, mine),
            scratch(mine, reach),
            pltpu.VMEM((heads, mine, CHUNK), BF),
            pltpu.VMEM((heads, n_chunks, KEYS, CHUNK), F32),
            scratch(KEYS, heads * CHUNK),
            scratch(mine, CHUNK, F32),
            scratch(8 * heads, CHUNK, F32),
        ],
        1,
        (*gmlp_state[3:5], fc1_piece),
    )(chunks, seq_offsets, queries, *sources)

    def to_slots(n, first, rows, w, deps=(), time=10):
        return stepped(
            functools.partial(rows_to_slots_kernel, first),
            BLOCKS,
            [SMEM, whole(rows.shape), whole(w.shape)],
            (slot_block, slot_block),
            (slot(width), slot(width)),
            weight_pair(n) + [scratch(rows_cap, n), scratch(rows_cap, width)],
            time,
            deps,
        )(info, rows, w)

    branch_state = collect_next(collect_begin(core_sum(*to_slots(mine, 0, attended, whole_out, (), 1))), (whole_fc1,))
    branch = collect_end(branch_state)
    first = stream + gate_rows * branch
    normed_mlp, inverse_mlp = layer_norm(first)
    modulated_mlp = (normed_mlp * (1.0 + scale_mlp) + shift_mlp).astype(BF)

    mm_own, mm_oth = spread(copy_after(modulated_mlp, (gmlp_oth,)))
    fc_block = block((rows_cap, fc))
    hid, slope = stepped(
        mlp_up_kernel,
        BLOCKS,
        [SMEM, slot_block, slot_block, columns_from(width, fc, 0), columns_from(width, fc, 1)],
        (fc_block, fc_block),
        (full(fc), full(fc)),
        [scratch(rows_cap, width), scratch(rows_cap, fc, F32)],
        1,
    )(info, mm_own, mm_oth, whole_fc1, whole_fc1)

    def slot_sums(left, right, deps, time):
        return stepped(
            slot_sums_kernel,
            BLOCKS,
            [SMEM, slot_block, slot_block, fc_block],
            kept((width, 2 * fc)),
            jax.ShapeDtypeStruct((width, 2 * fc), BF),
            [scratch(width, fc, F32), scratch(width, fc, F32), scratch(rows_cap, width)],
            time,
            deps,
        )(info, *left, right)

    def row_sums(left, rows, deps=()):
        n = rows.shape[1]
        return stepped(
            row_sums_kernel,
            BLOCKS,
            [SMEM, slot_block, slot_block, whole(rows.shape)],
            kept((width, 2 * n)),
            jax.ShapeDtypeStruct((width, 2 * n), BF),
            [scratch(width, n, F32), scratch(width, n, F32), scratch(rows_cap, width), scratch(rows_cap, n)],
            n / 42,
            deps,
        )(info, *left, rows)

    fc2_sums = slot_sums((gmlp_own, gmlp_oth), hid, (), 1)
    fc2_part = over_groups(fc2_sums)
    head_top = jnp.max(tops[:heads], axis=1)
    spot = jnp.arange(BLOCKS)[:, None] == q
    head_max = jnp.where(spot, head_top[None, :], NEGATIVE).reshape(1, -1)
    gm_own, gm_oth, gb = stepped(
        mlp_back_kernel,
        BLOCKS,
        [SMEM, slot_block, slot_block, fc_block] + [columns_from(width, fc, at) for at in (0, 1, 0, 1)],
        (slot_block, slot_block, fc_block),
        (slot(width), slot(width), full(fc)),
        [scratch(rows_cap, width), scratch(rows_cap, fc), scratch(rows_cap, width)],
        1,
        (fc2_sums,),
    )(info, gmlp_own, gmlp_oth, slope, whole_fc1, whole_fc1, whole_fc2, whole_fc2)

    gm_part = core_sum(gm_own, gm_oth)
    gm_state = collect_begin(gm_part)
    fc1_sums = slot_sums((mm_own, mm_oth), gb, gm_part, 12)
    fc1_part = over_groups(fc1_sums)
    gm_state = collect_next(gm_state, (fc1_sums,))
    head_max = max_over_groups(copy_after(head_max, gm_state[3:5]))
    mlp_own, mlp_oth = stepped(
        slots_to_slots_kernel,
        BLOCKS,
        [SMEM, fc_block, columns_from(width, fc, 0), columns_from(width, fc, 1)],
        (slot_block, slot_block),
        (slot(width), slot(width)),
        [scratch(rows_cap, width)],
        10,
        gm_state[3:5],
    )(info, hid, whole_fc2, whole_fc2)
    grad_mod_mlp = collect_end(gm_state, (mlp_own, head_max))

    grad_first = jnp.where(
        is_live,
        grad_stream + norm_back(grad_mod_mlp * (1.0 + scale_mlp), normed_mlp, inverse_mlp),
        0.0,
    )
    grad_branch = (gate_rows * grad_first).astype(BF)
    gbr_begun = spread_begin(grad_branch)
    gbr_own, gbr_oth = spread_end(spread_next(gbr_begun, (fc2_part,)))
    mlp_part = core_sum(mlp_own, mlp_oth, (gbr_oth,))
    grad_attended = stepped(
        functools.partial(back_project_kernel, 0),
        BLOCKS,
        [SMEM, slot_block, slot_block, whole(whole_out.shape)],
        kept((group_rows, mine)),
        rows_of(mine, BF),
        weight_pair(mine) + [scratch(rows_cap, width), scratch(rows_cap, mine)],
        1,
    )(info, gbr_own, gbr_oth, whole_out)

    mlp_state = collect_begin(mlp_part)
    head_max = max_over_plane(copy_after(head_max, mlp_part[:1]))
    dq, give_far_back, give_back, d_pairs, give_on, give_far_on = stepped(
        attend_back_kernel,
        n_tiles,
        [SMEM, SMEM, tile_spec, tile_spec, tile_spec, *source_specs, log_spec],
        (tile_spec, *(kept(s.shape) for s in sources)),
        (rows_of(mine, BF), pair(EDGE), pair(TAIL), rows_of(2 * mine, F32), pair(TAIL), pair(EDGE)),
        [
            scratch(reach, mine),
            scratch(reach, mine),
            scratch(mine, reach),
            scratch(heads * CHUNK, mine),
            scratch(heads * CHUNK, mine),
            pltpu.VMEM((heads, mine, CHUNK), BF),
            pltpu.VMEM((heads, mine, CHUNK), BF),
            pltpu.VMEM((heads, KEYS, CHUNK), F32),
            pltpu.VMEM((heads, KEYS, CHUNK), F32),
            scratch(KEYS, heads * CHUNK),
            scratch(KEYS, heads * CHUNK),
            scratch(mine, CHUNK, F32),
            scratch(reach, mine, F32),
            scratch(reach, mine, F32),
        ],
        1,
        (mlp_part[0],),
    )(chunks, seq_offsets, queries, grad_attended, attended_exact, *sources, logs)
    gave_back, gave_on = shift(give_back, -1), shift(give_on, 1)
    gave_far_back, gave_far_on = if_needed(
        need_far, lambda a, b: (shift(a, -2), shift(b, 2)), give_far_back, give_far_on
    )

    out_sums = row_sums((gbr_own, gbr_oth), attended, (dq,))
    out_part = over_groups(copy_after(out_sums, (gave_back, gave_on)))
    mlp_state = collect_next(mlp_state, (out_sums,))
    pieces_of = lambda part, deps: pick_pieces(part.reshape(BLOCKS, share, -1), place, deps)
    mlp_branch = collect_end(mlp_state, (gave_back, gave_on))
    grad_qkv = pl.pallas_call(
        after(gather_grads_kernel, 7, 4),
        out_shape=rows_of(3 * mine, BF),
        in_specs=[SMEM] + [VMEM] * 6 + [ANY] * 4,
        out_specs=VMEM,
        scratch_shapes=[scratch(group_rows, 2 * mine, F32)],
        compiler_params=pltpu.CompilerParams(vmem_limit_bytes=VMEM_LIMIT),
        cost_estimate=took_us(8),
    )(info, dq, d_pairs, gave_back, gave_on, gave_far_back, gave_far_on, mlp_branch, out_sums, fc1_part, head_max)

    qkv_sums = row_sums((mod_own, mod_oth), grad_qkv)
    qkv_part = over_groups(qkv_sums)
    mod_part = core_sum(*to_slots(3 * mine, 0, grad_qkv, whole_qkv, (qkv_sums,)))
    mod_state = collect_next(collect_begin(mod_part))
    pair_f32 = lambda *shape: (jax.ShapeDtypeStruct(shape, F32),) * 2
    mixed_rows = jnp.where(is_live, first + gate_mlp * mlp_branch, 0.0).astype(BF)
    mixed = both_halves(copy_after(mixed_rows, mod_part[:1]))
    late_max = copy_after(head_max, mod_part[:1])[0]
    root_factor = jnp.sqrt(clip_limits / jnp.maximum(late_max, clip_limits))
    column_scale = jnp.repeat(root_factor, HEAD)[None, None, :]
    clipped = tuple((w[:, :2, :].astype(F32) * column_scale).astype(BF) for w in (image_qkv, text_qkv))
    grad_modulated = collect_end(mod_state, (mixed, *clipped))
    fc2_picked, fc1_picked = pieces_of(fc2_part, mod_state[3:5]), pieces_of(fc1_part, mod_state[3:5])
    fc2_got, fc1_got = swap_pieces(fc2_picked), swap_pieces(fc1_picked)
    fc2_outs = arrange(fc2_got, place, give_turned, pair_f32(BLOCKS * fc, share))
    fc1_outs = arrange(fc1_got, place, give_wide, pair_f32(share, BLOCKS * fc))
    qkv_picked, out_picked = pieces_of(qkv_part, ()), pieces_of(out_part, (grad_modulated,))
    qkv_got, out_got = swap_pieces(qkv_picked), swap_pieces(out_picked)
    out_outs = arrange(out_got, place, give_turned, pair_f32(columns, share))
    qkv_outs = arrange(qkv_got, place, give_qkv, pair_f32(share, 3, columns))

    row_block = pl.BlockSpec((half // 4, width), lambda t: (t, 0))
    vectors_spec = whole(image_mod.shape)
    tokens_grad_rows, mod_sum = stepped(
        leave_kernel,
        4,
        [SMEM] + [row_block] * 7 + [vectors_spec] * 2,
        (row_block, kept((2 * seq_count, 6, width))),
        (
            jax.ShapeDtypeStruct((half, width), F32),
            jax.ShapeDtypeStruct((2 * seq_count, 6, width), F32),
        ),
        (),
        8,
        (qkv_picked[0], fc2_picked[0], fc1_picked[0], out_picked[0]),
    )(
        info,
        grad_modulated,
        grad_first,
        branch,
        grad_mod_mlp,
        mlp_branch,
        my_rows(tokens),
        my_rows(cotangent),
        image_mod,
        text_mod,
    )
    mod_sum = mod_sum.reshape(2 * seq_count * 6, -1, share)
    mod_sum = jnp.swapaxes(mod_sum, 0, 1)
    mod_sum = mod_sum + over_core(mod_sum)
    mod_sum = sums_of_shares(mod_sum, g, q, qkv_got)
    mod_sum = mod_sum.reshape(2, seq_count, 6, share)

    return (
        mixed,
        both_halves(tokens_grad_rows),
        mod_sum[0],
        mod_sum[1],
        *qkv_outs,
        *out_outs,
        *fc1_outs,
        *fc2_outs,
        head_max[0],
        *clipped,
    )


def solution(mesh):
    devices = mesh.devices
    split = Mesh(devices.reshape(devices.shape[0] // BLOCKS, 2, 2, devices.shape[1]), ("g", "y", "x", "c"))
    dp = ("g", "y", "x")
    placed = (
        P(dp, None),
        P(dp, None),
        P(),
        P(),
        P(),
        P(),
        P(dp, None, "c"),
        P(dp, None, "c"),
        P("c", dp),
        P("c", dp),
        P(dp, "c"),
        P(dp, "c"),
        P("c", dp),
        P("c", dp),
        P("c"),
    )
    return jax.shard_map(
        local,
        mesh=split,
        in_specs=placed,
        out_specs=(
            P(dp, None),
            P(dp, None),
            P(None, None, dp),
            P(None, None, dp),
            P(dp, None, "c"),
            P(dp, None, "c"),
            P("c", dp),
            P("c", dp),
            P(dp, "c"),
            P(dp, "c"),
            P("c", dp),
            P("c", dp),
            P("c"),
            P(dp, None, "c"),
            P(dp, None, "c"),
        ),
        check_vma=False,
    )
```

```python
import functools

import jax
import jax.numpy as jnp
from jax import lax
from jax.experimental import pallas as pl
from jax.experimental.pallas import tpu as pltpu
from jax.sharding import Mesh, PartitionSpec as P

HEAD = 64
IMG = 1024
TXT = 154
EPSILON = 1e-06
NEGATIVE = -1e30
BLOCKS = 4
SUB = 128
TAIL = 1184
TAIL_PAD = 1536
EDGE = 160
CHUNK = 256
KEYS = 512
SLAB = 64
ALIGN = 16
TEXT_ROWS = 176
BF = jnp.bfloat16
F32 = jnp.float32
SWAP = [(0, 1), (1, 0)]
VMEM_LIMIT = 60 * 1024 * 1024

VMEM = pl.BlockSpec(memory_space=pltpu.VMEM)
SMEM = pl.BlockSpec(memory_space=pltpu.SMEM)
ANY = pl.BlockSpec(memory_space=pl.ANY)

COUNT, OFFSET, TEXT_FROM, TEXT_TO = 0, 4, 8, 12
CORE, TAIL_FROM, EDGE_FROM, OWN_FROM, OWN_SEQ, NEXT_FROM, HALF, INFO = 16, 17, 18, 19, 20, 21, 22, 23


def dot(a, b):
    return jnp.dot(a, b, preferred_element_type=F32)


def dot_back(a, b):
    return lax.dot_general(a, b, (((1,), (1,)), ((), ())), preferred_element_type=F32)


def dot_rows(a, b):
    return lax.dot_general(a, b, (((0,), (0,)), ((), ())), preferred_element_type=F32)


def took_us(time):
    return pl.CostEstimate(flops=int(time * 1.15e9), bytes_accessed=int(time * 1e6), transcendentals=0)


def after(body, n_in, n_deps):
    return lambda *refs: body(*refs[:n_in], *refs[n_in + n_deps :])


def whole(shape):
    return pl.BlockSpec(shape, lambda j: (0,) * len(shape), pipeline_mode=pl.Buffered(1))


def kept(shape):
    return pl.BlockSpec(shape, lambda j: (0,) * len(shape))


def block(shape):
    return pl.BlockSpec((1,) + shape, lambda j: (j,) + (0,) * len(shape))


def columns_from(rows, n, at):
    return pl.BlockSpec((rows, n), lambda j: (0, at), pipeline_mode=pl.Buffered(1))


def stepped(body, steps, in_specs, out_specs, out_shape, scratch, time, deps=()):
    run = pl.pallas_call(
        after(body, len(in_specs), len(deps)),
        grid=(steps,),
        out_shape=out_shape,
        in_specs=list(in_specs) + [ANY] * len(deps),
        out_specs=out_specs,
        scratch_shapes=list(scratch),
        compiler_params=pltpu.CompilerParams(vmem_limit_bytes=VMEM_LIMIT),
        cost_estimate=took_us(time),
    )
    return lambda *args: run(*args, *deps)


def sum_after(parts, kind, deps, time=1):
    n = len(parts)

    def body(*refs):
        total = refs[0][...].astype(F32)
        for part in refs[1:n]:
            total = total + part[...].astype(F32)
        refs[n][...] = total.astype(kind)

    return pl.pallas_call(
        after(body, n, len(deps)),
        out_shape=jax.ShapeDtypeStruct(parts[0].shape, kind),
        in_specs=[VMEM] * n + [ANY] * len(deps),
        out_specs=VMEM,
        compiler_params=pltpu.CompilerParams(vmem_limit_bytes=VMEM_LIMIT),
        cost_estimate=took_us(time),
    )(*parts, *deps)


def window(start, rows, total):
    base = jnp.minimum(lax.shift_right_logical(start, 4) * ALIGN, total - rows - ALIGN)
    return pl.ds(pl.multiple_of(base, ALIGN), rows + ALIGN), start - base


def moved(part, skip):
    rows = part.shape[0]
    shape = (rows + ALIGN, rows)
    there = lax.broadcasted_iota(jnp.int32, shape, 0) - skip
    return dot((there == lax.broadcasted_iota(jnp.int32, shape, 1)).astype(F32).astype(BF), part)


def read_rows(ref, start, rows):
    place, skip = window(start, rows, ref.shape[0])
    shape = (rows, rows + ALIGN)
    here = lax.broadcasted_iota(jnp.int32, shape, 1) - skip
    pick = (here == lax.broadcasted_iota(jnp.int32, shape, 0)).astype(F32).astype(BF)
    return dot(pick, ref[place, :]).astype(BF)


def layout_kernel(group_rows, seq, blocks, place, info, chunks):
    g, q = place[0], place[1]
    n_groups, n_seq = (blocks.shape[0] - 1) // BLOCKS, seq.shape[0] - 1
    start, stop = blocks[g * BLOCKS], blocks[g * BLOCKS + BLOCKS]

    def seq_of(position, shift):
        found = jnp.int32(0)
        for s in range(n_seq):
            found = jnp.where(position >= seq[s], s + shift, found)
        return found

    for j in range(BLOCKS):
        b = g * BLOCKS + (q ^ j)
        low, high = blocks[b], blocks[b + 1]
        text_from, text_to = jnp.int32(0), jnp.int32(0)
        for s in range(n_seq):
            first, last = jnp.maximum(seq[s] + IMG, low), jnp.minimum(seq[s + 1], high)
            text_from = jnp.where(first < last, first - low, text_from)
            text_to = jnp.where(first < last, last - low, text_to)
        info[COUNT + j] = high - low
        info[OFFSET + j] = low - start
        info[TEXT_FROM + j] = text_from
        info[TEXT_TO + j] = text_to
    own = blocks[g * BLOCKS + q]
    info[CORE] = place[2]
    info[TAIL_FROM] = jnp.maximum(stop - start - TAIL, 0)
    info[EDGE_FROM] = jnp.maximum(stop - start - EDGE, 0)
    info[OWN_FROM] = own
    info[HALF] = group_rows // (2 * BLOCKS)
    info[OWN_SEQ] = seq_of(own, 0)
    info[NEXT_FROM] = seq[seq_of(own, 0) + 1]

    def span(steps):
        there = (g + steps >= 0) & (g + steps < n_groups)
        at = jnp.clip(g + steps, 0, n_groups - 1) * BLOCKS
        return jnp.where(there, blocks[at], 0), jnp.where(there, blocks[at + BLOCKS], 0)

    before, behind, ahead, beyond = span(-2), span(-1), span(1), span(2)
    n_chunks = (2 * KEYS + 2 * TAIL_PAD + group_rows) // KEYS
    i = 0
    for base, low, high, rows in (
        (jnp.maximum(before[1] - EDGE, before[0]) - (KEYS - EDGE), jnp.maximum(before[1] - EDGE, before[0]), before[1], KEYS),
        (
            jnp.maximum(behind[1] - TAIL, behind[0]) - (TAIL_PAD - TAIL),
            jnp.maximum(behind[1] - TAIL, behind[0]),
            behind[1],
            TAIL_PAD,
        ),
        (start, start, stop, group_rows),
        (ahead[0], ahead[0], jnp.minimum(ahead[1], ahead[0] + TAIL), TAIL_PAD),
        (beyond[0], beyond[0], jnp.minimum(beyond[1], beyond[0] + EDGE), KEYS),
    ):
        for step in range(rows // KEYS):
            chunks[i] = base + step * KEYS
            chunks[n_chunks + i] = low
            chunks[2 * n_chunks + i] = high
            i += 1
    n_tiles = group_rows // CHUNK
    for t in range(n_tiles):
        first = start + t * CHUNK
        last = jnp.minimum(first + CHUNK, stop) - 1
        chunks[3 * n_chunks + 2 * t] = jnp.where(first < stop, seq[seq_of(first, 0)], 0)
        chunks[3 * n_chunks + 2 * t + 1] = jnp.where(first < stop, seq[seq_of(last, 1)], 0)
        one = (first + CHUNK <= stop) & (seq_of(first, 0) == seq_of(last, 0))
        chunks[3 * n_chunks + 2 * n_tiles + 2 + t] = jnp.where(one, 1, 0)
    chunks[3 * n_chunks + 3 * n_tiles + 2] = seq[seq_of(start, 0)]
    chunks[3 * n_chunks + 3 * n_tiles + 3] = seq[seq_of(stop - 1, 1)]
    chunks[3 * n_chunks + 2 * n_tiles] = start
    chunks[3 * n_chunks + 2 * n_tiles + 1] = stop


def lane_spans(chunks, seq, n_chunks, n_tiles, t):
    start, stop = chunks[3 * n_chunks + 2 * n_tiles], chunks[3 * n_chunks + 2 * n_tiles + 1]
    position = start + t * CHUNK + lax.broadcasted_iota(jnp.int32, (1, CHUNK), 1)
    low, high = jnp.zeros_like(position), jnp.zeros_like(position)
    for s in range(seq.shape[0] - 1):
        hit = (position >= seq[s]) & (position < seq[s + 1]) & (position < stop)
        low, high = jnp.where(hit, seq[s], low), jnp.where(hit, seq[s + 1], high)
    return low, high


def own_kinds(info, first, rows):
    ids = row_ids(info[CORE] * info[HALF] + first, rows)
    live = ids < info[COUNT]
    is_text = live & (ids >= info[TEXT_FROM]) & (ids < info[TEXT_TO])
    is_next = live & (info[OWN_FROM] + ids >= info[NEXT_FROM])
    return live, live & jnp.logical_not(is_text | is_next), is_next, is_text


def vector_of(info, image_mod, text_mod, is_next, is_text):
    s = info[OWN_SEQ]
    after_s = jnp.minimum(s + 1, image_mod.shape[0] - 1)

    def pick(i):
        own, text, following = image_mod[s][i : i + 1], text_mod[s][i : i + 1], image_mod[after_s][i : i + 1]
        return jnp.where(is_text, text, jnp.where(is_next, following, own))

    return pick


def normal(rows):
    centered = rows - jnp.mean(rows, axis=1, keepdims=True)
    inverse = lax.rsqrt(jnp.mean(centered * centered, axis=1, keepdims=True) + EPSILON)
    return centered * inverse, inverse


def normal_back(grad, normed, inverse):
    return inverse * (
        grad - jnp.mean(grad, axis=1, keepdims=True) - normed * jnp.mean(grad * normed, axis=1, keepdims=True)
    )


def enter_kernel(info, tokens, cotangent, image_mod, text_mod, modulated, grad_mlp):
    half = modulated.shape[0]
    place = pl.ds(pl.multiple_of(info[CORE] * half, half), half)
    live, _, is_next, is_text = own_kinds(info, 0, half)
    pick = vector_of(info, image_mod, text_mod, is_next, is_text)
    normed, _ = normal(tokens[place, :].astype(F32))
    modulated[...] = (normed * (1.0 + pick(1)) + pick(0)).astype(BF)
    grad_mlp[...] = (pick(5) * jnp.where(live, cotangent[place, :].astype(F32), 0.0)).astype(BF)


def collected(mine, first_x, first_y, last_x, last_y, out):
    cut = out.shape[0] // 2
    out[:cut, :] = mine[:cut, :].astype(F32) + first_x[...].astype(F32) + last_y[...].astype(F32)
    out[cut:, :] = mine[cut:, :].astype(F32) + last_x[...].astype(F32) + first_y[...].astype(F32)


def middle_kernel(
    info, mine, first_x, first_y, last_x, last_y, tokens, image_mod, text_mod, branch, modulated_mlp
):
    collected(mine, first_x, first_y, last_x, last_y, branch)
    _, _, is_next, is_text = own_kinds(info, 0, branch.shape[0])
    pick = vector_of(info, image_mod, text_mod, is_next, is_text)
    normed, _ = normal(tokens[...].astype(F32) + pick(2) * branch[...])
    modulated_mlp[...] = (normed * (1.0 + pick(4)) + pick(3)).astype(BF)


def turn_kernel(
    info, mine, first_x, first_y, last_x, last_y, branch, tokens, cotangent, image_mod, text_mod,
    grad_mod_mlp, grad_first, grad_branch,
):
    collected(mine, first_x, first_y, last_x, last_y, grad_mod_mlp)
    live, _, is_next, is_text = own_kinds(info, 0, branch.shape[0])
    pick = vector_of(info, image_mod, text_mod, is_next, is_text)
    normed, inverse = normal(tokens[...].astype(F32) + pick(2) * branch[...])
    back = normal_back(grad_mod_mlp[...] * (1.0 + pick(4)), normed, inverse)
    result = jnp.where(live, cotangent[...].astype(F32) + back, 0.0)
    grad_first[...] = result
    grad_branch[...] = (pick(2) * result).astype(BF)


def leave_kernel(
    info, mine, first_x, first_y, last_x, last_y,
    mlp_mine, mlp_first_x, mlp_first_y, mlp_last_x, mlp_last_y,
    grad_first, branch, grad_mod_mlp, tokens, cotangent, image_mod, text_mod,
    tokens_grad, mixed, sums, grad_modulated, mlp_branch,
):
    collected(mine, first_x, first_y, last_x, last_y, grad_modulated)
    collected(mlp_mine, mlp_first_x, mlp_first_y, mlp_last_x, mlp_last_y, mlp_branch)
    sums[...] = jnp.zeros_like(sums)
    n_seq = image_mod.shape[0]
    s = info[OWN_SEQ]
    after_s = jnp.minimum(s + 1, n_seq - 1)
    step = 64
    for low in range(0, tokens_grad.shape[0], step):
        part = slice(low, low + step)
        live, is_own, is_next, is_text = own_kinds(info, low, step)
        pick = vector_of(info, image_mod, text_mod, is_next, is_text)
        rows = tokens[part, :].astype(F32)
        normed, inverse = normal(rows)
        first = rows + pick(2) * branch[part, :]
        normed_mlp, _ = normal(first)

        def add(i, term):
            for kept_rows, at in ((is_own, s), (is_next, after_s), (is_text, n_seq + s)):
                row = jnp.sum(jnp.where(kept_rows, term, 0.0), axis=0, keepdims=True)
                sums[at, i : i + 1, :] += row

        grads = grad_modulated[part, :]
        add(0, grads)
        add(1, grads * normed)
        add(2, grad_first[part, :] * branch[part, :])
        add(3, grad_mod_mlp[part, :])
        add(4, grad_mod_mlp[part, :] * normed_mlp)
        add(5, cotangent[part, :].astype(F32) * mlp_branch[part, :])
        back = normal_back(grads * (1.0 + pick(1)), normed, inverse)
        tokens_grad[part, :] = jnp.where(live, grad_first[part, :] + back, 0.0)
        mixed[part, :] = jnp.where(live, first + pick(5) * mlp_branch[part, :], 0.0).astype(BF)


def row_ids(base, rows):
    return base + lax.broadcasted_iota(jnp.int32, (rows, 1), 0)


def for_rows(info, cap, body):
    count = info[COUNT + pl.program_id(0)]
    low = 0
    for rows in range(cap // 2, cap + 1, SUB):

        @pl.when((count > low) & (count <= rows))
        def _():
            body(rows)

        low = rows


def for_text(info, cap, body):
    j = pl.program_id(0)
    low, high = info[TEXT_FROM + j], info[TEXT_TO + j]

    @pl.when(high > low)
    def _():
        base = jnp.minimum(lax.shift_right_logical(low, 4) * ALIGN, cap - TEXT_ROWS)
        base = pl.multiple_of(base, ALIGN)
        ids = row_ids(base, TEXT_ROWS)
        body(pl.ds(base, TEXT_ROWS), (ids >= low) & (ids < high))


def half_places(info, half):
    mine = pl.multiple_of(info[CORE] * half, half)
    return pl.ds(mine, half), pl.ds(pl.multiple_of(half - mine, half), half)


def join(info, own, oth, out):
    half = own.shape[1]
    at_own, at_oth = half_places(info, half)
    out[at_own, :] = own[0]
    out[at_oth, :] = oth[0]


def part_ways(info, rows_ref, own, oth):
    half = own.shape[1]
    at_own, at_oth = half_places(info, half)
    own[0] = rows_ref[at_own, :]
    oth[0] = rows_ref[at_oth, :]


def split_columns(w, first, image, text):
    n = image.shape[1]
    image[...] = w[:, first : first + n]
    text[...] = w[:, first + n : first + 2 * n]


def to_group_rows(info, own, oth, w_image, w_text, out, joined, tile):
    cap = joined.shape[0]
    join(info, own, oth, joined)

    @pl.when(pl.program_id(0) == 0)
    def _():
        out[...] = jnp.zeros_like(out)

    def body(rows):
        tile[:rows, :] = dot(joined[:rows, :], w_image[...]).astype(BF)

        def text(place, is_text):
            tile[place, :] = jnp.where(is_text, dot(joined[place, :], w_text[...]).astype(BF), tile[place, :])

        for_text(info, cap, text)
        j = pl.program_id(0)
        place, skip = window(info[OFFSET + j], rows, out.shape[0])
        part = moved(tile[:rows, :], skip).astype(BF)
        ids = row_ids(-skip, rows + ALIGN)
        out[place, :] = jnp.where((ids >= 0) & (ids < info[COUNT + j]), part, out[place, :])

    for_rows(info, cap, body)


def project_kernel(info, own, oth, w, q, kv, tail, edge, head, head_edge, w_image, w_text, out, joined, tile):
    @pl.when(pl.program_id(0) == 0)
    def _():
        split_columns(w, 0, w_image, w_text)

    to_group_rows(info, own, oth, w_image, w_text, out, joined, tile)

    @pl.when(pl.program_id(0) == BLOCKS - 1)
    def _():
        n = q.shape[1]
        q[...] = out[:, :n]
        kv[...] = out[:, n:]
        tail[...] = read_rows(kv, info[TAIL_FROM], TAIL)
        edge[...] = read_rows(kv, info[EDGE_FROM], EDGE)
        head[...] = kv[:TAIL, :]
        head_edge[...] = kv[:EDGE, :]


def back_project_kernel(first, info, own, oth, w, out, w_image, w_text, joined, tile):
    @pl.when(pl.program_id(0) == 0)
    def _():
        split_columns(w, first, w_image, w_text)

    to_group_rows(info, own, oth, w_image, w_text, out, joined, tile)


def times_turned(info, x, w_image, w_text, result):
    cap = result.shape[0]

    def body(rows):
        result[:rows, :] = dot_back(x[:rows, :], w_image[...]).astype(BF)
        if rows < cap:
            result[rows:, :] = jnp.zeros((cap - rows, result.shape[1]), BF)

        def text(place, is_text):
            part = dot_back(x[place, :], w_text[...]).astype(BF)
            result[place, :] = jnp.where(is_text, part, result[place, :])

        for_text(info, cap, text)

    for_rows(info, cap, body)


def rows_to_slots_kernel(first, info, rows_ref, w, own, oth, w_image, w_text, x, result):
    j = pl.program_id(0)

    @pl.when(j == 0)
    def _():
        split_columns(w, first, w_image, w_text)

    def take(rows):
        x[:rows, :] = read_rows(rows_ref, info[OFFSET + j], rows)

    for_rows(info, x.shape[0], take)
    times_turned(info, x, w_image, w_text, result)
    part_ways(info, result, own, oth)


def slots_to_slots_kernel(info, x, w_image, w_text, own, oth, result):
    times_turned(info, x.at[0], w_image, w_text, result)
    part_ways(info, result, own, oth)


def gelu_parts(v):
    k = 0.7978845608028654
    square = v * v
    t = jnp.tanh(k * v * (1.0 + 0.044715 * square))
    half = 0.5 * (1.0 + t)
    return v * half, half + 0.5 * v * (1.0 - t * t) * (k + 3 * 0.044715 * k * square)


def mlp_up_kernel(info, x_own, x_oth, w_image, w_text, hid, slope, x, before):
    cap = x.shape[0]
    join(info, x_own, x_oth, x)

    def body(rows):
        before[:rows, :] = dot(x[:rows, :], w_image[...])

        def text(place, is_text):
            before[place, :] = jnp.where(is_text, dot(x[place, :], w_text[...]), before[place, :])

        for_text(info, cap, text)
        value, steep = gelu_parts(before[:rows, :])
        hid[0, :rows, :] = value.astype(BF)
        slope[0, :rows, :] = steep.astype(BF)
        if rows < cap:
            for ref in (hid, slope):
                ref[0, rows:, :] = jnp.zeros((cap - rows, ref.shape[2]), BF)

    for_rows(info, cap, body)


def mlp_back_kernel(
    info, g_own, g_oth, slope, upper_image, upper_text, lower_image, lower_text, gm_own, gm_oth, gb, g, back, result
):
    cap = g.shape[0]
    join(info, g_own, g_oth, g)

    def body(rows):
        back[:rows, :] = dot(g[:rows, :], lower_image[...]).astype(BF)

        def text(place, is_text):
            back[place, :] = jnp.where(is_text, dot(g[place, :], lower_text[...]).astype(BF), back[place, :])

        for_text(info, cap, text)
        gb[0, :rows, :] = (back[:rows, :].astype(F32) * slope[0, :rows, :].astype(F32)).astype(BF)
        if rows < cap:
            gb[0, rows:, :] = jnp.zeros((cap - rows, gb.shape[2]), BF)

    for_rows(info, cap, body)
    times_turned(info, gb.at[0], upper_image, upper_text, result)
    part_ways(info, result, gm_own, gm_oth)


def add_sums(info, left, right, acc_image, acc_text):
    cap = left.shape[0]
    j = pl.program_id(0)

    @pl.when(j == 0)
    def _():
        acc_image[...] = jnp.zeros_like(acc_image)
        acc_text[...] = jnp.zeros_like(acc_text)

    def body(rows):
        ids = row_ids(0, rows)
        is_text = (ids >= info[TEXT_FROM + j]) & (ids < info[TEXT_TO + j])
        is_image = (ids < info[COUNT + j]) & jnp.logical_not(is_text)
        acc_image[...] += dot_rows(left[:rows, :], jnp.where(is_image, right[:rows, :], jnp.zeros((), BF)))

    for_rows(info, cap, body)

    def text(place, is_text):
        acc_text[...] += dot_rows(left[place, :], jnp.where(is_text, right[place, :], jnp.zeros((), BF)))

    for_text(info, cap, text)


def give_sums(out, acc_image, acc_text):
    cut = acc_image.shape[1]

    @pl.when(pl.program_id(0) == BLOCKS - 1)
    def _():
        out[:, :cut] = acc_image[...].astype(BF)
        out[:, cut:] = acc_text[...].astype(BF)


def slot_sums_kernel(info, l_own, l_oth, right, out, acc_image, acc_text, left):
    join(info, l_own, l_oth, left)
    add_sums(info, left, right.at[0], acc_image, acc_text)
    give_sums(out, acc_image, acc_text)


def row_sums_kernel(info, l_own, l_oth, rows_ref, out, acc_image, acc_text, left, right):
    join(info, l_own, l_oth, left)

    def take(rows):
        right[:rows, :] = read_rows(rows_ref, info[OFFSET + pl.program_id(0)], rows)

    for_rows(info, left.shape[0], take)
    add_sums(info, left, right, acc_image, acc_text)
    give_sums(out, acc_image, acc_text)


def head_rows(turned, h):
    ids = lax.broadcasted_iota(jnp.int32, turned.shape, 0)
    return jnp.where((ids >= h * HEAD) & (ids < (h + 1) * HEAD), turned, 0)


def head_columns(plain, h):
    ids = lax.broadcasted_iota(jnp.int32, plain.shape, 1)
    return jnp.where((ids >= h * HEAD) & (ids < (h + 1) * HEAD), plain, 0)


def fold(combine, rows):
    parts = [rows[at : at + 8, :] for at in range(0, rows.shape[0], 8)]
    while len(parts) > 1:
        parts = [combine(a, b) for a, b in zip(parts[::2], parts[1::2])]
    return parts[0]


def slab_mask(chunks, i, n_chunks, low, q_from, q_to):
    position = chunks[i] + low + lax.broadcasted_iota(jnp.int32, (SLAB, 1), 0)
    valid = (position >= chunks[n_chunks + i]) & (position < chunks[2 * n_chunks + i])
    position = jnp.where(valid, position, -1)
    return (position >= q_from) & (position < q_to)


def for_chunks(chunks, n_chunks, t, body):
    low, high = chunks[3 * n_chunks + 2 * t], chunks[3 * n_chunks + 2 * t + 1]
    one = chunks[3 * n_chunks + 2 * pl.num_programs(0) + 2 + t] > 0

    def step(i, carry):
        base = chunks[i]
        start = jnp.maximum(base, chunks[n_chunks + i])
        stop = jnp.minimum(base + KEYS, chunks[2 * n_chunks + i])
        reached = (start < high) & (stop > low) & (start < stop)
        inside = one & (start == base) & (stop == base + KEYS) & (base >= low) & (stop <= high)

        @pl.when(reached & inside)
        def _():
            body(i, True)

        @pl.when(reached & jnp.logical_not(inside))
        def _():
            body(i, False)

        return carry

    lax.fori_loop(0, n_chunks, step, 0)


def sources_at(far_back, near_back, kv, near_on, far_on):
    chunk = 0
    for source, size, last in (
        (far_back, KEYS, True),
        (near_back, TAIL_PAD, True),
        (kv, kv.shape[0], False),
        (near_on, TAIL_PAD, False),
        (far_on, KEYS, False),
    ):
        rows = source.shape[0]
        skip = size - rows if last else 0
        for low in range(0, size, KEYS):
            first, stop = max(low, skip), min(low + KEYS, skip + rows)
            yield chunk, source, slice(first - skip, stop - skip), first - low, stop - low
            chunk += 1


def if_reached(chunks, n_chunks, i, body, otherwise=None):
    last = 3 * n_chunks + 3 * pl.num_programs(0) + 2
    start = jnp.maximum(chunks[i], chunks[n_chunks + i])
    stop = jnp.minimum(chunks[i] + KEYS, chunks[2 * n_chunks + i])
    reached = (start < chunks[last + 1]) & (stop > chunks[last]) & (start < stop)
    pl.when(reached)(body)
    if otherwise:
        pl.when(jnp.logical_not(reached))(otherwise)


def gather_keys(chunks, sources, k, v, plain, turned):
    n = k.shape[1]
    n_chunks = k.shape[0] // KEYS
    for i, source, rows, first, stop in sources_at(*sources):

        def take():
            at = i * KEYS
            for ref, columns in ((k, slice(0, n)), (v, slice(n, 2 * n))):
                ref[at + first : at + stop, :] = source[rows, columns]
                for low, high in ((0, first), (stop, KEYS)):
                    if low < high:
                        ref[at + low : at + high, :] = jnp.zeros((high - low, n), BF)
            part = slice(at, at + KEYS)
            turned[:, part] = plain[part, :].T

        if_reached(chunks, n_chunks, i, take)


def attend_kernel(
    chunks, seq, q, far_back, near_back, kv, near_on, far_on,
    out, exact, lse, top,
    k, v, v_turned, q_turn, logits, probs, total, high,
):
    t = pl.program_id(0)
    n_chunks = k.shape[0] // KEYS
    heads = q.shape[1] // HEAD
    wide = q.shape[0]

    @pl.when(t == 0)
    def _():
        gather_keys(chunks, (far_back, near_back, kv, near_on, far_on), k, v, v, v_turned)
        top[...] = jnp.full_like(top, NEGATIVE)

    live = chunks[3 * n_chunks + 2 * t + 1] > 0

    @pl.when(live)
    def _():
        turned = (q[...].astype(F32) * HEAD**-0.5).T
        for h in range(heads):
            q_turn[h] = head_rows(turned, h).astype(BF)
        lanes_from, lanes_to = lane_spans(chunks, seq, n_chunks, pl.num_programs(0), t)
        total[...] = jnp.zeros_like(total)
        high[...] = jnp.full_like(high, NEGATIVE)

        def first(i, whole_chunk):
            place = pl.ds(pl.multiple_of(i * KEYS, KEYS), KEYS)
            for h in range(heads):
                logits[h, i] = dot(k[place, :], q_turn[h])
            for low in range(0, KEYS, SLAB):
                part = slice(low, low + SLAB)
                if not whole_chunk:
                    mask = slab_mask(chunks, i, n_chunks, low, lanes_from, lanes_to)
                for h in range(heads):
                    values = logits[h, i, part, :]
                    if not whole_chunk:
                        values = jnp.where(mask, values, NEGATIVE)
                        logits[h, i, part, :] = values
                    rows = slice(8 * h, 8 * h + 8)
                    high[rows, :] = jnp.maximum(high[rows, :], fold(jnp.maximum, values))

        for_chunks(chunks, n_chunks, t, first)
        tops = [jnp.max(high[8 * h : 8 * h + 8, :], axis=0, keepdims=True) for h in range(heads)]
        high[...] = jnp.zeros_like(high)

        def second(i, whole_chunk):
            place = pl.ds(pl.multiple_of(i * KEYS, KEYS), KEYS)
            for low in range(0, KEYS, SLAB):
                part = slice(low, low + SLAB)
                for h in range(heads):
                    p = jnp.exp(logits[h, i, part, :] - tops[h])
                    rows = slice(8 * h, 8 * h + 8)
                    high[rows, :] += fold(jnp.add, p)
                    probs[part, h * wide : (h + 1) * wide] = p.astype(BF)
            for h in range(heads):
                rows = slice(h * HEAD, (h + 1) * HEAD)
                total[rows, :] += dot(v_turned[rows, place], probs[:, h * wide : (h + 1) * wide])

        for_chunks(chunks, n_chunks, t, second)
        for h in range(heads):
            rows = slice(h * HEAD, (h + 1) * HEAD)
            sums = jnp.sum(high[8 * h : 8 * h + 8, :], axis=0, keepdims=True)
            total[rows, :] = total[rows, :] / sums
            lse[0, h : h + 1, :] = tops[h] + jnp.log(sums)
            seen = jnp.where(lanes_to > lanes_from, tops[h], NEGATIVE)
            top[h : h + 1, :] = jnp.maximum(top[h : h + 1, :], seen)
        result = total[...].T
        exact[...] = result
        out[...] = result.astype(BF)

    @pl.when(jnp.logical_not(live))
    def _():
        exact[...] = jnp.zeros_like(exact)
        out[...] = jnp.zeros_like(out)
        lse[...] = jnp.zeros_like(lse)


def attend_back_kernel(
    chunks, seq, q, g, attended, far_back, near_back, kv, near_on, far_on, lse,
    dq, d_far_back, d_near_back, d_kv, d_near_on, d_far_on,
    k, v, k_turned, q_stack, g_stack, q_turn, g_turn, logits, grads_of, probs, grad_logits, total, dk, dv,
):
    t = pl.program_id(0)
    n_chunks = k.shape[0] // KEYS
    heads = q.shape[1] // HEAD
    wide = q.shape[0]

    @pl.when(t == 0)
    def _():
        gather_keys(chunks, (far_back, near_back, kv, near_on, far_on), k, v, k, k_turned)
        for i in range(n_chunks):

            def clear():
                dk[i * KEYS : (i + 1) * KEYS, :] = jnp.zeros((KEYS, dk.shape[1]), F32)
                dv[i * KEYS : (i + 1) * KEYS, :] = jnp.zeros((KEYS, dk.shape[1]), F32)

            if_reached(chunks, n_chunks, i, clear)

    live = chunks[3 * n_chunks + 2 * t + 1] > 0

    @pl.when(live)
    def _():
        scaled = q[...].astype(F32) * HEAD**-0.5
        grads = g[...].astype(F32)
        q_turned, g_turned = scaled.T, grads.T
        product = g_turned * attended[...].T
        delta, logs = [], []
        for h in range(heads):
            rows = slice(h * wide, (h + 1) * wide)
            q_stack[rows, :] = head_columns(scaled, h).astype(BF)
            g_stack[rows, :] = head_columns(grads, h).astype(BF)
            q_turn[h] = head_rows(q_turned, h).astype(BF)
            g_turn[h] = head_rows(g_turned, h).astype(BF)
            delta.append(jnp.sum(product[h * HEAD : (h + 1) * HEAD, :], axis=0, keepdims=True))
            logs.append(lse[0, h : h + 1, :])
        lanes_from, lanes_to = lane_spans(chunks, seq, n_chunks, pl.num_programs(0), t)
        total[...] = jnp.zeros_like(total)

        def body(i, whole_chunk):
            place = pl.ds(pl.multiple_of(i * KEYS, KEYS), KEYS)
            for h in range(heads):
                logits[h] = dot(k[place, :], q_turn[h])
                grads_of[h] = dot(v[place, :], g_turn[h])
            for low in range(0, KEYS, SLAB):
                part = slice(low, low + SLAB)
                if not whole_chunk:
                    mask = slab_mask(chunks, i, n_chunks, low, lanes_from, lanes_to)
                for h in range(heads):
                    lanes = slice(h * wide, (h + 1) * wide)
                    p = jnp.exp(logits[h, part, :] - logs[h])
                    if not whole_chunk:
                        p = jnp.where(mask, p, 0.0)
                    probs[part, lanes] = p.astype(BF)
                    grad_logits[part, lanes] = (p * (grads_of[h, part, :] - delta[h])).astype(BF)
            for h in range(heads):
                rows = slice(h * HEAD, (h + 1) * HEAD)
                total[rows, :] += dot(k_turned[rows, place], grad_logits[:, h * wide : (h + 1) * wide])
            dv[place, :] += dot(probs[...], g_stack[...])
            dk[place, :] += dot(grad_logits[...], q_stack[...])

        for_chunks(chunks, n_chunks, t, body)
        dq[...] = (total[...].T * HEAD**-0.5).astype(BF)

    @pl.when(jnp.logical_not(live))
    def _():
        dq[...] = jnp.zeros_like(dq)

    @pl.when(t == pl.num_programs(0) - 1)
    def _():
        n = dk.shape[1]
        for i, out, rows, first, stop in sources_at(d_far_back, d_near_back, d_kv, d_near_on, d_far_on):

            def give():
                place = slice(i * KEYS + first, i * KEYS + stop)
                out[rows, :n] = dk[place, :].astype(out.dtype)
                out[rows, n:] = dv[place, :].astype(out.dtype)

            def blank():
                out[rows, :] = jnp.zeros((stop - first, 2 * n), out.dtype)

            if_reached(chunks, n_chunks, i, give, blank)


def gather_grads_kernel(info, dq, d_kv, near_back, near_on, far_back, far_on, out, total):
    total[...] = d_kv[...]
    for start, part in ((info[TAIL_FROM], near_back), (info[EDGE_FROM], far_back)):
        place, skip = window(start, part.shape[0], total.shape[0])
        total[place, :] += moved(part[...], skip)
    for part in (near_on, far_on):
        total[: part.shape[0], :] += part[...].astype(F32)
    n = dq.shape[1]
    out[:, :n] = dq[...]
    out[:, n:] = total[...].astype(BF)


def copy_after(source, deps):
    return sum_after([source], source.dtype, deps)


def shift(value, steps):
    count = lax.axis_size("g")
    pairs = [(i, i + steps) for i in range(count) if 0 <= i + steps < count]
    if not pairs:
        return jnp.zeros_like(value)
    return lax.ppermute(value, "g", pairs)


def if_needed(predicate, run, *values):
    return lax.cond(predicate, run, lambda *v: tuple(jnp.zeros_like(a) for a in v), *values)


def over_x(value):
    return lax.ppermute(value, "x", SWAP)


def over_y(value):
    return lax.ppermute(value, "y", SWAP)


def over_core(value):
    return lax.ppermute(value, "c", SWAP)


def over_xy(value):
    return lax.ppermute(value, ("y", "x"), [(0, 3), (1, 2), (2, 1), (3, 0)])


def over_groups(sums):
    return lax.psum_scatter(sums, "g", scatter_dimension=0, tiled=True)


def spread_begin(value):
    return value, over_x(value), over_y(value)


def spread_next(begun, deps=()):
    value, from_x, from_y = begun
    cut = value.shape[0] // 2
    on_y, on_x = from_x[:cut], from_y[cut:]
    if deps:
        on_y, on_x = sum_after([on_y], BF, deps), sum_after([on_x], BF, deps)
    return value, from_x, from_y, on_y, on_x, over_y(on_y), over_x(on_x)


def spread_end(state, deps=()):
    value, from_x, from_y, _, _, low, high = state
    if deps:
        low, high = sum_after([low], BF, deps), sum_after([high], BF, deps)
    own = jnp.stack([value, from_x, from_y, jnp.concatenate([low, high], axis=0)])
    return own, over_core(own)


def spread(value, deps=()):
    return spread_end(spread_next(spread_begin(value), deps))


def add16(*parts):
    total = parts[0].astype(F32)
    for part in parts[1:]:
        total = total + part.astype(F32)
    return total


def core_sum(own, oth, deps=(), time=3):
    other = over_core(oth)
    half, width = own.shape[1:]
    cut = half // 2
    cuts = ((0, 0, half), (3, 0, cut), (3, cut, half), (1, 0, cut), (1, cut, half), (2, 0, cut), (2, cut, half))

    def body(*refs):
        for out, (j, low, high) in zip(refs[2:], cuts):
            out[...] = (refs[0][j, low:high, :].astype(F32) + refs[1][j, low:high, :].astype(F32)).astype(BF)

    return pl.pallas_call(
        after(body, 2, len(deps)),
        out_shape=tuple(jax.ShapeDtypeStruct((high - low, width), BF) for _, low, high in cuts),
        in_specs=[VMEM] * 2 + [ANY] * len(deps),
        out_specs=(VMEM,) * len(cuts),
        compiler_params=pltpu.CompilerParams(vmem_limit_bytes=VMEM_LIMIT),
        cost_estimate=took_us(time),
    )(own, other, *deps)


def collect_begin(pieces):
    mine, far_x, far_y, x_low, x_high, y_low, y_high = pieces
    from_x, from_y = over_x(far_x), over_y(far_y)
    return mine, x_high, y_low, from_x, from_y, over_x(x_low), over_y(y_high)


def collect_next(begun, deps=(), time=1):
    mine, x_high, y_low, from_x, from_y, first_x, first_y = begun
    on_x, on_y = sum_after((x_high, from_y), BF, deps, time), sum_after((y_low, from_x), BF, deps, time)
    return mine, first_x, first_y, on_x, on_y, over_x(on_x), over_y(on_y)


def sums_of_shares(shares, top_rows, g, q, deps):
    groups = lax.axis_size("g")
    pick = lambda values, at: lax.dynamic_index_in_dim(values, at, 0, keepdims=False)
    is_top = (jnp.arange(shares.shape[1]) >= shares.shape[1] - top_rows)[:, None]
    join = lambda a, b: jnp.where(is_top, jnp.maximum(a, b), a + b)
    shares = jnp.moveaxis(shares.reshape((groups, BLOCKS) + shares.shape[1:]), 1, 0)
    got = [over_x(pick(shares, q ^ 1)), over_y(pick(shares, q ^ 2)), over_xy(pick(shares, q ^ 3))]
    shares = join(join(pick(shares, q), got[0]), join(got[1], got[2]))
    shares = sum_after([shares], F32, deps)
    total = pick(shares, g)
    for step in range(1, groups):
        pairs = [(i, (i + step) % groups) for i in range(groups)]
        total = join(total, lax.ppermute(pick(shares, lax.rem(g + step, groups)), "g", pairs))
    return total


def pick_pieces(pieces, place, deps=()):
    shape = pieces.shape[1:]

    def body(place_ref, source, *outs):
        for j, out in enumerate(outs):
            out[...] = source[place_ref[1] ^ j]

    return pl.pallas_call(
        after(body, 2, len(deps)),
        out_shape=(jax.ShapeDtypeStruct(shape, pieces.dtype),) * BLOCKS,
        in_specs=[SMEM, VMEM] + [ANY] * len(deps),
        out_specs=(VMEM,) * BLOCKS,
        compiler_params=pltpu.CompilerParams(vmem_limit_bytes=VMEM_LIMIT),
        cost_estimate=took_us(2),
    )(place, pieces, *deps)


def swap_pieces(picked):
    own, to_x, to_y, to_xy = picked
    return own, over_x(to_x), over_y(to_y), over_xy(to_xy)


def exchange(pieces, place):
    return swap_pieces(pick_pieces(pieces, place))


def arrange(got, place, body, out_shape, deps=(), time=2):
    n = len(got)

    def kernel(place_ref, *refs):
        for j in range(n):
            body(place_ref[1] ^ j, refs[j], refs[n:])

    return pl.pallas_call(
        after(kernel, 1 + n, len(deps)),
        out_shape=out_shape,
        in_specs=[SMEM] + [VMEM] * n + [ANY] * len(deps),
        out_specs=(VMEM,) * len(out_shape),
        compiler_params=pltpu.CompilerParams(vmem_limit_bytes=VMEM_LIMIT),
        cost_estimate=took_us(time),
    )(place, *got, *deps)


def stack_rows(b, piece, outs):
    rows, at = piece.shape[0], 0
    for out in outs:
        n = out.shape[1]
        out[pl.ds(pl.multiple_of(b * rows, ALIGN), rows), :] = piece[:, at : at + n]
        at += n


def give_wide(b, piece, outs):
    n = piece.shape[1] // 2
    for k, out in enumerate(outs):
        out[:, pl.ds(pl.multiple_of(b * n, SUB), n)] = piece[:, k * n : (k + 1) * n].astype(F32)


def give_qkv(b, piece, outs):
    n = piece.shape[1] // 6
    for at in range(BLOCKS):

        @pl.when(b == at)
        def _():
            for k, out in enumerate(outs):
                for p in range(3):
                    out[p, :, at * n : (at + 1) * n] = piece[:, (3 * k + p) * n : (3 * k + p + 1) * n].astype(F32)


def give_narrow(b, piece, outs):
    n = piece.shape[1] // 2
    for at in range(BLOCKS):

        @pl.when(b == at)
        def _():
            for k, out in enumerate(outs):
                out[:, at * n : (at + 1) * n] = piece[:, k * n : (k + 1) * n].astype(F32)


def local(
    tokens,
    cotangent,
    seq_offsets,
    block_offsets,
    image_mod,
    text_mod,
    image_qkv,
    text_qkv,
    image_out,
    text_out,
    image_fc1,
    text_fc1,
    image_fc2,
    text_fc2,
    clip_limits,
):
    rows_cap, width = tokens.shape
    half = rows_cap // 2
    share = image_qkv.shape[0]
    columns = image_qkv.shape[2]
    group_rows = BLOCKS * rows_cap
    mine = columns // BLOCKS
    fc = image_fc1.shape[1] // BLOCKS
    heads = mine // HEAD
    seq_count = seq_offsets.shape[0] - 1
    n_groups = lax.axis_size("g")
    g, c = lax.axis_index("g"), lax.axis_index("c")
    q = 2 * lax.axis_index("y") + lax.axis_index("x")

    def both_halves(rows):
        other = over_core(rows)
        return jnp.where(c == 0, jnp.concatenate([rows, other], axis=0), jnp.concatenate([other, rows], axis=0))

    def quarter(inputs):
        return jnp.moveaxis(inputs.reshape(share, -1, BLOCKS, mine), 2, 0).reshape(BLOCKS, share, -1)

    def quarter_turned(inputs):
        return jnp.swapaxes(inputs.reshape(BLOCKS, -1, share), 1, 2)

    def quarter_wide(inputs):
        return jnp.swapaxes(inputs.reshape(share, BLOCKS, -1), 0, 1)

    pack_qkv = jnp.concatenate([quarter(image_qkv), quarter(text_qkv)], axis=2)
    place = jnp.stack([g, q, c]).astype(jnp.int32)
    plane_of = lambda *cuts: tuple(jax.ShapeDtypeStruct((BLOCKS * share, n), BF) for n in cuts)
    (plane_qkv,) = arrange(exchange(pack_qkv, place), place, stack_rows, plane_of(6 * mine))

    n_tiles = group_rows // CHUNK
    reach = 2 * KEYS + 2 * TAIL_PAD + group_rows
    n_chunks = reach // KEYS
    info, chunks = pl.pallas_call(
        functools.partial(layout_kernel, group_rows),
        out_shape=(
            jax.ShapeDtypeStruct((INFO,), jnp.int32),
            jax.ShapeDtypeStruct((3 * n_chunks + 3 * n_tiles + 4,), jnp.int32),
        ),
        in_specs=[SMEM] * 3,
        out_specs=(SMEM, SMEM),
        cost_estimate=took_us(1),
    )(seq_offsets, block_offsets, place)

    my_rows = lambda inputs: lax.dynamic_slice_in_dim(inputs, c * half, half, 0)
    my_tokens, my_cotangent = my_rows(tokens), my_rows(cotangent)

    def rows_kernel(body, kinds, args, time, deps=(), extra=(), scratches=()):
        return pl.pallas_call(
            after(body, 1 + len(args), len(deps)),
            out_shape=tuple(jax.ShapeDtypeStruct((half, width), kind) for kind in kinds) + tuple(extra),
            in_specs=[SMEM] + [VMEM] * len(args) + [ANY] * len(deps),
            out_specs=(VMEM,) * (len(kinds) + len(extra)),
            scratch_shapes=list(scratches),
            compiler_params=pltpu.CompilerParams(vmem_limit_bytes=VMEM_LIMIT),
            cost_estimate=took_us(time),
        )(info, *args, *deps)

    parts_of = lambda state: (*state[:3], *state[5:])
    modulated, grad_mlp = rows_kernel(enter_kernel, (BF, BF), (tokens, cotangent, image_mod, text_mod), 4)

    slot = lambda n: jax.ShapeDtypeStruct((BLOCKS, half, n), BF)
    full = lambda n: jax.ShapeDtypeStruct((BLOCKS, rows_cap, n), BF)
    rows_of = lambda n, kind: jax.ShapeDtypeStruct((group_rows, n), kind)
    slot_block = block((half, width))
    scratch = lambda rows, n, kind=BF: pltpu.VMEM((rows, n), kind)
    weight_pair = lambda n: [scratch(width, n), scratch(width, n)]

    whole_qkv = lax.all_gather(plane_qkv, "g", axis=0, tiled=True)
    mod_begun = spread_begin(modulated)
    pack_rest = jnp.concatenate(
        [
            quarter_wide(image_fc1),
            quarter_wide(text_fc1),
            quarter_turned(image_fc2),
            quarter_turned(text_fc2),
            quarter_turned(image_out),
            quarter_turned(text_out),
        ],
        axis=2,
    )
    rest_picked = pick_pieces(pack_rest, place)
    rest_got = swap_pieces(rest_picked)
    mod_own, mod_oth = spread_end(spread_next(mod_begun, rest_picked[:1]), rest_got[1:])
    plane_fc1, plane_fc2, plane_out = arrange(rest_got, place, stack_rows, plane_of(2 * fc, 2 * fc, 2 * mine))
    whole_out = lax.all_gather(plane_out, "g", axis=0, tiled=True)
    whole_fc2 = lax.all_gather(plane_fc2, "g", axis=0, tiled=True)

    pair = lambda rows: jax.ShapeDtypeStruct((rows, 2 * mine), BF)
    queries, pairs, tail, edge, head, head_edge = stepped(
        project_kernel,
        BLOCKS,
        [SMEM, slot_block, slot_block, whole(whole_qkv.shape)],
        [kept(s) for s in ((group_rows, mine), (group_rows, 2 * mine), (TAIL, 2 * mine), (EDGE, 2 * mine), (TAIL, 2 * mine), (EDGE, 2 * mine))],
        (rows_of(mine, BF), pair(group_rows), pair(TAIL), pair(EDGE), pair(TAIL), pair(EDGE)),
        weight_pair(3 * mine) + [scratch(group_rows, 3 * mine), scratch(rows_cap, width), scratch(rows_cap, 3 * mine)],
        6,
    )(info, mod_own, mod_oth, whole_qkv)

    near_back, near_on = shift(tail, 1), shift(head, -1)
    gmlp_begun = spread_begin(copy_after(grad_mlp, (queries,)))
    fc1_piece = copy_after(plane_fc1, (near_back, near_on, *gmlp_begun[1:]))
    whole_fc1 = lax.all_gather(fc1_piece, "g", axis=0, tiled=True)
    gmlp_state = spread_next(gmlp_begun, (near_back, near_on, whole_out))
    gmlp_own, gmlp_oth = spread_end(gmlp_state)
    need_far = jnp.min(block_offsets[BLOCKS::BLOCKS] - block_offsets[:-1:BLOCKS]) < IMG + TXT
    far_back, far_on = if_needed(need_far, lambda a, b: (shift(a, 2), shift(b, -2)), edge, head_edge)
    sources = (far_back, near_back, pairs, near_on, far_on)
    source_specs = [whole(s.shape) for s in sources]

    tile_spec = pl.BlockSpec((CHUNK, mine), lambda t: (t, 0))
    log_spec = block((8, CHUNK))
    attended, attended_exact, logs, tops = stepped(
        attend_kernel,
        n_tiles,
        [SMEM, SMEM, tile_spec, *source_specs],
        (tile_spec, tile_spec, log_spec, kept((8, CHUNK))),
        (
            rows_of(mine, BF),
            rows_of(mine, F32),
            jax.ShapeDtypeStruct((n_tiles, 8, CHUNK), F32),
            jax.ShapeDtypeStruct((8, CHUNK), F32),
        ),
        [
            scratch(reach, mine),
            scratch(reach, mine),
            scratch(mine, reach),
            pltpu.VMEM((heads, mine, CHUNK), BF),
            pltpu.VMEM((heads, n_chunks, KEYS, CHUNK), F32),
            scratch(KEYS, heads * CHUNK),
            scratch(mine, CHUNK, F32),
            scratch(8 * heads, CHUNK, F32),
        ],
        1,
        (*gmlp_state[3:5], fc1_piece),
    )(chunks, seq_offsets, queries, *sources)

    def to_slots(n, first, rows, w, deps=(), time=10):
        return stepped(
            functools.partial(rows_to_slots_kernel, first),
            BLOCKS,
            [SMEM, whole(rows.shape), whole(w.shape)],
            (slot_block, slot_block),
            (slot(width), slot(width)),
            weight_pair(n) + [scratch(rows_cap, n), scratch(rows_cap, width)],
            time,
            deps,
        )(info, rows, w)

    branch_state = collect_next(collect_begin(core_sum(*to_slots(mine, 0, attended, whole_out, (), 1))), (whole_fc1,))
    branch, modulated_mlp = rows_kernel(
        middle_kernel, (F32, BF), (*parts_of(branch_state), my_tokens, image_mod, text_mod), 4, (gmlp_oth,)
    )
    mm_own, mm_oth = spread(modulated_mlp)
    fc_block = block((rows_cap, fc))
    hid, slope = stepped(
        mlp_up_kernel,
        BLOCKS,
        [SMEM, slot_block, slot_block, columns_from(width, fc, 0), columns_from(width, fc, 1)],
        (fc_block, fc_block),
        (full(fc), full(fc)),
        [scratch(rows_cap, width), scratch(rows_cap, fc, F32)],
        1,
    )(info, mm_own, mm_oth, whole_fc1, whole_fc1)

    def slot_sums(left, right, deps, time):
        return stepped(
            slot_sums_kernel,
            BLOCKS,
            [SMEM, slot_block, slot_block, fc_block],
            kept((width, 2 * fc)),
            jax.ShapeDtypeStruct((width, 2 * fc), BF),
            [scratch(width, fc, F32), scratch(width, fc, F32), scratch(rows_cap, width)],
            time,
            deps,
        )(info, *left, right)

    def row_sums(left, rows, deps=(), time=0.1):
        n = rows.shape[1]
        return stepped(
            row_sums_kernel,
            BLOCKS,
            [SMEM, slot_block, slot_block, whole(rows.shape)],
            kept((width, 2 * n)),
            jax.ShapeDtypeStruct((width, 2 * n), BF),
            [scratch(width, n, F32), scratch(width, n, F32), scratch(rows_cap, width), scratch(rows_cap, n)],
            time,
            deps,
        )(info, *left, rows)

    fc2_sums = slot_sums((gmlp_own, gmlp_oth), hid, (), 1)
    fc2_part = over_groups(fc2_sums)
    gm_own, gm_oth, gb = stepped(
        mlp_back_kernel,
        BLOCKS,
        [SMEM, slot_block, slot_block, fc_block] + [columns_from(width, fc, at) for at in (0, 1, 0, 1)],
        (slot_block, slot_block, fc_block),
        (slot(width), slot(width), full(fc)),
        [scratch(rows_cap, width), scratch(rows_cap, fc), scratch(rows_cap, width)],
        1,
        (fc2_sums,),
    )(info, gmlp_own, gmlp_oth, slope, whole_fc1, whole_fc1, whole_fc2, whole_fc2)

    gm_part = core_sum(gm_own, gm_oth)
    gm_state = collect_begin(gm_part)
    fc1_sums = slot_sums((mm_own, mm_oth), gb, gm_part, 12)
    fc1_part = over_groups(fc1_sums)
    gm_state = collect_next(gm_state, (fc1_sums,), 1)
    mlp_own, mlp_oth = stepped(
        slots_to_slots_kernel,
        BLOCKS,
        [SMEM, fc_block, columns_from(width, fc, 0), columns_from(width, fc, 1)],
        (slot_block, slot_block),
        (slot(width), slot(width)),
        [scratch(rows_cap, width)],
        25,
        gm_state[3:5],
    )(info, hid, whole_fc2, whole_fc2)
    grad_mod_mlp, grad_first, grad_branch = rows_kernel(
        turn_kernel,
        (F32, F32, BF),
        (*parts_of(gm_state), branch, my_tokens, my_cotangent, image_mod, text_mod),
        5,
        (mlp_own,),
    )
    gbr_begun = spread_begin(grad_branch)
    gbr_own, gbr_oth = spread_end(spread_next(gbr_begun, (fc2_part,)))
    grad_attended = stepped(
        functools.partial(back_project_kernel, 0),
        BLOCKS,
        [SMEM, slot_block, slot_block, whole(whole_out.shape)],
        kept((group_rows, mine)),
        rows_of(mine, BF),
        weight_pair(mine) + [scratch(rows_cap, width), scratch(rows_cap, mine)],
        1,
    )(info, gbr_own, gbr_oth, whole_out)

    mlp_part = core_sum(mlp_own, mlp_oth, (gbr_oth,), 3)
    mlp_state = collect_begin(mlp_part)
    dq, give_far_back, give_back, d_pairs, give_on, give_far_on = stepped(
        attend_back_kernel,
        n_tiles,
        [SMEM, SMEM, tile_spec, tile_spec, tile_spec, *source_specs, log_spec],
        (tile_spec, *(kept(s.shape) for s in sources)),
        (rows_of(mine, BF), pair(EDGE), pair(TAIL), rows_of(2 * mine, F32), pair(TAIL), pair(EDGE)),
        [
            scratch(reach, mine),
            scratch(reach, mine),
            scratch(mine, reach),
            scratch(heads * CHUNK, mine),
            scratch(heads * CHUNK, mine),
            pltpu.VMEM((heads, mine, CHUNK), BF),
            pltpu.VMEM((heads, mine, CHUNK), BF),
            pltpu.VMEM((heads, KEYS, CHUNK), F32),
            pltpu.VMEM((heads, KEYS, CHUNK), F32),
            scratch(KEYS, heads * CHUNK),
            scratch(KEYS, heads * CHUNK),
            scratch(mine, CHUNK, F32),
            scratch(reach, mine, F32),
            scratch(reach, mine, F32),
        ],
        1,
        (mlp_part[0],),
    )(chunks, seq_offsets, queries, grad_attended, attended_exact, *sources, logs)
    gave_back, gave_on = shift(give_back, -1), shift(give_on, 1)
    gave_far_back, gave_far_on = if_needed(
        need_far, lambda a, b: (shift(a, -2), shift(b, 2)), give_far_back, give_far_on
    )

    out_sums = row_sums((gbr_own, gbr_oth), attended, (dq,))
    out_part = over_groups(copy_after(out_sums, (gave_back, gave_on)))
    mlp_state = collect_next(mlp_state, (out_sums,), 1)
    pieces_of = lambda part, deps: pick_pieces(part.reshape(BLOCKS, share, -1), place, deps)
    grad_qkv = pl.pallas_call(
        after(gather_grads_kernel, 7, 2),
        out_shape=rows_of(3 * mine, BF),
        in_specs=[SMEM] + [VMEM] * 6 + [ANY] * 2,
        out_specs=VMEM,
        scratch_shapes=[scratch(group_rows, 2 * mine, F32)],
        compiler_params=pltpu.CompilerParams(vmem_limit_bytes=VMEM_LIMIT),
        cost_estimate=took_us(8),
    )(info, dq, d_pairs, gave_back, gave_on, gave_far_back, gave_far_on, out_sums, fc1_part)

    mod_sent = to_slots(3 * mine, 0, grad_qkv, whole_qkv, mlp_state[3:5], 0.1)
    qkv_sums = row_sums((mod_own, mod_oth), grad_qkv, (*mod_sent, *mlp_state[5:]), 14)
    qkv_part = over_groups(qkv_sums)
    mod_part = core_sum(*mod_sent, (qkv_sums,), 3)
    mod_state = collect_next(collect_begin(mod_part), mod_part[:1], 1)
    pair_f32 = lambda *shape: (jax.ShapeDtypeStruct(shape, F32),) * 2
    fc2_picked, fc1_picked = pieces_of(fc2_part, mod_state[3:5]), pieces_of(fc1_part, mod_state[3:5])
    out_picked = pieces_of(out_part, mod_state[3:5])
    fc2_got, fc1_got, out_got = swap_pieces(fc2_picked), swap_pieces(fc1_picked), swap_pieces(out_picked)
    tokens_grad_rows, mixed_rows, mod_sum = rows_kernel(
        leave_kernel,
        (F32, BF),
        (
            *parts_of(mod_state),
            *parts_of(mlp_state),
            grad_first,
            branch,
            grad_mod_mlp,
            my_tokens,
            my_cotangent,
            image_mod,
            text_mod,
        ),
        12,
        (fc2_picked[0], fc1_picked[0], out_picked[0]),
        (jax.ShapeDtypeStruct((2 * seq_count, 6, width), F32),),
        (scratch(half, width, F32), scratch(half, width, F32)),
    )
    mixed = both_halves(mixed_rows)
    qkv_got = swap_pieces(pieces_of(qkv_part, (mod_sum,)))
    fc2_outs = arrange(fc2_got, place, give_wide, pair_f32(share, BLOCKS * fc))
    fc1_outs = arrange(fc1_got, place, give_wide, pair_f32(share, BLOCKS * fc))
    out_outs = arrange(out_got, place, give_narrow, pair_f32(share, columns))
    qkv_outs = arrange(qkv_got, place, give_qkv, pair_f32(3, share, columns))
    mod_sum = mod_sum.reshape(2 * seq_count * 6, -1, share)
    mod_sum = jnp.swapaxes(mod_sum, 0, 1)
    mod_sum = mod_sum + over_core(mod_sum)
    head_top = jnp.max(tops[:heads], axis=1)
    spot = jnp.arange(BLOCKS)[:, None] == q
    head_top = jnp.where(spot, head_top[None, :], NEGATIVE).reshape(-1)
    n_heads = head_top.shape[0]
    head_top = jnp.pad(head_top, (0, -n_heads % share))[None, :]
    top_rows = -(-n_heads // share)
    head_top = jnp.broadcast_to(head_top.reshape(1, top_rows, share), (mod_sum.shape[0], top_rows, share))
    mod_sum = sums_of_shares(jnp.concatenate([mod_sum, head_top], axis=1), top_rows, g, q, qkv_got)
    head_max = mod_sum[-top_rows:].reshape(-1)[:n_heads]
    mod_sum = mod_sum[:-top_rows].reshape(2, seq_count, 6, share)
    root_factor = jnp.sqrt(clip_limits / jnp.maximum(head_max, clip_limits))
    column_scale = jnp.repeat(root_factor, HEAD)[None, None, :]
    clipped = tuple((w[:, :2, :].astype(F32) * column_scale).astype(BF) for w in (image_qkv, text_qkv))

    return (
        mixed,
        both_halves(tokens_grad_rows),
        mod_sum[0],
        mod_sum[1],
        *(jnp.swapaxes(part, 0, 1) for part in qkv_outs),
        *(part.T for part in out_outs),
        *fc1_outs,
        *(part.T for part in fc2_outs),
        head_max,
        *clipped,
    )


def solution(mesh):
    devices = mesh.devices
    split = Mesh(devices.reshape(devices.shape[0] // BLOCKS, 2, 2, devices.shape[1]), ("g", "y", "x", "c"))
    dp = ("g", "y", "x")
    placed = (
        P(dp, None),
        P(dp, None),
        P(),
        P(),
        P(),
        P(),
        P(dp, None, "c"),
        P(dp, None, "c"),
        P("c", dp),
        P("c", dp),
        P(dp, "c"),
        P(dp, "c"),
        P("c", dp),
        P("c", dp),
        P("c"),
    )
    return jax.shard_map(
        local,
        mesh=split,
        in_specs=placed,
        out_specs=(
            P(dp, None),
            P(dp, None),
            P(None, None, dp),
            P(None, None, dp),
            P(dp, None, "c"),
            P(dp, None, "c"),
            P("c", dp),
            P("c", dp),
            P(dp, "c"),
            P(dp, "c"),
            P("c", dp),
            P("c", dp),
            P("c"),
            P(dp, None, "c"),
            P(dp, None, "c"),
        ),
        check_vma=False,
    )
```

```python
import functools

import jax
import jax.numpy as jnp
from jax import lax
from jax.experimental import pallas as pl
from jax.experimental.pallas import tpu as pltpu
from jax.sharding import Mesh, PartitionSpec as P

HEAD = 64
IMG = 1024
TXT = 154
EPSILON = 1e-06
NEGATIVE = -1e30
BLOCKS = 4
SUB = 128
TAIL = 1184
TAIL_PAD = 1536
EDGE = 160
CHUNK = 256
KEYS = 512
SLAB = 64
ALIGN = 16
TEXT_ROWS = 176
BF = jnp.bfloat16
F32 = jnp.float32
SWAP = [(0, 1), (1, 0)]
VMEM_LIMIT = 60 * 1024 * 1024

VMEM = pl.BlockSpec(memory_space=pltpu.VMEM)
SMEM = pl.BlockSpec(memory_space=pltpu.SMEM)
ANY = pl.BlockSpec(memory_space=pl.ANY)

COUNT, OFFSET, TEXT_FROM, TEXT_TO = 0, 4, 8, 12
CORE, TAIL_FROM, EDGE_FROM, OWN_FROM, OWN_SEQ, NEXT_FROM, HALF, INFO = 16, 17, 18, 19, 20, 21, 22, 23


def dot(a, b):
    return jnp.dot(a, b, preferred_element_type=F32)


def dot_back(a, b):
    return lax.dot_general(a, b, (((1,), (1,)), ((), ())), preferred_element_type=F32)


def dot_rows(a, b):
    return lax.dot_general(a, b, (((0,), (0,)), ((), ())), preferred_element_type=F32)


def took_us(time):
    return pl.CostEstimate(flops=int(time * 1.15e9), bytes_accessed=int(time * 1e6), transcendentals=0)


def after(body, n_in, n_deps):
    return lambda *refs: body(*refs[:n_in], *refs[n_in + n_deps :])


def whole(shape):
    return pl.BlockSpec(shape, lambda j: (0,) * len(shape), pipeline_mode=pl.Buffered(1))


def kept(shape):
    return pl.BlockSpec(shape, lambda j: (0,) * len(shape))


def block(shape):
    return pl.BlockSpec((1,) + shape, lambda j: (j,) + (0,) * len(shape))


def columns_from(rows, n, at):
    return pl.BlockSpec((rows, n), lambda j: (0, at), pipeline_mode=pl.Buffered(1))


def stepped(body, steps, in_specs, out_specs, out_shape, scratch, time, deps=()):
    run = pl.pallas_call(
        after(body, len(in_specs), len(deps)),
        grid=(steps,),
        out_shape=out_shape,
        in_specs=list(in_specs) + [ANY] * len(deps),
        out_specs=out_specs,
        scratch_shapes=list(scratch),
        compiler_params=pltpu.CompilerParams(vmem_limit_bytes=VMEM_LIMIT),
        cost_estimate=took_us(time),
    )
    return lambda *args: run(*args, *deps)


def sum_after(parts, kind, deps, time=1):
    n = len(parts)

    def body(*refs):
        total = refs[0][...].astype(F32)
        for part in refs[1:n]:
            total = total + part[...].astype(F32)
        refs[n][...] = total.astype(kind)

    return pl.pallas_call(
        after(body, n, len(deps)),
        out_shape=jax.ShapeDtypeStruct(parts[0].shape, kind),
        in_specs=[VMEM] * n + [ANY] * len(deps),
        out_specs=VMEM,
        compiler_params=pltpu.CompilerParams(vmem_limit_bytes=VMEM_LIMIT),
        cost_estimate=took_us(time),
    )(*parts, *deps)


def window(start, rows, total):
    base = jnp.minimum(lax.shift_right_logical(start, 4) * ALIGN, total - rows - ALIGN)
    return pl.ds(pl.multiple_of(base, ALIGN), rows + ALIGN), start - base


def moved(part, skip):
    rows = part.shape[0]
    shape = (rows + ALIGN, rows)
    there = lax.broadcasted_iota(jnp.int32, shape, 0) - skip
    return dot((there == lax.broadcasted_iota(jnp.int32, shape, 1)).astype(F32).astype(BF), part)


def read_rows(ref, start, rows):
    place, skip = window(start, rows, ref.shape[0])
    shape = (rows, rows + ALIGN)
    here = lax.broadcasted_iota(jnp.int32, shape, 1) - skip
    pick = (here == lax.broadcasted_iota(jnp.int32, shape, 0)).astype(F32).astype(BF)
    return dot(pick, ref[place, :]).astype(BF)


def layout_kernel(group_rows, seq, blocks, place, info, chunks):
    g, q = place[0], place[1]
    n_groups, n_seq = (blocks.shape[0] - 1) // BLOCKS, seq.shape[0] - 1
    start, stop = blocks[g * BLOCKS], blocks[g * BLOCKS + BLOCKS]

    def seq_of(position, shift):
        found = jnp.int32(0)
        for s in range(n_seq):
            found = jnp.where(position >= seq[s], s + shift, found)
        return found

    for j in range(BLOCKS):
        b = g * BLOCKS + (q ^ j)
        low, high = blocks[b], blocks[b + 1]
        text_from, text_to = jnp.int32(0), jnp.int32(0)
        for s in range(n_seq):
            first, last = jnp.maximum(seq[s] + IMG, low), jnp.minimum(seq[s + 1], high)
            text_from = jnp.where(first < last, first - low, text_from)
            text_to = jnp.where(first < last, last - low, text_to)
        info[COUNT + j] = high - low
        info[OFFSET + j] = low - start
        info[TEXT_FROM + j] = text_from
        info[TEXT_TO + j] = text_to
    own = blocks[g * BLOCKS + q]
    info[CORE] = place[2]
    info[TAIL_FROM] = jnp.maximum(stop - start - TAIL, 0)
    info[EDGE_FROM] = jnp.maximum(stop - start - EDGE, 0)
    info[OWN_FROM] = own
    info[HALF] = group_rows // (2 * BLOCKS)
    info[OWN_SEQ] = seq_of(own, 0)
    info[NEXT_FROM] = seq[seq_of(own, 0) + 1]

    def span(steps):
        there = (g + steps >= 0) & (g + steps < n_groups)
        at = jnp.clip(g + steps, 0, n_groups - 1) * BLOCKS
        return jnp.where(there, blocks[at], 0), jnp.where(there, blocks[at + BLOCKS], 0)

    before, behind, ahead, beyond = span(-2), span(-1), span(1), span(2)
    n_chunks = (2 * KEYS + 2 * TAIL_PAD + group_rows) // KEYS
    i = 0
    for base, low, high, rows in (
        (jnp.maximum(before[1] - EDGE, before[0]) - (KEYS - EDGE), jnp.maximum(before[1] - EDGE, before[0]), before[1], KEYS),
        (
            jnp.maximum(behind[1] - TAIL, behind[0]) - (TAIL_PAD - TAIL),
            jnp.maximum(behind[1] - TAIL, behind[0]),
            behind[1],
            TAIL_PAD,
        ),
        (start, start, stop, group_rows),
        (ahead[0], ahead[0], jnp.minimum(ahead[1], ahead[0] + TAIL), TAIL_PAD),
        (beyond[0], beyond[0], jnp.minimum(beyond[1], beyond[0] + EDGE), KEYS),
    ):
        for step in range(rows // KEYS):
            chunks[i] = base + step * KEYS
            chunks[n_chunks + i] = low
            chunks[2 * n_chunks + i] = high
            i += 1
    n_tiles = group_rows // CHUNK
    for t in range(n_tiles):
        first = start + t * CHUNK
        last = jnp.minimum(first + CHUNK, stop) - 1
        chunks[3 * n_chunks + 2 * t] = jnp.where(first < stop, seq[seq_of(first, 0)], 0)
        chunks[3 * n_chunks + 2 * t + 1] = jnp.where(first < stop, seq[seq_of(last, 1)], 0)
        one = (first + CHUNK <= stop) & (seq_of(first, 0) == seq_of(last, 0))
        chunks[3 * n_chunks + 2 * n_tiles + 2 + t] = jnp.where(one, 1, 0)
    chunks[3 * n_chunks + 3 * n_tiles + 2] = seq[seq_of(start, 0)]
    chunks[3 * n_chunks + 3 * n_tiles + 3] = seq[seq_of(stop - 1, 1)]
    chunks[3 * n_chunks + 2 * n_tiles] = start
    chunks[3 * n_chunks + 2 * n_tiles + 1] = stop


def lane_spans(chunks, seq, n_chunks, n_tiles, t):
    start, stop = chunks[3 * n_chunks + 2 * n_tiles], chunks[3 * n_chunks + 2 * n_tiles + 1]
    position = start + t * CHUNK + lax.broadcasted_iota(jnp.int32, (1, CHUNK), 1)
    low, high = jnp.zeros_like(position), jnp.zeros_like(position)
    for s in range(seq.shape[0] - 1):
        hit = (position >= seq[s]) & (position < seq[s + 1]) & (position < stop)
        low, high = jnp.where(hit, seq[s], low), jnp.where(hit, seq[s + 1], high)
    return low, high


def own_kinds(info, first, rows):
    ids = row_ids(info[CORE] * info[HALF] + first, rows)
    live = ids < info[COUNT]
    is_text = live & (ids >= info[TEXT_FROM]) & (ids < info[TEXT_TO])
    is_next = live & (info[OWN_FROM] + ids >= info[NEXT_FROM])
    return live, live & jnp.logical_not(is_text | is_next), is_next, is_text


def vector_of(info, image_mod, text_mod, is_next, is_text):
    s = info[OWN_SEQ]
    after_s = jnp.minimum(s + 1, image_mod.shape[0] - 1)

    def pick(i):
        own, text, following = image_mod[s][i : i + 1], text_mod[s][i : i + 1], image_mod[after_s][i : i + 1]
        return jnp.where(is_text, text, jnp.where(is_next, following, own))

    return pick


def normal(rows):
    centered = rows - jnp.mean(rows, axis=1, keepdims=True)
    inverse = lax.rsqrt(jnp.mean(centered * centered, axis=1, keepdims=True) + EPSILON)
    return centered * inverse, inverse


def normal_back(grad, normed, inverse):
    return inverse * (
        grad - jnp.mean(grad, axis=1, keepdims=True) - normed * jnp.mean(grad * normed, axis=1, keepdims=True)
    )


def enter_kernel(info, tokens, cotangent, image_mod, text_mod, modulated, grad_mlp):
    half = modulated.shape[0]
    place = pl.ds(pl.multiple_of(info[CORE] * half, half), half)
    live, _, is_next, is_text = own_kinds(info, 0, half)
    pick = vector_of(info, image_mod, text_mod, is_next, is_text)
    normed, _ = normal(tokens[place, :].astype(F32))
    modulated[...] = (normed * (1.0 + pick(1)) + pick(0)).astype(BF)
    grad_mlp[...] = (pick(5) * jnp.where(live, cotangent[place, :].astype(F32), 0.0)).astype(BF)


def collected(mine, first_x, first_y, last_x, last_y, out):
    cut = out.shape[0] // 2
    out[:cut, :] = mine[:cut, :].astype(F32) + first_x[...].astype(F32) + last_y[...].astype(F32)
    out[cut:, :] = mine[cut:, :].astype(F32) + last_x[...].astype(F32) + first_y[...].astype(F32)


def middle_kernel(
    info, mine, first_x, first_y, last_x, last_y, tokens, image_mod, text_mod, branch, modulated_mlp
):
    collected(mine, first_x, first_y, last_x, last_y, branch)
    _, _, is_next, is_text = own_kinds(info, 0, branch.shape[0])
    pick = vector_of(info, image_mod, text_mod, is_next, is_text)
    normed, _ = normal(tokens[...].astype(F32) + pick(2) * branch[...])
    modulated_mlp[...] = (normed * (1.0 + pick(4)) + pick(3)).astype(BF)


def turn_kernel(
    info, mine, first_x, first_y, last_x, last_y, branch, tokens, cotangent, image_mod, text_mod,
    grad_mod_mlp, grad_first, grad_branch,
):
    collected(mine, first_x, first_y, last_x, last_y, grad_mod_mlp)
    live, _, is_next, is_text = own_kinds(info, 0, branch.shape[0])
    pick = vector_of(info, image_mod, text_mod, is_next, is_text)
    normed, inverse = normal(tokens[...].astype(F32) + pick(2) * branch[...])
    back = normal_back(grad_mod_mlp[...] * (1.0 + pick(4)), normed, inverse)
    result = jnp.where(live, cotangent[...].astype(F32) + back, 0.0)
    grad_first[...] = result
    grad_branch[...] = (pick(2) * result).astype(BF)


def leave_kernel(
    info, mine, first_x, first_y, last_x, last_y,
    mlp_mine, mlp_first_x, mlp_first_y, mlp_last_x, mlp_last_y,
    grad_first, branch, grad_mod_mlp, tokens, cotangent, image_mod, text_mod,
    tokens_grad, mixed, sums, grad_modulated, mlp_branch,
):
    collected(mine, first_x, first_y, last_x, last_y, grad_modulated)
    collected(mlp_mine, mlp_first_x, mlp_first_y, mlp_last_x, mlp_last_y, mlp_branch)
    sums[...] = jnp.zeros_like(sums)
    n_seq = image_mod.shape[0]
    s = info[OWN_SEQ]
    after_s = jnp.minimum(s + 1, n_seq - 1)
    step = 64
    for low in range(0, tokens_grad.shape[0], step):
        part = slice(low, low + step)
        live, is_own, is_next, is_text = own_kinds(info, low, step)
        pick = vector_of(info, image_mod, text_mod, is_next, is_text)
        rows = tokens[part, :].astype(F32)
        normed, inverse = normal(rows)
        first = rows + pick(2) * branch[part, :]
        normed_mlp, _ = normal(first)

        def add(i, term):
            for kept_rows, at in ((is_own, s), (is_next, after_s), (is_text, n_seq + s)):
                row = jnp.sum(jnp.where(kept_rows, term, 0.0), axis=0, keepdims=True)
                sums[at, i : i + 1, :] += row

        grads = grad_modulated[part, :]
        add(0, grads)
        add(1, grads * normed)
        add(2, grad_first[part, :] * branch[part, :])
        add(3, grad_mod_mlp[part, :])
        add(4, grad_mod_mlp[part, :] * normed_mlp)
        add(5, cotangent[part, :].astype(F32) * mlp_branch[part, :])
        back = normal_back(grads * (1.0 + pick(1)), normed, inverse)
        tokens_grad[part, :] = jnp.where(live, grad_first[part, :] + back, 0.0)
        mixed[part, :] = jnp.where(live, first + pick(5) * mlp_branch[part, :], 0.0).astype(BF)


def row_ids(base, rows):
    return base + lax.broadcasted_iota(jnp.int32, (rows, 1), 0)


def for_rows(info, cap, body):
    count = info[COUNT + pl.program_id(0)]
    low = 0
    for rows in range(cap // 2, cap + 1, SUB):

        @pl.when((count > low) & (count <= rows))
        def _():
            body(rows)

        low = rows


def for_text(info, cap, body):
    j = pl.program_id(0)
    low, high = info[TEXT_FROM + j], info[TEXT_TO + j]

    @pl.when(high > low)
    def _():
        base = jnp.minimum(lax.shift_right_logical(low, 4) * ALIGN, cap - TEXT_ROWS)
        base = pl.multiple_of(base, ALIGN)
        ids = row_ids(base, TEXT_ROWS)
        body(pl.ds(base, TEXT_ROWS), (ids >= low) & (ids < high))


def half_places(info, half):
    mine = pl.multiple_of(info[CORE] * half, half)
    return pl.ds(mine, half), pl.ds(pl.multiple_of(half - mine, half), half)


def join(info, own, oth, out):
    half = own.shape[1]
    at_own, at_oth = half_places(info, half)
    out[at_own, :] = own[0]
    out[at_oth, :] = oth[0]


def part_ways(info, rows_ref, own, oth):
    half = own.shape[1]
    at_own, at_oth = half_places(info, half)
    own[0] = rows_ref[at_own, :]
    oth[0] = rows_ref[at_oth, :]


def split_columns(w, first, image, text):
    n = image.shape[1]
    image[...] = w[:, first : first + n]
    text[...] = w[:, first + n : first + 2 * n]


def to_group_rows(info, own, oth, w_image, w_text, out, joined, tile):
    cap = joined.shape[0]
    join(info, own, oth, joined)

    @pl.when(pl.program_id(0) == 0)
    def _():
        out[...] = jnp.zeros_like(out)

    def body(rows):
        tile[:rows, :] = dot(joined[:rows, :], w_image[...]).astype(BF)

        def text(place, is_text):
            tile[place, :] = jnp.where(is_text, dot(joined[place, :], w_text[...]).astype(BF), tile[place, :])

        for_text(info, cap, text)
        j = pl.program_id(0)
        place, skip = window(info[OFFSET + j], rows, out.shape[0])
        part = moved(tile[:rows, :], skip).astype(BF)
        ids = row_ids(-skip, rows + ALIGN)
        out[place, :] = jnp.where((ids >= 0) & (ids < info[COUNT + j]), part, out[place, :])

    for_rows(info, cap, body)


def project_kernel(info, own, oth, w, q, kv, tail, edge, head, head_edge, w_image, w_text, out, joined, tile):
    @pl.when(pl.program_id(0) == 0)
    def _():
        split_columns(w, 0, w_image, w_text)

    to_group_rows(info, own, oth, w_image, w_text, out, joined, tile)

    @pl.when(pl.program_id(0) == BLOCKS - 1)
    def _():
        n = q.shape[1]
        q[...] = out[:, :n]
        kv[...] = out[:, n:]
        tail[...] = read_rows(kv, info[TAIL_FROM], TAIL)
        edge[...] = read_rows(kv, info[EDGE_FROM], EDGE)
        head[...] = kv[:TAIL, :]
        head_edge[...] = kv[:EDGE, :]


def back_project_kernel(first, info, own, oth, w, out, w_image, w_text, joined, tile):
    @pl.when(pl.program_id(0) == 0)
    def _():
        split_columns(w, first, w_image, w_text)

    to_group_rows(info, own, oth, w_image, w_text, out, joined, tile)


def times_turned(info, x, w_image, w_text, result):
    cap = result.shape[0]

    def body(rows):
        result[:rows, :] = dot_back(x[:rows, :], w_image[...]).astype(BF)
        if rows < cap:
            result[rows:, :] = jnp.zeros((cap - rows, result.shape[1]), BF)

        def text(place, is_text):
            part = dot_back(x[place, :], w_text[...]).astype(BF)
            result[place, :] = jnp.where(is_text, part, result[place, :])

        for_text(info, cap, text)

    for_rows(info, cap, body)


def rows_to_slots_kernel(first, info, rows_ref, w, own, oth, w_image, w_text, x, result):
    j = pl.program_id(0)

    @pl.when(j == 0)
    def _():
        split_columns(w, first, w_image, w_text)

    def take(rows):
        x[:rows, :] = read_rows(rows_ref, info[OFFSET + j], rows)

    for_rows(info, x.shape[0], take)
    times_turned(info, x, w_image, w_text, result)
    part_ways(info, result, own, oth)


def slots_to_slots_kernel(info, x, w_image, w_text, own, oth, result):
    times_turned(info, x.at[0], w_image, w_text, result)
    part_ways(info, result, own, oth)


def gelu_parts(v):
    k = 0.7978845608028654
    square = v * v
    t = jnp.tanh(k * v * (1.0 + 0.044715 * square))
    half = 0.5 * (1.0 + t)
    return v * half, half + 0.5 * v * (1.0 - t * t) * (k + 3 * 0.044715 * k * square)


def mlp_up_kernel(info, x_own, x_oth, w_image, w_text, hid, slope, x, before):
    cap = x.shape[0]
    join(info, x_own, x_oth, x)

    def body(rows):
        before[:rows, :] = dot(x[:rows, :], w_image[...])

        def text(place, is_text):
            before[place, :] = jnp.where(is_text, dot(x[place, :], w_text[...]), before[place, :])

        for_text(info, cap, text)
        value, steep = gelu_parts(before[:rows, :])
        hid[0, :rows, :] = value.astype(BF)
        slope[0, :rows, :] = steep.astype(BF)
        if rows < cap:
            for ref in (hid, slope):
                ref[0, rows:, :] = jnp.zeros((cap - rows, ref.shape[2]), BF)

    for_rows(info, cap, body)


def mlp_back_kernel(
    info, g_own, g_oth, slope, upper_image, upper_text, lower_image, lower_text, gm_own, gm_oth, gb, g, back, result
):
    cap = g.shape[0]
    join(info, g_own, g_oth, g)

    def body(rows):
        back[:rows, :] = dot(g[:rows, :], lower_image[...]).astype(BF)

        def text(place, is_text):
            back[place, :] = jnp.where(is_text, dot(g[place, :], lower_text[...]).astype(BF), back[place, :])

        for_text(info, cap, text)
        gb[0, :rows, :] = (back[:rows, :].astype(F32) * slope[0, :rows, :].astype(F32)).astype(BF)
        if rows < cap:
            gb[0, rows:, :] = jnp.zeros((cap - rows, gb.shape[2]), BF)

    for_rows(info, cap, body)
    times_turned(info, gb.at[0], upper_image, upper_text, result)
    part_ways(info, result, gm_own, gm_oth)


def add_sums(info, left, right, acc_image, acc_text):
    cap = left.shape[0]
    j = pl.program_id(0)

    @pl.when(j == 0)
    def _():
        acc_image[...] = jnp.zeros_like(acc_image)
        acc_text[...] = jnp.zeros_like(acc_text)

    def body(rows):
        ids = row_ids(0, rows)
        is_text = (ids >= info[TEXT_FROM + j]) & (ids < info[TEXT_TO + j])
        is_image = (ids < info[COUNT + j]) & jnp.logical_not(is_text)
        acc_image[...] += dot_rows(left[:rows, :], jnp.where(is_image, right[:rows, :], jnp.zeros((), BF)))

    for_rows(info, cap, body)

    def text(place, is_text):
        acc_text[...] += dot_rows(left[place, :], jnp.where(is_text, right[place, :], jnp.zeros((), BF)))

    for_text(info, cap, text)


def give_sums(out, acc_image, acc_text):
    cut = acc_image.shape[1]

    @pl.when(pl.program_id(0) == BLOCKS - 1)
    def _():
        out[:, :cut] = acc_image[...].astype(BF)
        out[:, cut:] = acc_text[...].astype(BF)


def slot_sums_kernel(info, l_own, l_oth, right, out, acc_image, acc_text, left):
    join(info, l_own, l_oth, left)
    add_sums(info, left, right.at[0], acc_image, acc_text)
    give_sums(out, acc_image, acc_text)


def row_sums_kernel(info, l_own, l_oth, rows_ref, out, acc_image, acc_text, left, right):
    join(info, l_own, l_oth, left)

    def take(rows):
        right[:rows, :] = read_rows(rows_ref, info[OFFSET + pl.program_id(0)], rows)

    for_rows(info, left.shape[0], take)
    add_sums(info, left, right, acc_image, acc_text)
    give_sums(out, acc_image, acc_text)


def head_rows(turned, h):
    ids = lax.broadcasted_iota(jnp.int32, turned.shape, 0)
    return jnp.where((ids >= h * HEAD) & (ids < (h + 1) * HEAD), turned, 0)


def head_columns(plain, h):
    ids = lax.broadcasted_iota(jnp.int32, plain.shape, 1)
    return jnp.where((ids >= h * HEAD) & (ids < (h + 1) * HEAD), plain, 0)


def fold(combine, rows):
    parts = [rows[at : at + 8, :] for at in range(0, rows.shape[0], 8)]
    while len(parts) > 1:
        parts = [combine(a, b) for a, b in zip(parts[::2], parts[1::2])]
    return parts[0]


def slab_mask(chunks, i, n_chunks, low, q_from, q_to):
    position = chunks[i] + low + lax.broadcasted_iota(jnp.int32, (SLAB, 1), 0)
    valid = (position >= chunks[n_chunks + i]) & (position < chunks[2 * n_chunks + i])
    position = jnp.where(valid, position, -1)
    return (position >= q_from) & (position < q_to)


def for_chunks(chunks, n_chunks, t, body):
    low, high = chunks[3 * n_chunks + 2 * t], chunks[3 * n_chunks + 2 * t + 1]
    one = chunks[3 * n_chunks + 2 * pl.num_programs(0) + 2 + t] > 0

    def step(i, carry):
        base = chunks[i]
        start = jnp.maximum(base, chunks[n_chunks + i])
        stop = jnp.minimum(base + KEYS, chunks[2 * n_chunks + i])
        reached = (start < high) & (stop > low) & (start < stop)
        inside = one & (start == base) & (stop == base + KEYS) & (base >= low) & (stop <= high)

        @pl.when(reached & inside)
        def _():
            body(i, True)

        @pl.when(reached & jnp.logical_not(inside))
        def _():
            body(i, False)

        return carry

    lax.fori_loop(0, n_chunks, step, 0)


def sources_at(far_back, near_back, kv, near_on, far_on):
    chunk = 0
    for source, size, last in (
        (far_back, KEYS, True),
        (near_back, TAIL_PAD, True),
        (kv, kv.shape[0], False),
        (near_on, TAIL_PAD, False),
        (far_on, KEYS, False),
    ):
        rows = source.shape[0]
        skip = size - rows if last else 0
        for low in range(0, size, KEYS):
            first, stop = max(low, skip), min(low + KEYS, skip + rows)
            yield chunk, source, slice(first - skip, stop - skip), first - low, stop - low
            chunk += 1


def if_reached(chunks, n_chunks, i, body, otherwise=None):
    last = 3 * n_chunks + 3 * pl.num_programs(0) + 2
    start = jnp.maximum(chunks[i], chunks[n_chunks + i])
    stop = jnp.minimum(chunks[i] + KEYS, chunks[2 * n_chunks + i])
    reached = (start < chunks[last + 1]) & (stop > chunks[last]) & (start < stop)
    pl.when(reached)(body)
    if otherwise:
        pl.when(jnp.logical_not(reached))(otherwise)


def gather_keys(chunks, sources, k, v, plain, turned):
    n = k.shape[1]
    n_chunks = k.shape[0] // KEYS
    for i, source, rows, first, stop in sources_at(*sources):

        def take():
            at = i * KEYS
            for ref, columns in ((k, slice(0, n)), (v, slice(n, 2 * n))):
                ref[at + first : at + stop, :] = source[rows, columns]
                for low, high in ((0, first), (stop, KEYS)):
                    if low < high:
                        ref[at + low : at + high, :] = jnp.zeros((high - low, n), BF)
            part = slice(at, at + KEYS)
            turned[:, part] = plain[part, :].T

        if_reached(chunks, n_chunks, i, take)


def attend_kernel(
    chunks, seq, q, far_back, near_back, kv, near_on, far_on,
    out, exact, lse, top,
    k, v, v_turned, q_turn, logits, probs, total, high,
):
    t = pl.program_id(0)
    n_chunks = k.shape[0] // KEYS
    heads = q.shape[1] // HEAD
    wide = q.shape[0]

    @pl.when(t == 0)
    def _():
        gather_keys(chunks, (far_back, near_back, kv, near_on, far_on), k, v, v, v_turned)
        top[...] = jnp.full_like(top, NEGATIVE)

    live = chunks[3 * n_chunks + 2 * t + 1] > 0

    @pl.when(live)
    def _():
        turned = (q[...].astype(F32) * HEAD**-0.5).T
        for h in range(heads):
            q_turn[h] = head_rows(turned, h).astype(BF)
        lanes_from, lanes_to = lane_spans(chunks, seq, n_chunks, pl.num_programs(0), t)
        total[...] = jnp.zeros_like(total)
        high[...] = jnp.full_like(high, NEGATIVE)

        def first(i, whole_chunk):
            place = pl.ds(pl.multiple_of(i * KEYS, KEYS), KEYS)
            for h in range(heads):
                logits[h, i] = dot(k[place, :], q_turn[h])
            for low in range(0, KEYS, SLAB):
                part = slice(low, low + SLAB)
                if not whole_chunk:
                    mask = slab_mask(chunks, i, n_chunks, low, lanes_from, lanes_to)
                for h in range(heads):
                    values = logits[h, i, part, :]
                    if not whole_chunk:
                        values = jnp.where(mask, values, NEGATIVE)
                        logits[h, i, part, :] = values
                    rows = slice(8 * h, 8 * h + 8)
                    high[rows, :] = jnp.maximum(high[rows, :], fold(jnp.maximum, values))

        for_chunks(chunks, n_chunks, t, first)
        tops = [jnp.max(high[8 * h : 8 * h + 8, :], axis=0, keepdims=True) for h in range(heads)]
        high[...] = jnp.zeros_like(high)

        def second(i, whole_chunk):
            place = pl.ds(pl.multiple_of(i * KEYS, KEYS), KEYS)
            for low in range(0, KEYS, SLAB):
                part = slice(low, low + SLAB)
                for h in range(heads):
                    p = jnp.exp(logits[h, i, part, :] - tops[h])
                    rows = slice(8 * h, 8 * h + 8)
                    high[rows, :] += fold(jnp.add, p)
                    probs[part, h * wide : (h + 1) * wide] = p.astype(BF)
            for h in range(heads):
                rows = slice(h * HEAD, (h + 1) * HEAD)
                total[rows, :] += dot(v_turned[rows, place], probs[:, h * wide : (h + 1) * wide])

        for_chunks(chunks, n_chunks, t, second)
        for h in range(heads):
            rows = slice(h * HEAD, (h + 1) * HEAD)
            sums = jnp.sum(high[8 * h : 8 * h + 8, :], axis=0, keepdims=True)
            total[rows, :] = total[rows, :] / sums
            lse[0, h : h + 1, :] = tops[h] + jnp.log(sums)
            seen = jnp.where(lanes_to > lanes_from, tops[h], NEGATIVE)
            top[h : h + 1, :] = jnp.maximum(top[h : h + 1, :], seen)
        result = total[...].T
        exact[...] = result
        out[...] = result.astype(BF)

    @pl.when(jnp.logical_not(live))
    def _():
        exact[...] = jnp.zeros_like(exact)
        out[...] = jnp.zeros_like(out)
        lse[...] = jnp.zeros_like(lse)


def attend_back_kernel(
    chunks, seq, q, g, attended, far_back, near_back, kv, near_on, far_on, lse,
    dq, d_far_back, d_near_back, d_kv, d_near_on, d_far_on,
    k, v, k_turned, q_stack, g_stack, q_turn, g_turn, logits, grads_of, probs, grad_logits, total, dk, dv,
):
    t = pl.program_id(0)
    n_chunks = k.shape[0] // KEYS
    heads = q.shape[1] // HEAD
    wide = q.shape[0]

    @pl.when(t == 0)
    def _():
        gather_keys(chunks, (far_back, near_back, kv, near_on, far_on), k, v, k, k_turned)
        for i in range(n_chunks):

            def clear():
                dk[i * KEYS : (i + 1) * KEYS, :] = jnp.zeros((KEYS, dk.shape[1]), F32)
                dv[i * KEYS : (i + 1) * KEYS, :] = jnp.zeros((KEYS, dk.shape[1]), F32)

            if_reached(chunks, n_chunks, i, clear)

    live = chunks[3 * n_chunks + 2 * t + 1] > 0

    @pl.when(live)
    def _():
        scaled = q[...].astype(F32) * HEAD**-0.5
        grads = g[...].astype(F32)
        q_turned, g_turned = scaled.T, grads.T
        product = g_turned * attended[...].T
        delta, logs = [], []
        for h in range(heads):
            rows = slice(h * wide, (h + 1) * wide)
            q_stack[rows, :] = head_columns(scaled, h).astype(BF)
            g_stack[rows, :] = head_columns(grads, h).astype(BF)
            q_turn[h] = head_rows(q_turned, h).astype(BF)
            g_turn[h] = head_rows(g_turned, h).astype(BF)
            delta.append(jnp.sum(product[h * HEAD : (h + 1) * HEAD, :], axis=0, keepdims=True))
            logs.append(lse[0, h : h + 1, :])
        lanes_from, lanes_to = lane_spans(chunks, seq, n_chunks, pl.num_programs(0), t)
        total[...] = jnp.zeros_like(total)

        def body(i, whole_chunk):
            place = pl.ds(pl.multiple_of(i * KEYS, KEYS), KEYS)
            for h in range(heads):
                logits[h] = dot(k[place, :], q_turn[h])
                grads_of[h] = dot(v[place, :], g_turn[h])
            for low in range(0, KEYS, SLAB):
                part = slice(low, low + SLAB)
                if not whole_chunk:
                    mask = slab_mask(chunks, i, n_chunks, low, lanes_from, lanes_to)
                for h in range(heads):
                    lanes = slice(h * wide, (h + 1) * wide)
                    p = jnp.exp(logits[h, part, :] - logs[h])
                    if not whole_chunk:
                        p = jnp.where(mask, p, 0.0)
                    probs[part, lanes] = p.astype(BF)
                    grad_logits[part, lanes] = (p * (grads_of[h, part, :] - delta[h])).astype(BF)
            for h in range(heads):
                rows = slice(h * HEAD, (h + 1) * HEAD)
                total[rows, :] += dot(k_turned[rows, place], grad_logits[:, h * wide : (h + 1) * wide])
            dv[place, :] += dot(probs[...], g_stack[...])
            dk[place, :] += dot(grad_logits[...], q_stack[...])

        for_chunks(chunks, n_chunks, t, body)
        dq[...] = (total[...].T * HEAD**-0.5).astype(BF)

    @pl.when(jnp.logical_not(live))
    def _():
        dq[...] = jnp.zeros_like(dq)

    @pl.when(t == pl.num_programs(0) - 1)
    def _():
        n = dk.shape[1]
        for i, out, rows, first, stop in sources_at(d_far_back, d_near_back, d_kv, d_near_on, d_far_on):

            def give():
                place = slice(i * KEYS + first, i * KEYS + stop)
                out[rows, :n] = dk[place, :].astype(out.dtype)
                out[rows, n:] = dv[place, :].astype(out.dtype)

            def blank():
                out[rows, :] = jnp.zeros((stop - first, 2 * n), out.dtype)

            if_reached(chunks, n_chunks, i, give, blank)


def gather_grads_kernel(info, dq, d_kv, near_back, near_on, far_back, far_on, out, total):
    total[...] = d_kv[...]
    for start, part in ((info[TAIL_FROM], near_back), (info[EDGE_FROM], far_back)):
        place, skip = window(start, part.shape[0], total.shape[0])
        total[place, :] += moved(part[...], skip)
    for part in (near_on, far_on):
        total[: part.shape[0], :] += part[...].astype(F32)
    n = dq.shape[1]
    out[:, :n] = dq[...]
    out[:, n:] = total[...].astype(BF)


def copy_after(source, deps):
    return sum_after([source], source.dtype, deps)


def shift(value, steps):
    count = lax.axis_size("g")
    pairs = [(i, i + steps) for i in range(count) if 0 <= i + steps < count]
    if not pairs:
        return jnp.zeros_like(value)
    return lax.ppermute(value, "g", pairs)


def if_needed(predicate, run, *values):
    return lax.cond(predicate, run, lambda *v: tuple(jnp.zeros_like(a) for a in v), *values)


def over_x(value):
    return lax.ppermute(value, "x", SWAP)


def over_y(value):
    return lax.ppermute(value, "y", SWAP)


def over_core(value):
    return lax.ppermute(value, "c", SWAP)


def over_xy(value):
    return lax.ppermute(value, ("y", "x"), [(0, 3), (1, 2), (2, 1), (3, 0)])


def over_groups(sums):
    return lax.psum_scatter(sums, "g", scatter_dimension=0, tiled=True)


def spread_begin(value):
    return value, over_x(value), over_y(value)


def spread_next(begun, deps=()):
    value, from_x, from_y = begun
    cut = value.shape[0] // 2
    on_y, on_x = from_x[:cut], from_y[cut:]
    if deps:
        on_y, on_x = sum_after([on_y], BF, deps), sum_after([on_x], BF, deps)
    return value, from_x, from_y, on_y, on_x, over_y(on_y), over_x(on_x)


def spread_end(state, deps=()):
    value, from_x, from_y, _, _, low, high = state
    if deps:
        low, high = sum_after([low], BF, deps), sum_after([high], BF, deps)
    own = jnp.stack([value, from_x, from_y, jnp.concatenate([low, high], axis=0)])
    return own, over_core(own)


def spread(value, deps=()):
    return spread_end(spread_next(spread_begin(value), deps))


def add16(*parts):
    total = parts[0].astype(F32)
    for part in parts[1:]:
        total = total + part.astype(F32)
    return total


def core_sum(own, oth, deps=(), time=3):
    other = over_core(oth)
    half, width = own.shape[1:]
    cut = half // 2
    cuts = ((0, 0, half), (3, 0, cut), (3, cut, half), (1, 0, cut), (1, cut, half), (2, 0, cut), (2, cut, half))

    def body(*refs):
        for out, (j, low, high) in zip(refs[2:], cuts):
            out[...] = (refs[0][j, low:high, :].astype(F32) + refs[1][j, low:high, :].astype(F32)).astype(BF)

    return pl.pallas_call(
        after(body, 2, len(deps)),
        out_shape=tuple(jax.ShapeDtypeStruct((high - low, width), BF) for _, low, high in cuts),
        in_specs=[VMEM] * 2 + [ANY] * len(deps),
        out_specs=(VMEM,) * len(cuts),
        compiler_params=pltpu.CompilerParams(vmem_limit_bytes=VMEM_LIMIT),
        cost_estimate=took_us(time),
    )(own, other, *deps)


def collect_begin(pieces):
    mine, far_x, far_y, x_low, x_high, y_low, y_high = pieces
    from_x, from_y = over_x(far_x), over_y(far_y)
    return mine, x_high, y_low, from_x, from_y, over_x(x_low), over_y(y_high)


def collect_next(begun, deps=(), time=1):
    mine, x_high, y_low, from_x, from_y, first_x, first_y = begun
    on_x, on_y = sum_after((x_high, from_y), BF, deps, time), sum_after((y_low, from_x), BF, deps, time)
    return mine, first_x, first_y, on_x, on_y, over_x(on_x), over_y(on_y)


def sums_of_shares(shares, top_rows, g, q, deps):
    groups = lax.axis_size("g")
    pick = lambda values, at: lax.dynamic_index_in_dim(values, at, 0, keepdims=False)
    is_top = (jnp.arange(shares.shape[1]) >= shares.shape[1] - top_rows)[:, None]
    join = lambda a, b: jnp.where(is_top, jnp.maximum(a, b), a + b)
    shares = jnp.moveaxis(shares.reshape((groups, BLOCKS) + shares.shape[1:]), 1, 0)
    got = [over_x(pick(shares, q ^ 1)), over_y(pick(shares, q ^ 2)), over_xy(pick(shares, q ^ 3))]
    shares = join(join(pick(shares, q), got[0]), join(got[1], got[2]))
    shares = sum_after([shares], F32, deps)
    total = pick(shares, g)
    for step in range(1, groups):
        pairs = [(i, (i + step) % groups) for i in range(groups)]
        total = join(total, lax.ppermute(pick(shares, lax.rem(g + step, groups)), "g", pairs))
    return total


def pick_pieces(pieces, place, deps=()):
    shape = pieces.shape[1:]

    def body(place_ref, source, *outs):
        for j, out in enumerate(outs):
            out[...] = source[place_ref[1] ^ j]

    return pl.pallas_call(
        after(body, 2, len(deps)),
        out_shape=(jax.ShapeDtypeStruct(shape, pieces.dtype),) * BLOCKS,
        in_specs=[SMEM, VMEM] + [ANY] * len(deps),
        out_specs=(VMEM,) * BLOCKS,
        compiler_params=pltpu.CompilerParams(vmem_limit_bytes=VMEM_LIMIT),
        cost_estimate=took_us(2),
    )(place, pieces, *deps)


def swap_pieces(picked):
    own, to_x, to_y, to_xy = picked
    return own, over_x(to_x), over_y(to_y), over_xy(to_xy)


def pick_heads(image, text, place):
    share, parts, columns = image.shape
    n = columns // BLOCKS

    def body(place_ref, image_ref, text_ref, *outs):
        for j, out in enumerate(outs):
            for b in range(BLOCKS):

                @pl.when((place_ref[1] ^ j) == b)
                def _():
                    for k, source in enumerate((image_ref, text_ref)):
                        for p in range(parts):
                            at = (parts * k + p) * n
                            out[:, at : at + n] = source[p, :, b * n : (b + 1) * n]

    return pl.pallas_call(
        body,
        out_shape=(jax.ShapeDtypeStruct((share, 2 * parts * n), image.dtype),) * BLOCKS,
        in_specs=[SMEM, VMEM, VMEM],
        out_specs=(VMEM,) * BLOCKS,
        compiler_params=pltpu.CompilerParams(vmem_limit_bytes=VMEM_LIMIT),
        cost_estimate=took_us(2),
    )(place, jnp.swapaxes(image, 0, 1), jnp.swapaxes(text, 0, 1))


def arrange(got, place, body, out_shape, deps=(), time=2):
    n = len(got)

    def kernel(place_ref, *refs):
        for j in range(n):
            body(place_ref[1] ^ j, refs[j], refs[n:])

    return pl.pallas_call(
        after(kernel, 1 + n, len(deps)),
        out_shape=out_shape,
        in_specs=[SMEM] + [VMEM] * n + [ANY] * len(deps),
        out_specs=(VMEM,) * len(out_shape),
        compiler_params=pltpu.CompilerParams(vmem_limit_bytes=VMEM_LIMIT),
        cost_estimate=took_us(time),
    )(place, *got, *deps)


def stack_rows(b, piece, outs):
    rows, at = piece.shape[0], 0
    for out in outs:
        n = out.shape[1]
        out[pl.ds(pl.multiple_of(b * rows, ALIGN), rows), :] = piece[:, at : at + n]
        at += n


def give_wide(b, piece, outs):
    n = piece.shape[1] // 2
    for k, out in enumerate(outs):
        out[:, pl.ds(pl.multiple_of(b * n, SUB), n)] = piece[:, k * n : (k + 1) * n].astype(F32)


def give_qkv(b, piece, outs):
    n = piece.shape[1] // 6
    for at in range(BLOCKS):

        @pl.when(b == at)
        def _():
            for k, out in enumerate(outs):
                for p in range(3):
                    out[p, :, at * n : (at + 1) * n] = piece[:, (3 * k + p) * n : (3 * k + p + 1) * n].astype(F32)


def give_narrow(b, piece, outs):
    n = piece.shape[1] // 2
    for at in range(BLOCKS):

        @pl.when(b == at)
        def _():
            for k, out in enumerate(outs):
                out[:, at * n : (at + 1) * n] = piece[:, k * n : (k + 1) * n].astype(F32)


def local(
    tokens,
    cotangent,
    seq_offsets,
    block_offsets,
    image_mod,
    text_mod,
    image_qkv,
    text_qkv,
    image_out,
    text_out,
    image_fc1,
    text_fc1,
    image_fc2,
    text_fc2,
    clip_limits,
):
    rows_cap, width = tokens.shape
    half = rows_cap // 2
    share = image_qkv.shape[0]
    columns = image_qkv.shape[2]
    group_rows = BLOCKS * rows_cap
    mine = columns // BLOCKS
    fc = image_fc1.shape[1] // BLOCKS
    heads = mine // HEAD
    seq_count = seq_offsets.shape[0] - 1
    n_groups = lax.axis_size("g")
    g, c = lax.axis_index("g"), lax.axis_index("c")
    q = 2 * lax.axis_index("y") + lax.axis_index("x")

    def both_halves(rows):
        other = over_core(rows)
        return jnp.where(c == 0, jnp.concatenate([rows, other], axis=0), jnp.concatenate([other, rows], axis=0))

    def quarter_turned(inputs):
        return jnp.swapaxes(inputs.reshape(BLOCKS, -1, share), 1, 2)

    def quarter_wide(inputs):
        return jnp.swapaxes(inputs.reshape(share, BLOCKS, -1), 0, 1)

    place = jnp.stack([g, q, c]).astype(jnp.int32)
    plane_of = lambda *cuts: tuple(jax.ShapeDtypeStruct((BLOCKS * share, n), BF) for n in cuts)
    (plane_qkv,) = arrange(swap_pieces(pick_heads(image_qkv, text_qkv, place)), place, stack_rows, plane_of(6 * mine))

    n_tiles = group_rows // CHUNK
    reach = 2 * KEYS + 2 * TAIL_PAD + group_rows
    n_chunks = reach // KEYS
    info, chunks = pl.pallas_call(
        functools.partial(layout_kernel, group_rows),
        out_shape=(
            jax.ShapeDtypeStruct((INFO,), jnp.int32),
            jax.ShapeDtypeStruct((3 * n_chunks + 3 * n_tiles + 4,), jnp.int32),
        ),
        in_specs=[SMEM] * 3,
        out_specs=(SMEM, SMEM),
        cost_estimate=took_us(1),
    )(seq_offsets, block_offsets, place)

    my_rows = lambda inputs: lax.dynamic_slice_in_dim(inputs, c * half, half, 0)
    my_tokens, my_cotangent = my_rows(tokens), my_rows(cotangent)

    def rows_kernel(body, kinds, args, time, deps=(), extra=(), scratches=()):
        return pl.pallas_call(
            after(body, 1 + len(args), len(deps)),
            out_shape=tuple(jax.ShapeDtypeStruct((half, width), kind) for kind in kinds) + tuple(extra),
            in_specs=[SMEM] + [VMEM] * len(args) + [ANY] * len(deps),
            out_specs=(VMEM,) * (len(kinds) + len(extra)),
            scratch_shapes=list(scratches),
            compiler_params=pltpu.CompilerParams(vmem_limit_bytes=VMEM_LIMIT),
            cost_estimate=took_us(time),
        )(info, *args, *deps)

    parts_of = lambda state: (*state[:3], *state[5:])
    modulated, grad_mlp = rows_kernel(enter_kernel, (BF, BF), (tokens, cotangent, image_mod, text_mod), 4)

    slot = lambda n: jax.ShapeDtypeStruct((BLOCKS, half, n), BF)
    full = lambda n: jax.ShapeDtypeStruct((BLOCKS, rows_cap, n), BF)
    rows_of = lambda n, kind: jax.ShapeDtypeStruct((group_rows, n), kind)
    slot_block = block((half, width))
    scratch = lambda rows, n, kind=BF: pltpu.VMEM((rows, n), kind)
    weight_pair = lambda n: [scratch(width, n), scratch(width, n)]

    whole_qkv = lax.all_gather(plane_qkv, "g", axis=0, tiled=True)
    mod_begun = spread_begin(modulated)
    pack_rest = jnp.concatenate(
        [
            quarter_wide(image_fc1),
            quarter_wide(text_fc1),
            quarter_turned(image_fc2),
            quarter_turned(text_fc2),
            quarter_turned(image_out),
            quarter_turned(text_out),
        ],
        axis=2,
    )
    rest_picked = pick_pieces(pack_rest, place)
    rest_got = swap_pieces(rest_picked)
    mod_own, mod_oth = spread_end(spread_next(mod_begun, rest_picked[:1]), rest_got[1:])
    plane_fc1, plane_fc2, plane_out = arrange(rest_got, place, stack_rows, plane_of(2 * fc, 2 * fc, 2 * mine))
    whole_out = lax.all_gather(plane_out, "g", axis=0, tiled=True)
    whole_fc2 = lax.all_gather(plane_fc2, "g", axis=0, tiled=True)

    pair = lambda rows: jax.ShapeDtypeStruct((rows, 2 * mine), BF)
    queries, pairs, tail, edge, head, head_edge = stepped(
        project_kernel,
        BLOCKS,
        [SMEM, slot_block, slot_block, whole(whole_qkv.shape)],
        [kept(s) for s in ((group_rows, mine), (group_rows, 2 * mine), (TAIL, 2 * mine), (EDGE, 2 * mine), (TAIL, 2 * mine), (EDGE, 2 * mine))],
        (rows_of(mine, BF), pair(group_rows), pair(TAIL), pair(EDGE), pair(TAIL), pair(EDGE)),
        weight_pair(3 * mine) + [scratch(group_rows, 3 * mine), scratch(rows_cap, width), scratch(rows_cap, 3 * mine)],
        6,
    )(info, mod_own, mod_oth, whole_qkv)

    near_back, near_on = shift(tail, 1), shift(head, -1)
    gmlp_begun = spread_begin(copy_after(grad_mlp, (queries,)))
    fc1_piece = copy_after(plane_fc1, (near_back, near_on, *gmlp_begun[1:]))
    whole_fc1 = lax.all_gather(fc1_piece, "g", axis=0, tiled=True)
    gmlp_state = spread_next(gmlp_begun, (near_back, near_on, whole_out))
    gmlp_own, gmlp_oth = spread_end(gmlp_state)
    need_far = jnp.min(block_offsets[BLOCKS::BLOCKS] - block_offsets[:-1:BLOCKS]) < IMG + TXT
    far_back, far_on = if_needed(need_far, lambda a, b: (shift(a, 2), shift(b, -2)), edge, head_edge)
    sources = (far_back, near_back, pairs, near_on, far_on)
    source_specs = [whole(s.shape) for s in sources]

    tile_spec = pl.BlockSpec((CHUNK, mine), lambda t: (t, 0))
    log_spec = block((8, CHUNK))
    attended, attended_exact, logs, tops = stepped(
        attend_kernel,
        n_tiles,
        [SMEM, SMEM, tile_spec, *source_specs],
        (tile_spec, tile_spec, log_spec, kept((8, CHUNK))),
        (
            rows_of(mine, BF),
            rows_of(mine, F32),
            jax.ShapeDtypeStruct((n_tiles, 8, CHUNK), F32),
            jax.ShapeDtypeStruct((8, CHUNK), F32),
        ),
        [
            scratch(reach, mine),
            scratch(reach, mine),
            scratch(mine, reach),
            pltpu.VMEM((heads, mine, CHUNK), BF),
            pltpu.VMEM((heads, n_chunks, KEYS, CHUNK), F32),
            scratch(KEYS, heads * CHUNK),
            scratch(mine, CHUNK, F32),
            scratch(8 * heads, CHUNK, F32),
        ],
        1,
        (*gmlp_state[3:5], fc1_piece),
    )(chunks, seq_offsets, queries, *sources)

    def to_slots(n, first, rows, w, deps=(), time=10):
        return stepped(
            functools.partial(rows_to_slots_kernel, first),
            BLOCKS,
            [SMEM, whole(rows.shape), whole(w.shape)],
            (slot_block, slot_block),
            (slot(width), slot(width)),
            weight_pair(n) + [scratch(rows_cap, n), scratch(rows_cap, width)],
            time,
            deps,
        )(info, rows, w)

    branch_state = collect_next(collect_begin(core_sum(*to_slots(mine, 0, attended, whole_out, (), 1))), (whole_fc1,))
    branch, modulated_mlp = rows_kernel(
        middle_kernel, (F32, BF), (*parts_of(branch_state), my_tokens, image_mod, text_mod), 4, (gmlp_oth,)
    )
    mm_own, mm_oth = spread(modulated_mlp)
    fc_block = block((rows_cap, fc))
    hid, slope = stepped(
        mlp_up_kernel,
        BLOCKS,
        [SMEM, slot_block, slot_block, columns_from(width, fc, 0), columns_from(width, fc, 1)],
        (fc_block, fc_block),
        (full(fc), full(fc)),
        [scratch(rows_cap, width), scratch(rows_cap, fc, F32)],
        1,
    )(info, mm_own, mm_oth, whole_fc1, whole_fc1)

    def slot_sums(left, right, deps, time):
        return stepped(
            slot_sums_kernel,
            BLOCKS,
            [SMEM, slot_block, slot_block, fc_block],
            kept((width, 2 * fc)),
            jax.ShapeDtypeStruct((width, 2 * fc), BF),
            [scratch(width, fc, F32), scratch(width, fc, F32), scratch(rows_cap, width)],
            time,
            deps,
        )(info, *left, right)

    def row_sums(left, rows, deps=(), time=0.1):
        n = rows.shape[1]
        return stepped(
            row_sums_kernel,
            BLOCKS,
            [SMEM, slot_block, slot_block, whole(rows.shape)],
            kept((width, 2 * n)),
            jax.ShapeDtypeStruct((width, 2 * n), BF),
            [scratch(width, n, F32), scratch(width, n, F32), scratch(rows_cap, width), scratch(rows_cap, n)],
            time,
            deps,
        )(info, *left, rows)

    fc2_sums = slot_sums((gmlp_own, gmlp_oth), hid, (), 1)
    fc2_part = over_groups(fc2_sums)
    gm_own, gm_oth, gb = stepped(
        mlp_back_kernel,
        BLOCKS,
        [SMEM, slot_block, slot_block, fc_block] + [columns_from(width, fc, at) for at in (0, 1, 0, 1)],
        (slot_block, slot_block, fc_block),
        (slot(width), slot(width), full(fc)),
        [scratch(rows_cap, width), scratch(rows_cap, fc), scratch(rows_cap, width)],
        1,
        (fc2_sums,),
    )(info, gmlp_own, gmlp_oth, slope, whole_fc1, whole_fc1, whole_fc2, whole_fc2)

    gm_part = core_sum(gm_own, gm_oth)
    gm_state = collect_begin(gm_part)
    fc1_sums = slot_sums((mm_own, mm_oth), gb, gm_part, 12)
    fc1_part = over_groups(fc1_sums)
    gm_state = collect_next(gm_state, (fc1_sums,), 1)
    mlp_own, mlp_oth = stepped(
        slots_to_slots_kernel,
        BLOCKS,
        [SMEM, fc_block, columns_from(width, fc, 0), columns_from(width, fc, 1)],
        (slot_block, slot_block),
        (slot(width), slot(width)),
        [scratch(rows_cap, width)],
        25,
        gm_state[3:5],
    )(info, hid, whole_fc2, whole_fc2)
    grad_mod_mlp, grad_first, grad_branch = rows_kernel(
        turn_kernel,
        (F32, F32, BF),
        (*parts_of(gm_state), branch, my_tokens, my_cotangent, image_mod, text_mod),
        5,
        (mlp_own,),
    )
    gbr_begun = spread_begin(grad_branch)
    gbr_own, gbr_oth = spread_end(spread_next(gbr_begun, (fc2_part,)))
    grad_attended = stepped(
        functools.partial(back_project_kernel, 0),
        BLOCKS,
        [SMEM, slot_block, slot_block, whole(whole_out.shape)],
        kept((group_rows, mine)),
        rows_of(mine, BF),
        weight_pair(mine) + [scratch(rows_cap, width), scratch(rows_cap, mine)],
        1,
    )(info, gbr_own, gbr_oth, whole_out)

    mlp_part = core_sum(mlp_own, mlp_oth, (gbr_oth,), 3)
    mlp_state = collect_begin(mlp_part)
    dq, give_far_back, give_back, d_pairs, give_on, give_far_on = stepped(
        attend_back_kernel,
        n_tiles,
        [SMEM, SMEM, tile_spec, tile_spec, tile_spec, *source_specs, log_spec],
        (tile_spec, *(kept(s.shape) for s in sources)),
        (rows_of(mine, BF), pair(EDGE), pair(TAIL), rows_of(2 * mine, F32), pair(TAIL), pair(EDGE)),
        [
            scratch(reach, mine),
            scratch(reach, mine),
            scratch(mine, reach),
            scratch(heads * CHUNK, mine),
            scratch(heads * CHUNK, mine),
            pltpu.VMEM((heads, mine, CHUNK), BF),
            pltpu.VMEM((heads, mine, CHUNK), BF),
            pltpu.VMEM((heads, KEYS, CHUNK), F32),
            pltpu.VMEM((heads, KEYS, CHUNK), F32),
            scratch(KEYS, heads * CHUNK),
            scratch(KEYS, heads * CHUNK),
            scratch(mine, CHUNK, F32),
            scratch(reach, mine, F32),
            scratch(reach, mine, F32),
        ],
        1,
        (mlp_part[0],),
    )(chunks, seq_offsets, queries, grad_attended, attended_exact, *sources, logs)
    gave_back, gave_on = shift(give_back, -1), shift(give_on, 1)
    gave_far_back, gave_far_on = if_needed(
        need_far, lambda a, b: (shift(a, -2), shift(b, 2)), give_far_back, give_far_on
    )

    out_sums = row_sums((gbr_own, gbr_oth), attended, (dq,))
    out_part = over_groups(copy_after(out_sums, (gave_back, gave_on)))
    mlp_state = collect_next(mlp_state, (out_sums,), 1)
    pieces_of = lambda part, deps: pick_pieces(part.reshape(BLOCKS, share, -1), place, deps)
    grad_qkv = pl.pallas_call(
        after(gather_grads_kernel, 7, 2),
        out_shape=rows_of(3 * mine, BF),
        in_specs=[SMEM] + [VMEM] * 6 + [ANY] * 2,
        out_specs=VMEM,
        scratch_shapes=[scratch(group_rows, 2 * mine, F32)],
        compiler_params=pltpu.CompilerParams(vmem_limit_bytes=VMEM_LIMIT),
        cost_estimate=took_us(8),
    )(info, dq, d_pairs, gave_back, gave_on, gave_far_back, gave_far_on, out_sums, fc1_part)

    mod_sent = to_slots(3 * mine, 0, grad_qkv, whole_qkv, mlp_state[3:5], 0.1)
    qkv_sums = row_sums((mod_own, mod_oth), grad_qkv, (*mod_sent, *mlp_state[5:]), 14)
    qkv_part = over_groups(qkv_sums)
    mod_part = core_sum(*mod_sent, (qkv_sums,), 3)
    mod_state = collect_next(collect_begin(mod_part), mod_part[:1], 1)
    pair_f32 = lambda *shape: (jax.ShapeDtypeStruct(shape, F32),) * 2
    fc2_picked, fc1_picked = pieces_of(fc2_part, mod_state[3:5]), pieces_of(fc1_part, mod_state[3:5])
    out_picked = pieces_of(out_part, mod_state[3:5])
    fc2_got, fc1_got, out_got = swap_pieces(fc2_picked), swap_pieces(fc1_picked), swap_pieces(out_picked)
    tokens_grad_rows, mixed_rows, mod_sum = rows_kernel(
        leave_kernel,
        (F32, BF),
        (
            *parts_of(mod_state),
            *parts_of(mlp_state),
            grad_first,
            branch,
            grad_mod_mlp,
            my_tokens,
            my_cotangent,
            image_mod,
            text_mod,
        ),
        12,
        (fc2_picked[0], fc1_picked[0], out_picked[0]),
        (jax.ShapeDtypeStruct((2 * seq_count, 6, width), F32),),
        (scratch(half, width, F32), scratch(half, width, F32)),
    )
    mixed = both_halves(mixed_rows)
    qkv_got = swap_pieces(pieces_of(qkv_part, (mod_sum,)))
    fc2_outs = arrange(fc2_got, place, give_wide, pair_f32(share, BLOCKS * fc))
    fc1_outs = arrange(fc1_got, place, give_wide, pair_f32(share, BLOCKS * fc))
    out_outs = arrange(out_got, place, give_narrow, pair_f32(share, columns))
    qkv_outs = arrange(qkv_got, place, give_qkv, pair_f32(3, share, columns))
    mod_sum = mod_sum.reshape(2 * seq_count * 6, -1, share)
    mod_sum = jnp.swapaxes(mod_sum, 0, 1)
    mod_sum = mod_sum + over_core(mod_sum)
    head_top = jnp.max(tops[:heads], axis=1)
    spot = jnp.arange(BLOCKS)[:, None] == q
    head_top = jnp.where(spot, head_top[None, :], NEGATIVE).reshape(-1)
    n_heads = head_top.shape[0]
    head_top = jnp.pad(head_top, (0, -n_heads % share))[None, :]
    top_rows = -(-n_heads // share)
    head_top = jnp.broadcast_to(head_top.reshape(1, top_rows, share), (mod_sum.shape[0], top_rows, share))
    mod_sum = sums_of_shares(jnp.concatenate([mod_sum, head_top], axis=1), top_rows, g, q, qkv_got)
    head_max = mod_sum[-top_rows:].reshape(-1)[:n_heads]
    mod_sum = mod_sum[:-top_rows].reshape(2, seq_count, 6, share)
    root_factor = jnp.sqrt(clip_limits / jnp.maximum(head_max, clip_limits))
    column_scale = jnp.repeat(root_factor, HEAD)[None, None, :]
    clipped = tuple((w[:, :2, :].astype(F32) * column_scale).astype(BF) for w in (image_qkv, text_qkv))

    return (
        mixed,
        both_halves(tokens_grad_rows),
        mod_sum[0],
        mod_sum[1],
        *(jnp.swapaxes(part, 0, 1) for part in qkv_outs),
        *(part.T for part in out_outs),
        *fc1_outs,
        *(part.T for part in fc2_outs),
        head_max,
        *clipped,
    )


def solution(mesh):
    devices = mesh.devices
    split = Mesh(devices.reshape(devices.shape[0] // BLOCKS, 2, 2, devices.shape[1]), ("g", "y", "x", "c"))
    dp = ("g", "y", "x")
    placed = (
        P(dp, None),
        P(dp, None),
        P(),
        P(),
        P(),
        P(),
        P(dp, None, "c"),
        P(dp, None, "c"),
        P("c", dp),
        P("c", dp),
        P(dp, "c"),
        P(dp, "c"),
        P("c", dp),
        P("c", dp),
        P("c"),
    )
    return jax.shard_map(
        local,
        mesh=split,
        in_specs=placed,
        out_specs=(
            P(dp, None),
            P(dp, None),
            P(None, None, dp),
            P(None, None, dp),
            P(dp, None, "c"),
            P(dp, None, "c"),
            P("c", dp),
            P("c", dp),
            P(dp, "c"),
            P(dp, "c"),
            P("c", dp),
            P("c", dp),
            P("c"),
            P(dp, None, "c"),
            P(dp, None, "c"),
        ),
        check_vma=False,
    )
```

```python
import functools

import jax
import jax.numpy as jnp
from jax import lax
from jax.experimental import pallas as pl
from jax.experimental.pallas import tpu as pltpu
from jax.sharding import Mesh, PartitionSpec as P

HEAD = 64
IMG = 1024
TXT = 154
EPSILON = 1e-06
NEGATIVE = -1e30
BLOCKS = 4
SUB = 128
TAIL = 1184
TAIL_PAD = 1536
EDGE = 160
CHUNK = 256
KEYS = 512
SLAB = 64
ALIGN = 16
TEXT_ROWS = 176
BF = jnp.bfloat16
F32 = jnp.float32
SWAP = [(0, 1), (1, 0)]
VMEM_LIMIT = 60 * 1024 * 1024

VMEM = pl.BlockSpec(memory_space=pltpu.VMEM)
SMEM = pl.BlockSpec(memory_space=pltpu.SMEM)
ANY = pl.BlockSpec(memory_space=pl.ANY)

COUNT, OFFSET, TEXT_FROM, TEXT_TO = 0, 4, 8, 12
CORE, TAIL_FROM, EDGE_FROM, OWN_FROM, OWN_SEQ, NEXT_FROM, HALF, INFO = 16, 17, 18, 19, 20, 21, 22, 23


def dot(a, b):
    return jnp.dot(a, b, preferred_element_type=F32)


def dot_back(a, b):
    return lax.dot_general(a, b, (((1,), (1,)), ((), ())), preferred_element_type=F32)


def dot_rows(a, b):
    return lax.dot_general(a, b, (((0,), (0,)), ((), ())), preferred_element_type=F32)


def took_us(time):
    return pl.CostEstimate(flops=int(time * 1.15e9), bytes_accessed=int(time * 1e6), transcendentals=0)


def after(body, n_in, n_deps):
    return lambda *refs: body(*refs[:n_in], *refs[n_in + n_deps :])


def whole(shape):
    return pl.BlockSpec(shape, lambda j: (0,) * len(shape), pipeline_mode=pl.Buffered(1))


def kept(shape):
    return pl.BlockSpec(shape, lambda j: (0,) * len(shape))


def block(shape):
    return pl.BlockSpec((1,) + shape, lambda j: (j,) + (0,) * len(shape))


def columns_from(rows, n, at):
    return pl.BlockSpec((rows, n), lambda j: (0, at), pipeline_mode=pl.Buffered(1))


def stepped(body, steps, in_specs, out_specs, out_shape, scratch, time, deps=()):
    run = pl.pallas_call(
        after(body, len(in_specs), len(deps)),
        grid=(steps,),
        out_shape=out_shape,
        in_specs=list(in_specs) + [ANY] * len(deps),
        out_specs=out_specs,
        scratch_shapes=list(scratch),
        compiler_params=pltpu.CompilerParams(vmem_limit_bytes=VMEM_LIMIT),
        cost_estimate=took_us(time),
    )
    return lambda *args: run(*args, *deps)


def sum_after(parts, kind, deps, time=1):
    n = len(parts)

    def body(*refs):
        total = refs[0][...].astype(F32)
        for part in refs[1:n]:
            total = total + part[...].astype(F32)
        refs[n][...] = total.astype(kind)

    return pl.pallas_call(
        after(body, n, len(deps)),
        out_shape=jax.ShapeDtypeStruct(parts[0].shape, kind),
        in_specs=[VMEM] * n + [ANY] * len(deps),
        out_specs=VMEM,
        compiler_params=pltpu.CompilerParams(vmem_limit_bytes=VMEM_LIMIT),
        cost_estimate=took_us(time),
    )(*parts, *deps)


def window(start, rows, total):
    base = jnp.minimum(lax.shift_right_logical(start, 4) * ALIGN, total - rows - ALIGN)
    return pl.ds(pl.multiple_of(base, ALIGN), rows + ALIGN), start - base


def moved(part, skip):
    rows = part.shape[0]
    shape = (rows + ALIGN, rows)
    there = lax.broadcasted_iota(jnp.int32, shape, 0) - skip
    return dot((there == lax.broadcasted_iota(jnp.int32, shape, 1)).astype(F32).astype(BF), part)


def read_rows(ref, start, rows):
    place, skip = window(start, rows, ref.shape[0])
    shape = (rows, rows + ALIGN)
    here = lax.broadcasted_iota(jnp.int32, shape, 1) - skip
    pick = (here == lax.broadcasted_iota(jnp.int32, shape, 0)).astype(F32).astype(BF)
    return dot(pick, ref[place, :]).astype(BF)


def layout_kernel(group_rows, seq, blocks, place, info, chunks):
    g, q = place[0], place[1]
    n_groups, n_seq = (blocks.shape[0] - 1) // BLOCKS, seq.shape[0] - 1
    start, stop = blocks[g * BLOCKS], blocks[g * BLOCKS + BLOCKS]

    def seq_of(position, shift):
        found = jnp.int32(0)
        for s in range(n_seq):
            found = jnp.where(position >= seq[s], s + shift, found)
        return found

    for j in range(BLOCKS):
        b = g * BLOCKS + (q ^ j)
        low, high = blocks[b], blocks[b + 1]
        text_from, text_to = jnp.int32(0), jnp.int32(0)
        for s in range(n_seq):
            first, last = jnp.maximum(seq[s] + IMG, low), jnp.minimum(seq[s + 1], high)
            text_from = jnp.where(first < last, first - low, text_from)
            text_to = jnp.where(first < last, last - low, text_to)
        info[COUNT + j] = high - low
        info[OFFSET + j] = low - start
        info[TEXT_FROM + j] = text_from
        info[TEXT_TO + j] = text_to
    own = blocks[g * BLOCKS + q]
    info[CORE] = place[2]
    info[TAIL_FROM] = jnp.maximum(stop - start - TAIL, 0)
    info[EDGE_FROM] = jnp.maximum(stop - start - EDGE, 0)
    info[OWN_FROM] = own
    info[HALF] = group_rows // (2 * BLOCKS)
    info[OWN_SEQ] = seq_of(own, 0)
    info[NEXT_FROM] = seq[seq_of(own, 0) + 1]

    def span(steps):
        there = (g + steps >= 0) & (g + steps < n_groups)
        at = jnp.clip(g + steps, 0, n_groups - 1) * BLOCKS
        return jnp.where(there, blocks[at], 0), jnp.where(there, blocks[at + BLOCKS], 0)

    before, behind, ahead, beyond = span(-2), span(-1), span(1), span(2)
    n_chunks = (2 * KEYS + 2 * TAIL_PAD + group_rows) // KEYS
    i = 0
    for base, low, high, rows in (
        (jnp.maximum(before[1] - EDGE, before[0]) - (KEYS - EDGE), jnp.maximum(before[1] - EDGE, before[0]), before[1], KEYS),
        (
            jnp.maximum(behind[1] - TAIL, behind[0]) - (TAIL_PAD - TAIL),
            jnp.maximum(behind[1] - TAIL, behind[0]),
            behind[1],
            TAIL_PAD,
        ),
        (start, start, stop, group_rows),
        (ahead[0], ahead[0], jnp.minimum(ahead[1], ahead[0] + TAIL), TAIL_PAD),
        (beyond[0], beyond[0], jnp.minimum(beyond[1], beyond[0] + EDGE), KEYS),
    ):
        for step in range(rows // KEYS):
            chunks[i] = base + step * KEYS
            chunks[n_chunks + i] = low
            chunks[2 * n_chunks + i] = high
            i += 1
    n_tiles = group_rows // CHUNK
    for t in range(n_tiles):
        first = start + t * CHUNK
        last = jnp.minimum(first + CHUNK, stop) - 1
        chunks[3 * n_chunks + 2 * t] = jnp.where(first < stop, seq[seq_of(first, 0)], 0)
        chunks[3 * n_chunks + 2 * t + 1] = jnp.where(first < stop, seq[seq_of(last, 1)], 0)
        one = (first + CHUNK <= stop) & (seq_of(first, 0) == seq_of(last, 0))
        chunks[3 * n_chunks + 2 * n_tiles + 2 + t] = jnp.where(one, 1, 0)
    chunks[3 * n_chunks + 3 * n_tiles + 2] = seq[seq_of(start, 0)]
    chunks[3 * n_chunks + 3 * n_tiles + 3] = seq[seq_of(stop - 1, 1)]
    chunks[3 * n_chunks + 2 * n_tiles] = start
    chunks[3 * n_chunks + 2 * n_tiles + 1] = stop


def lane_spans(chunks, seq, n_chunks, n_tiles, t):
    start, stop = chunks[3 * n_chunks + 2 * n_tiles], chunks[3 * n_chunks + 2 * n_tiles + 1]
    position = start + t * CHUNK + lax.broadcasted_iota(jnp.int32, (1, CHUNK), 1)
    low, high = jnp.zeros_like(position), jnp.zeros_like(position)
    for s in range(seq.shape[0] - 1):
        hit = (position >= seq[s]) & (position < seq[s + 1]) & (position < stop)
        low, high = jnp.where(hit, seq[s], low), jnp.where(hit, seq[s + 1], high)
    return low, high


def own_kinds(info, first, rows):
    ids = row_ids(info[CORE] * info[HALF] + first, rows)
    live = ids < info[COUNT]
    is_text = live & (ids >= info[TEXT_FROM]) & (ids < info[TEXT_TO])
    is_next = live & (info[OWN_FROM] + ids >= info[NEXT_FROM])
    return live, live & jnp.logical_not(is_text | is_next), is_next, is_text


def vector_of(info, image_mod, text_mod, is_next, is_text):
    s = info[OWN_SEQ]
    after_s = jnp.minimum(s + 1, image_mod.shape[0] - 1)

    def pick(i):
        own, text, following = image_mod[s][i : i + 1], text_mod[s][i : i + 1], image_mod[after_s][i : i + 1]
        return jnp.where(is_text, text, jnp.where(is_next, following, own))

    return pick


def normal(rows):
    centered = rows - jnp.mean(rows, axis=1, keepdims=True)
    inverse = lax.rsqrt(jnp.mean(centered * centered, axis=1, keepdims=True) + EPSILON)
    return centered * inverse, inverse


def normal_back(grad, normed, inverse):
    return inverse * (
        grad - jnp.mean(grad, axis=1, keepdims=True) - normed * jnp.mean(grad * normed, axis=1, keepdims=True)
    )


def enter_kernel(info, tokens, cotangent, image_mod, text_mod, modulated, grad_mlp):
    half = modulated.shape[0]
    place = pl.ds(pl.multiple_of(info[CORE] * half, half), half)
    live, _, is_next, is_text = own_kinds(info, 0, half)
    pick = vector_of(info, image_mod, text_mod, is_next, is_text)
    normed, _ = normal(tokens[place, :].astype(F32))
    modulated[...] = (normed * (1.0 + pick(1)) + pick(0)).astype(BF)
    grad_mlp[...] = (pick(5) * jnp.where(live, cotangent[place, :].astype(F32), 0.0)).astype(BF)


def collected(mine, first_x, first_y, last_x, last_y, out):
    cut = out.shape[0] // 2
    out[:cut, :] = mine[:cut, :].astype(F32) + first_x[...].astype(F32) + last_y[...].astype(F32)
    out[cut:, :] = mine[cut:, :].astype(F32) + last_x[...].astype(F32) + first_y[...].astype(F32)


def middle_kernel(
    info, mine, first_x, first_y, last_x, last_y, tokens, image_mod, text_mod, branch, modulated_mlp
):
    collected(mine, first_x, first_y, last_x, last_y, branch)
    _, _, is_next, is_text = own_kinds(info, 0, branch.shape[0])
    pick = vector_of(info, image_mod, text_mod, is_next, is_text)
    normed, _ = normal(tokens[...].astype(F32) + pick(2) * branch[...])
    modulated_mlp[...] = (normed * (1.0 + pick(4)) + pick(3)).astype(BF)


def turn_kernel(
    info, mine, first_x, first_y, last_x, last_y, branch, tokens, cotangent, image_mod, text_mod,
    grad_mod_mlp, grad_first, grad_branch,
):
    collected(mine, first_x, first_y, last_x, last_y, grad_mod_mlp)
    live, _, is_next, is_text = own_kinds(info, 0, branch.shape[0])
    pick = vector_of(info, image_mod, text_mod, is_next, is_text)
    normed, inverse = normal(tokens[...].astype(F32) + pick(2) * branch[...])
    back = normal_back(grad_mod_mlp[...] * (1.0 + pick(4)), normed, inverse)
    result = jnp.where(live, cotangent[...].astype(F32) + back, 0.0)
    grad_first[...] = result
    grad_branch[...] = (pick(2) * result).astype(BF)


def leave_kernel(
    info, mine, first_x, first_y, last_x, last_y,
    mlp_mine, mlp_first_x, mlp_first_y, mlp_last_x, mlp_last_y,
    grad_first, branch, grad_mod_mlp, tokens, cotangent, image_mod, text_mod,
    tokens_grad, mixed, sums, grad_modulated, mlp_branch,
):
    collected(mine, first_x, first_y, last_x, last_y, grad_modulated)
    collected(mlp_mine, mlp_first_x, mlp_first_y, mlp_last_x, mlp_last_y, mlp_branch)
    sums[...] = jnp.zeros_like(sums)
    n_seq = image_mod.shape[0]
    s = info[OWN_SEQ]
    after_s = jnp.minimum(s + 1, n_seq - 1)
    step = 64
    for low in range(0, tokens_grad.shape[0], step):
        part = slice(low, low + step)
        live, is_own, is_next, is_text = own_kinds(info, low, step)
        pick = vector_of(info, image_mod, text_mod, is_next, is_text)
        rows = tokens[part, :].astype(F32)
        normed, inverse = normal(rows)
        first = rows + pick(2) * branch[part, :]
        normed_mlp, _ = normal(first)

        def add(i, term):
            for kept_rows, at in ((is_own, s), (is_next, after_s), (is_text, n_seq + s)):
                row = jnp.sum(jnp.where(kept_rows, term, 0.0), axis=0, keepdims=True)
                sums[at, i : i + 1, :] += row

        grads = grad_modulated[part, :]
        add(0, grads)
        add(1, grads * normed)
        add(2, grad_first[part, :] * branch[part, :])
        add(3, grad_mod_mlp[part, :])
        add(4, grad_mod_mlp[part, :] * normed_mlp)
        add(5, cotangent[part, :].astype(F32) * mlp_branch[part, :])
        back = normal_back(grads * (1.0 + pick(1)), normed, inverse)
        tokens_grad[part, :] = jnp.where(live, grad_first[part, :] + back, 0.0)
        mixed[part, :] = jnp.where(live, first + pick(5) * mlp_branch[part, :], 0.0).astype(BF)


def row_ids(base, rows):
    return base + lax.broadcasted_iota(jnp.int32, (rows, 1), 0)


def for_rows(info, cap, body):
    count = info[COUNT + pl.program_id(0)]
    low = 0
    for rows in range(cap // 2, cap + 1, SUB):

        @pl.when((count > low) & (count <= rows))
        def _():
            body(rows)

        low = rows


def for_text(info, cap, body):
    j = pl.program_id(0)
    low, high = info[TEXT_FROM + j], info[TEXT_TO + j]

    @pl.when(high > low)
    def _():
        base = jnp.minimum(lax.shift_right_logical(low, 4) * ALIGN, cap - TEXT_ROWS)
        base = pl.multiple_of(base, ALIGN)
        ids = row_ids(base, TEXT_ROWS)
        body(pl.ds(base, TEXT_ROWS), (ids >= low) & (ids < high))


def half_places(info, half):
    mine = pl.multiple_of(info[CORE] * half, half)
    return pl.ds(mine, half), pl.ds(pl.multiple_of(half - mine, half), half)


def join(info, own, oth, out):
    half = own.shape[1]
    at_own, at_oth = half_places(info, half)
    out[at_own, :] = own[0]
    out[at_oth, :] = oth[0]


def part_ways(info, rows_ref, own, oth):
    half = own.shape[1]
    at_own, at_oth = half_places(info, half)
    own[0] = rows_ref[at_own, :]
    oth[0] = rows_ref[at_oth, :]


def split_columns(w, first, image, text):
    n = image.shape[1]
    image[...] = w[:, first : first + n]
    text[...] = w[:, first + n : first + 2 * n]


def to_group_rows(info, own, oth, w_image, w_text, out, joined, tile):
    cap = joined.shape[0]
    join(info, own, oth, joined)

    @pl.when(pl.program_id(0) == 0)
    def _():
        out[...] = jnp.zeros_like(out)

    def body(rows):
        tile[:rows, :] = dot(joined[:rows, :], w_image[...]).astype(BF)

        def text(place, is_text):
            tile[place, :] = jnp.where(is_text, dot(joined[place, :], w_text[...]).astype(BF), tile[place, :])

        for_text(info, cap, text)
        j = pl.program_id(0)
        place, skip = window(info[OFFSET + j], rows, out.shape[0])
        part = moved(tile[:rows, :], skip).astype(BF)
        ids = row_ids(-skip, rows + ALIGN)
        out[place, :] = jnp.where((ids >= 0) & (ids < info[COUNT + j]), part, out[place, :])

    for_rows(info, cap, body)


def project_kernel(info, own, oth, w, q, kv, tail, edge, head, head_edge, w_image, w_text, out, joined, tile):
    @pl.when(pl.program_id(0) == 0)
    def _():
        split_columns(w, 0, w_image, w_text)

    to_group_rows(info, own, oth, w_image, w_text, out, joined, tile)

    @pl.when(pl.program_id(0) == BLOCKS - 1)
    def _():
        n = q.shape[1]
        q[...] = out[:, :n]
        kv[...] = out[:, n:]
        tail[...] = read_rows(kv, info[TAIL_FROM], TAIL)
        edge[...] = read_rows(kv, info[EDGE_FROM], EDGE)
        head[...] = kv[:TAIL, :]
        head_edge[...] = kv[:EDGE, :]


def back_project_kernel(first, info, own, oth, w, out, w_image, w_text, joined, tile):
    @pl.when(pl.program_id(0) == 0)
    def _():
        split_columns(w, first, w_image, w_text)

    to_group_rows(info, own, oth, w_image, w_text, out, joined, tile)


def times_turned(info, x, w_image, w_text, result):
    cap = result.shape[0]

    def body(rows):
        result[:rows, :] = dot_back(x[:rows, :], w_image[...]).astype(BF)
        if rows < cap:
            result[rows:, :] = jnp.zeros((cap - rows, result.shape[1]), BF)

        def text(place, is_text):
            part = dot_back(x[place, :], w_text[...]).astype(BF)
            result[place, :] = jnp.where(is_text, part, result[place, :])

        for_text(info, cap, text)

    for_rows(info, cap, body)


def rows_to_slots_kernel(first, info, rows_ref, w, own, oth, w_image, w_text, x, result):
    j = pl.program_id(0)

    @pl.when(j == 0)
    def _():
        split_columns(w, first, w_image, w_text)

    def take(rows):
        x[:rows, :] = read_rows(rows_ref, info[OFFSET + j], rows)

    for_rows(info, x.shape[0], take)
    times_turned(info, x, w_image, w_text, result)
    part_ways(info, result, own, oth)


def slots_to_slots_kernel(info, x, w_image, w_text, own, oth, result):
    times_turned(info, x.at[0], w_image, w_text, result)
    part_ways(info, result, own, oth)


def gelu_parts(v):
    k = 0.7978845608028654
    square = v * v
    t = jnp.tanh(k * v * (1.0 + 0.044715 * square))
    half = 0.5 * (1.0 + t)
    return v * half, half + 0.5 * v * (1.0 - t * t) * (k + 3 * 0.044715 * k * square)


def mlp_up_kernel(info, x_own, x_oth, w_image, w_text, hid, slope, x, before):
    cap = x.shape[0]
    join(info, x_own, x_oth, x)

    def body(rows):
        before[:rows, :] = dot(x[:rows, :], w_image[...])

        def text(place, is_text):
            before[place, :] = jnp.where(is_text, dot(x[place, :], w_text[...]), before[place, :])

        for_text(info, cap, text)
        value, steep = gelu_parts(before[:rows, :])
        hid[0, :rows, :] = value.astype(BF)
        slope[0, :rows, :] = steep.astype(BF)
        if rows < cap:
            for ref in (hid, slope):
                ref[0, rows:, :] = jnp.zeros((cap - rows, ref.shape[2]), BF)

    for_rows(info, cap, body)


def mlp_back_kernel(
    info, g_own, g_oth, slope, upper_image, upper_text, lower_image, lower_text, gm_own, gm_oth, gb, g, back, result
):
    cap = g.shape[0]
    join(info, g_own, g_oth, g)

    def body(rows):
        back[:rows, :] = dot(g[:rows, :], lower_image[...]).astype(BF)

        def text(place, is_text):
            back[place, :] = jnp.where(is_text, dot(g[place, :], lower_text[...]).astype(BF), back[place, :])

        for_text(info, cap, text)
        gb[0, :rows, :] = (back[:rows, :].astype(F32) * slope[0, :rows, :].astype(F32)).astype(BF)
        if rows < cap:
            gb[0, rows:, :] = jnp.zeros((cap - rows, gb.shape[2]), BF)

    for_rows(info, cap, body)
    times_turned(info, gb.at[0], upper_image, upper_text, result)
    part_ways(info, result, gm_own, gm_oth)


def add_sums(info, left, right, acc_image, acc_text):
    cap = left.shape[0]
    j = pl.program_id(0)

    @pl.when(j == 0)
    def _():
        acc_image[...] = jnp.zeros_like(acc_image)
        acc_text[...] = jnp.zeros_like(acc_text)

    def body(rows):
        ids = row_ids(0, rows)
        is_text = (ids >= info[TEXT_FROM + j]) & (ids < info[TEXT_TO + j])
        is_image = (ids < info[COUNT + j]) & jnp.logical_not(is_text)
        acc_image[...] += dot_rows(left[:rows, :], jnp.where(is_image, right[:rows, :], jnp.zeros((), BF)))

    for_rows(info, cap, body)

    def text(place, is_text):
        acc_text[...] += dot_rows(left[place, :], jnp.where(is_text, right[place, :], jnp.zeros((), BF)))

    for_text(info, cap, text)


def give_sums(out, acc_image, acc_text):
    cut = acc_image.shape[1]

    @pl.when(pl.program_id(0) == BLOCKS - 1)
    def _():
        out[:, :cut] = acc_image[...].astype(BF)
        out[:, cut:] = acc_text[...].astype(BF)


def slot_sums_kernel(info, l_own, l_oth, right, out, acc_image, acc_text, left):
    join(info, l_own, l_oth, left)
    add_sums(info, left, right.at[0], acc_image, acc_text)
    give_sums(out, acc_image, acc_text)


def row_sums_kernel(info, l_own, l_oth, rows_ref, out, acc_image, acc_text, left, right):
    join(info, l_own, l_oth, left)

    def take(rows):
        right[:rows, :] = read_rows(rows_ref, info[OFFSET + pl.program_id(0)], rows)

    for_rows(info, left.shape[0], take)
    add_sums(info, left, right, acc_image, acc_text)
    give_sums(out, acc_image, acc_text)


def head_rows(turned, h):
    ids = lax.broadcasted_iota(jnp.int32, turned.shape, 0)
    return jnp.where((ids >= h * HEAD) & (ids < (h + 1) * HEAD), turned, 0)


def head_columns(plain, h):
    ids = lax.broadcasted_iota(jnp.int32, plain.shape, 1)
    return jnp.where((ids >= h * HEAD) & (ids < (h + 1) * HEAD), plain, 0)


def fold(combine, rows):
    parts = [rows[at : at + 8, :] for at in range(0, rows.shape[0], 8)]
    while len(parts) > 1:
        parts = [combine(a, b) for a, b in zip(parts[::2], parts[1::2])]
    return parts[0]


def slab_mask(chunks, i, n_chunks, low, q_from, q_to):
    position = chunks[i] + low + lax.broadcasted_iota(jnp.int32, (SLAB, 1), 0)
    valid = (position >= chunks[n_chunks + i]) & (position < chunks[2 * n_chunks + i])
    position = jnp.where(valid, position, -1)
    return (position >= q_from) & (position < q_to)


def for_chunks(chunks, n_chunks, t, body):
    low, high = chunks[3 * n_chunks + 2 * t], chunks[3 * n_chunks + 2 * t + 1]
    one = chunks[3 * n_chunks + 2 * pl.num_programs(0) + 2 + t] > 0

    def step(i, carry):
        base = chunks[i]
        start = jnp.maximum(base, chunks[n_chunks + i])
        stop = jnp.minimum(base + KEYS, chunks[2 * n_chunks + i])
        reached = (start < high) & (stop > low) & (start < stop)
        inside = one & (start == base) & (stop == base + KEYS) & (base >= low) & (stop <= high)

        @pl.when(reached & inside)
        def _():
            body(i, True)

        @pl.when(reached & jnp.logical_not(inside))
        def _():
            body(i, False)

        return carry

    lax.fori_loop(0, n_chunks, step, 0)


def sources_at(far_back, near_back, kv, near_on, far_on):
    chunk = 0
    for source, size, last in (
        (far_back, KEYS, True),
        (near_back, TAIL_PAD, True),
        (kv, kv.shape[0], False),
        (near_on, TAIL_PAD, False),
        (far_on, KEYS, False),
    ):
        rows = source.shape[0]
        skip = size - rows if last else 0
        for low in range(0, size, KEYS):
            first, stop = max(low, skip), min(low + KEYS, skip + rows)
            yield chunk, source, slice(first - skip, stop - skip), first - low, stop - low
            chunk += 1


def if_reached(chunks, n_chunks, i, body, otherwise=None):
    last = 3 * n_chunks + 3 * pl.num_programs(0) + 2
    start = jnp.maximum(chunks[i], chunks[n_chunks + i])
    stop = jnp.minimum(chunks[i] + KEYS, chunks[2 * n_chunks + i])
    reached = (start < chunks[last + 1]) & (stop > chunks[last]) & (start < stop)
    pl.when(reached)(body)
    if otherwise:
        pl.when(jnp.logical_not(reached))(otherwise)


def gather_keys(chunks, sources, k, v, plain, turned):
    n = k.shape[1]
    n_chunks = k.shape[0] // KEYS
    for i, source, rows, first, stop in sources_at(*sources):

        def take():
            at = i * KEYS
            for ref, columns in ((k, slice(0, n)), (v, slice(n, 2 * n))):
                ref[at + first : at + stop, :] = source[rows, columns]
                for low, high in ((0, first), (stop, KEYS)):
                    if low < high:
                        ref[at + low : at + high, :] = jnp.zeros((high - low, n), BF)
            part = slice(at, at + KEYS)
            turned[:, part] = plain[part, :].T

        if_reached(chunks, n_chunks, i, take)


def attend_kernel(
    chunks, seq, q, far_back, near_back, kv, near_on, far_on,
    out, exact, lse, top,
    k, v, v_turned, q_turn, logits, probs, total, high,
):
    t = pl.program_id(0)
    n_chunks = k.shape[0] // KEYS
    heads = q.shape[1] // HEAD
    wide = q.shape[0]

    @pl.when(t == 0)
    def _():
        gather_keys(chunks, (far_back, near_back, kv, near_on, far_on), k, v, v, v_turned)
        top[...] = jnp.full_like(top, NEGATIVE)

    live = chunks[3 * n_chunks + 2 * t + 1] > 0

    @pl.when(live)
    def _():
        turned = (q[...].astype(F32) * HEAD**-0.5).T
        for h in range(heads):
            q_turn[h] = head_rows(turned, h).astype(BF)
        lanes_from, lanes_to = lane_spans(chunks, seq, n_chunks, pl.num_programs(0), t)
        total[...] = jnp.zeros_like(total)
        high[...] = jnp.full_like(high, NEGATIVE)

        def first(i, whole_chunk):
            place = pl.ds(pl.multiple_of(i * KEYS, KEYS), KEYS)
            for h in range(heads):
                logits[h, i] = dot(k[place, :], q_turn[h])
            for low in range(0, KEYS, SLAB):
                part = slice(low, low + SLAB)
                if not whole_chunk:
                    mask = slab_mask(chunks, i, n_chunks, low, lanes_from, lanes_to)
                for h in range(heads):
                    values = logits[h, i, part, :]
                    if not whole_chunk:
                        values = jnp.where(mask, values, NEGATIVE)
                        logits[h, i, part, :] = values
                    rows = slice(8 * h, 8 * h + 8)
                    high[rows, :] = jnp.maximum(high[rows, :], fold(jnp.maximum, values))

        for_chunks(chunks, n_chunks, t, first)
        tops = [jnp.max(high[8 * h : 8 * h + 8, :], axis=0, keepdims=True) for h in range(heads)]
        high[...] = jnp.zeros_like(high)

        def second(i, whole_chunk):
            place = pl.ds(pl.multiple_of(i * KEYS, KEYS), KEYS)
            for low in range(0, KEYS, SLAB):
                part = slice(low, low + SLAB)
                for h in range(heads):
                    p = jnp.exp(logits[h, i, part, :] - tops[h])
                    rows = slice(8 * h, 8 * h + 8)
                    high[rows, :] += fold(jnp.add, p)
                    probs[part, h * wide : (h + 1) * wide] = p.astype(BF)
            for h in range(heads):
                rows = slice(h * HEAD, (h + 1) * HEAD)
                total[rows, :] += dot(v_turned[rows, place], probs[:, h * wide : (h + 1) * wide])

        for_chunks(chunks, n_chunks, t, second)
        for h in range(heads):
            rows = slice(h * HEAD, (h + 1) * HEAD)
            sums = jnp.sum(high[8 * h : 8 * h + 8, :], axis=0, keepdims=True)
            total[rows, :] = total[rows, :] / sums
            lse[0, h : h + 1, :] = tops[h] + jnp.log(sums)
            seen = jnp.where(lanes_to > lanes_from, tops[h], NEGATIVE)
            top[h : h + 1, :] = jnp.maximum(top[h : h + 1, :], seen)
        result = total[...].T
        exact[...] = result
        out[...] = result.astype(BF)

    @pl.when(jnp.logical_not(live))
    def _():
        exact[...] = jnp.zeros_like(exact)
        out[...] = jnp.zeros_like(out)
        lse[...] = jnp.zeros_like(lse)


def attend_back_kernel(
    chunks, seq, q, g, attended, far_back, near_back, kv, near_on, far_on, lse,
    dq, d_far_back, d_near_back, d_kv, d_near_on, d_far_on,
    k, v, k_turned, q_stack, g_stack, q_turn, g_turn, logits, grads_of, probs, grad_logits, total, dk, dv,
):
    t = pl.program_id(0)
    n_chunks = k.shape[0] // KEYS
    heads = q.shape[1] // HEAD
    wide = q.shape[0]

    @pl.when(t == 0)
    def _():
        gather_keys(chunks, (far_back, near_back, kv, near_on, far_on), k, v, k, k_turned)
        for i in range(n_chunks):

            def clear():
                dk[i * KEYS : (i + 1) * KEYS, :] = jnp.zeros((KEYS, dk.shape[1]), F32)
                dv[i * KEYS : (i + 1) * KEYS, :] = jnp.zeros((KEYS, dk.shape[1]), F32)

            if_reached(chunks, n_chunks, i, clear)

    live = chunks[3 * n_chunks + 2 * t + 1] > 0

    @pl.when(live)
    def _():
        scaled = q[...].astype(F32) * HEAD**-0.5
        grads = g[...].astype(F32)
        q_turned, g_turned = scaled.T, grads.T
        product = g_turned * attended[...].T
        delta, logs = [], []
        for h in range(heads):
            rows = slice(h * wide, (h + 1) * wide)
            q_stack[rows, :] = head_columns(scaled, h).astype(BF)
            g_stack[rows, :] = head_columns(grads, h).astype(BF)
            q_turn[h] = head_rows(q_turned, h).astype(BF)
            g_turn[h] = head_rows(g_turned, h).astype(BF)
            delta.append(jnp.sum(product[h * HEAD : (h + 1) * HEAD, :], axis=0, keepdims=True))
            logs.append(lse[0, h : h + 1, :])
        lanes_from, lanes_to = lane_spans(chunks, seq, n_chunks, pl.num_programs(0), t)
        total[...] = jnp.zeros_like(total)

        def body(i, whole_chunk):
            place = pl.ds(pl.multiple_of(i * KEYS, KEYS), KEYS)
            for h in range(heads):
                logits[h] = dot(k[place, :], q_turn[h])
                grads_of[h] = dot(v[place, :], g_turn[h])
            for low in range(0, KEYS, SLAB):
                part = slice(low, low + SLAB)
                if not whole_chunk:
                    mask = slab_mask(chunks, i, n_chunks, low, lanes_from, lanes_to)
                for h in range(heads):
                    lanes = slice(h * wide, (h + 1) * wide)
                    p = jnp.exp(logits[h, part, :] - logs[h])
                    if not whole_chunk:
                        p = jnp.where(mask, p, 0.0)
                    probs[part, lanes] = p.astype(BF)
                    grad_logits[part, lanes] = (p * (grads_of[h, part, :] - delta[h])).astype(BF)
            for h in range(heads):
                rows = slice(h * HEAD, (h + 1) * HEAD)
                total[rows, :] += dot(k_turned[rows, place], grad_logits[:, h * wide : (h + 1) * wide])
            dv[place, :] += dot(probs[...], g_stack[...])
            dk[place, :] += dot(grad_logits[...], q_stack[...])

        for_chunks(chunks, n_chunks, t, body)
        dq[...] = (total[...].T * HEAD**-0.5).astype(BF)

    @pl.when(jnp.logical_not(live))
    def _():
        dq[...] = jnp.zeros_like(dq)

    @pl.when(t == pl.num_programs(0) - 1)
    def _():
        n = dk.shape[1]
        for i, out, rows, first, stop in sources_at(d_far_back, d_near_back, d_kv, d_near_on, d_far_on):

            def give():
                place = slice(i * KEYS + first, i * KEYS + stop)
                out[rows, :n] = dk[place, :].astype(out.dtype)
                out[rows, n:] = dv[place, :].astype(out.dtype)

            def blank():
                out[rows, :] = jnp.zeros((stop - first, 2 * n), out.dtype)

            if_reached(chunks, n_chunks, i, give, blank)


def gather_grads_kernel(info, dq, d_kv, near_back, near_on, far_back, far_on, out, total):
    total[...] = d_kv[...].astype(F32)
    for start, part in ((info[TAIL_FROM], near_back), (info[EDGE_FROM], far_back)):
        place, skip = window(start, part.shape[0], total.shape[0])
        total[place, :] += moved(part[...], skip)
    for part in (near_on, far_on):
        total[: part.shape[0], :] += part[...].astype(F32)
    n = dq.shape[1]
    out[:, :n] = dq[...]
    out[:, n:] = total[...].astype(BF)


def copy_after(source, deps):
    return sum_after([source], source.dtype, deps)


def shift(value, steps):
    count = lax.axis_size("g")
    pairs = [(i, i + steps) for i in range(count) if 0 <= i + steps < count]
    if not pairs:
        return jnp.zeros_like(value)
    return lax.ppermute(value, "g", pairs)


def if_needed(predicate, run, *values):
    return lax.cond(predicate, run, lambda *v: tuple(jnp.zeros_like(a) for a in v), *values)


def over_x(value):
    return lax.ppermute(value, "x", SWAP)


def over_y(value):
    return lax.ppermute(value, "y", SWAP)


def over_core(value):
    return lax.ppermute(value, "c", SWAP)


def over_xy(value):
    return lax.ppermute(value, ("y", "x"), [(0, 3), (1, 2), (2, 1), (3, 0)])


def over_groups(sums):
    return lax.psum_scatter(sums, "g", scatter_dimension=0, tiled=True)


def spread_begin(value):
    return value, over_x(value), over_y(value)


def spread_next(begun, deps=()):
    value, from_x, from_y = begun
    cut = value.shape[0] // 2
    on_y, on_x = from_x[:cut], from_y[cut:]
    if deps:
        on_y, on_x = sum_after([on_y], BF, deps), sum_after([on_x], BF, deps)
    return value, from_x, from_y, on_y, on_x, over_y(on_y), over_x(on_x)


def spread_end(state, deps=()):
    value, from_x, from_y, _, _, low, high = state
    if deps:
        low, high = sum_after([low], BF, deps), sum_after([high], BF, deps)
    own = jnp.stack([value, from_x, from_y, jnp.concatenate([low, high], axis=0)])
    return own, over_core(own)


def spread(value, deps=()):
    return spread_end(spread_next(spread_begin(value), deps))


def add16(*parts):
    total = parts[0].astype(F32)
    for part in parts[1:]:
        total = total + part.astype(F32)
    return total


def core_sum(own, oth, deps=(), time=3):
    other = over_core(oth)
    half, width = own.shape[1:]
    cut = half // 2
    cuts = ((0, 0, half), (3, 0, cut), (3, cut, half), (1, 0, cut), (1, cut, half), (2, 0, cut), (2, cut, half))

    def body(*refs):
        for out, (j, low, high) in zip(refs[2:], cuts):
            out[...] = (refs[0][j, low:high, :].astype(F32) + refs[1][j, low:high, :].astype(F32)).astype(BF)

    return pl.pallas_call(
        after(body, 2, len(deps)),
        out_shape=tuple(jax.ShapeDtypeStruct((high - low, width), BF) for _, low, high in cuts),
        in_specs=[VMEM] * 2 + [ANY] * len(deps),
        out_specs=(VMEM,) * len(cuts),
        compiler_params=pltpu.CompilerParams(vmem_limit_bytes=VMEM_LIMIT),
        cost_estimate=took_us(time),
    )(own, other, *deps)


def collect_begin(pieces):
    mine, far_x, far_y, x_low, x_high, y_low, y_high = pieces
    from_x, from_y = over_x(far_x), over_y(far_y)
    return mine, x_high, y_low, from_x, from_y, over_x(x_low), over_y(y_high)


def collect_next(begun, deps=(), time=1):
    mine, x_high, y_low, from_x, from_y, first_x, first_y = begun
    on_x, on_y = sum_after((x_high, from_y), BF, deps, time), sum_after((y_low, from_x), BF, deps, time)
    return mine, first_x, first_y, on_x, on_y, over_x(on_x), over_y(on_y)


def sums_of_shares(shares, top_rows, g, q, deps):
    groups = lax.axis_size("g")
    pick = lambda values, at: lax.dynamic_index_in_dim(values, at, 0, keepdims=False)
    is_top = (jnp.arange(shares.shape[1]) >= shares.shape[1] - top_rows)[:, None]
    join = lambda a, b: jnp.where(is_top, jnp.maximum(a, b), a + b)
    shares = jnp.moveaxis(shares.reshape((groups, BLOCKS) + shares.shape[1:]), 1, 0)
    got = [over_x(pick(shares, q ^ 1)), over_y(pick(shares, q ^ 2)), over_xy(pick(shares, q ^ 3))]
    shares = join(join(pick(shares, q), got[0]), join(got[1], got[2]))
    shares = sum_after([shares], F32, deps)
    total = pick(shares, g)
    for step in range(1, groups):
        pairs = [(i, (i + step) % groups) for i in range(groups)]
        total = join(total, lax.ppermute(pick(shares, lax.rem(g + step, groups)), "g", pairs))
    return total


def pick_pieces(pieces, place, deps=()):
    shape = pieces.shape[1:]

    def body(place_ref, source, *outs):
        for j, out in enumerate(outs):
            out[...] = source[place_ref[1] ^ j]

    return pl.pallas_call(
        after(body, 2, len(deps)),
        out_shape=(jax.ShapeDtypeStruct(shape, pieces.dtype),) * BLOCKS,
        in_specs=[SMEM, VMEM] + [ANY] * len(deps),
        out_specs=(VMEM,) * BLOCKS,
        compiler_params=pltpu.CompilerParams(vmem_limit_bytes=VMEM_LIMIT),
        cost_estimate=took_us(2),
    )(place, pieces, *deps)


def swap_pieces(picked):
    own, to_x, to_y, to_xy = picked
    return own, over_x(to_x), over_y(to_y), over_xy(to_xy)


def pick_heads(image, text, place):
    share, parts, columns = image.shape
    n = columns // BLOCKS

    def body(place_ref, image_ref, text_ref, *outs):
        for j, out in enumerate(outs):
            for b in range(BLOCKS):

                @pl.when((place_ref[1] ^ j) == b)
                def _():
                    for k, source in enumerate((image_ref, text_ref)):
                        for p in range(parts):
                            at = (parts * k + p) * n
                            out[:, at : at + n] = source[p, :, b * n : (b + 1) * n]

    return pl.pallas_call(
        body,
        out_shape=(jax.ShapeDtypeStruct((share, 2 * parts * n), image.dtype),) * BLOCKS,
        in_specs=[SMEM, VMEM, VMEM],
        out_specs=(VMEM,) * BLOCKS,
        compiler_params=pltpu.CompilerParams(vmem_limit_bytes=VMEM_LIMIT),
        cost_estimate=took_us(2),
    )(place, jnp.swapaxes(image, 0, 1), jnp.swapaxes(text, 0, 1))


def arrange(got, place, body, out_shape, deps=(), time=2):
    n = len(got)

    def kernel(place_ref, *refs):
        for j in range(n):
            body(place_ref[1] ^ j, refs[j], refs[n:])

    return pl.pallas_call(
        after(kernel, 1 + n, len(deps)),
        out_shape=out_shape,
        in_specs=[SMEM] + [VMEM] * n + [ANY] * len(deps),
        out_specs=(VMEM,) * len(out_shape),
        compiler_params=pltpu.CompilerParams(vmem_limit_bytes=VMEM_LIMIT),
        cost_estimate=took_us(time),
    )(place, *got, *deps)


def stack_rows(b, piece, outs):
    rows, at = piece.shape[0], 0
    for out in outs:
        n = out.shape[1]
        out[pl.ds(pl.multiple_of(b * rows, ALIGN), rows), :] = piece[:, at : at + n]
        at += n


def give_wide(b, piece, outs):
    n = piece.shape[1] // 2
    for k, out in enumerate(outs):
        out[:, pl.ds(pl.multiple_of(b * n, SUB), n)] = piece[:, k * n : (k + 1) * n].astype(F32)


def give_qkv(b, piece, outs):
    n = piece.shape[1] // 6
    for at in range(BLOCKS):

        @pl.when(b == at)
        def _():
            for k, out in enumerate(outs):
                for p in range(3):
                    out[p, :, at * n : (at + 1) * n] = piece[:, (3 * k + p) * n : (3 * k + p + 1) * n].astype(F32)


def give_narrow(b, piece, outs):
    n = piece.shape[1] // 2
    for at in range(BLOCKS):

        @pl.when(b == at)
        def _():
            for k, out in enumerate(outs):
                out[:, at * n : (at + 1) * n] = piece[:, k * n : (k + 1) * n].astype(F32)


def local(
    tokens,
    cotangent,
    seq_offsets,
    block_offsets,
    image_mod,
    text_mod,
    image_qkv,
    text_qkv,
    image_out,
    text_out,
    image_fc1,
    text_fc1,
    image_fc2,
    text_fc2,
    clip_limits,
):
    rows_cap, width = tokens.shape
    half = rows_cap // 2
    share = image_qkv.shape[0]
    columns = image_qkv.shape[2]
    group_rows = BLOCKS * rows_cap
    mine = columns // BLOCKS
    fc = image_fc1.shape[1] // BLOCKS
    heads = mine // HEAD
    seq_count = seq_offsets.shape[0] - 1
    n_groups = lax.axis_size("g")
    g, c = lax.axis_index("g"), lax.axis_index("c")
    q = 2 * lax.axis_index("y") + lax.axis_index("x")

    def both_halves(rows):
        other = over_core(rows)
        return jnp.where(c == 0, jnp.concatenate([rows, other], axis=0), jnp.concatenate([other, rows], axis=0))

    def quarter_turned(inputs):
        return jnp.swapaxes(inputs.reshape(BLOCKS, -1, share), 1, 2)

    def quarter_wide(inputs):
        return jnp.swapaxes(inputs.reshape(share, BLOCKS, -1), 0, 1)

    place = jnp.stack([g, q, c]).astype(jnp.int32)
    plane_of = lambda *cuts: tuple(jax.ShapeDtypeStruct((BLOCKS * share, n), BF) for n in cuts)
    (plane_qkv,) = arrange(swap_pieces(pick_heads(image_qkv, text_qkv, place)), place, stack_rows, plane_of(6 * mine))

    n_tiles = group_rows // CHUNK
    reach = 2 * KEYS + 2 * TAIL_PAD + group_rows
    n_chunks = reach // KEYS
    info, chunks = pl.pallas_call(
        functools.partial(layout_kernel, group_rows),
        out_shape=(
            jax.ShapeDtypeStruct((INFO,), jnp.int32),
            jax.ShapeDtypeStruct((3 * n_chunks + 3 * n_tiles + 4,), jnp.int32),
        ),
        in_specs=[SMEM] * 3,
        out_specs=(SMEM, SMEM),
        cost_estimate=took_us(1),
    )(seq_offsets, block_offsets, place)

    my_rows = lambda inputs: lax.dynamic_slice_in_dim(inputs, c * half, half, 0)
    my_tokens, my_cotangent = my_rows(tokens), my_rows(cotangent)

    def rows_kernel(body, kinds, args, time, deps=(), extra=(), scratches=()):
        return pl.pallas_call(
            after(body, 1 + len(args), len(deps)),
            out_shape=tuple(jax.ShapeDtypeStruct((half, width), kind) for kind in kinds) + tuple(extra),
            in_specs=[SMEM] + [VMEM] * len(args) + [ANY] * len(deps),
            out_specs=(VMEM,) * (len(kinds) + len(extra)),
            scratch_shapes=list(scratches),
            compiler_params=pltpu.CompilerParams(vmem_limit_bytes=VMEM_LIMIT),
            cost_estimate=took_us(time),
        )(info, *args, *deps)

    parts_of = lambda state: (*state[:3], *state[5:])
    modulated, grad_mlp = rows_kernel(enter_kernel, (BF, BF), (tokens, cotangent, image_mod, text_mod), 4)

    slot = lambda n: jax.ShapeDtypeStruct((BLOCKS, half, n), BF)
    full = lambda n: jax.ShapeDtypeStruct((BLOCKS, rows_cap, n), BF)
    rows_of = lambda n, kind: jax.ShapeDtypeStruct((group_rows, n), kind)
    slot_block = block((half, width))
    scratch = lambda rows, n, kind=BF: pltpu.VMEM((rows, n), kind)
    weight_pair = lambda n: [scratch(width, n), scratch(width, n)]

    whole_qkv = lax.all_gather(plane_qkv, "g", axis=0, tiled=True)
    mod_begun = spread_begin(modulated)
    pack_rest = jnp.concatenate(
        [
            quarter_wide(image_fc1),
            quarter_wide(text_fc1),
            quarter_turned(image_fc2),
            quarter_turned(text_fc2),
            quarter_turned(image_out),
            quarter_turned(text_out),
        ],
        axis=2,
    )
    rest_picked = pick_pieces(pack_rest, place)
    rest_got = swap_pieces(rest_picked)
    mod_own, mod_oth = spread_end(spread_next(mod_begun, rest_picked[:1]), rest_got[1:])
    plane_fc1, plane_fc2, plane_out = arrange(rest_got, place, stack_rows, plane_of(2 * fc, 2 * fc, 2 * mine))
    whole_out = lax.all_gather(plane_out, "g", axis=0, tiled=True)
    whole_fc2 = lax.all_gather(plane_fc2, "g", axis=0, tiled=True)

    pair = lambda rows: jax.ShapeDtypeStruct((rows, 2 * mine), BF)
    queries, pairs, tail, edge, head, head_edge = stepped(
        project_kernel,
        BLOCKS,
        [SMEM, slot_block, slot_block, whole(whole_qkv.shape)],
        [kept(s) for s in ((group_rows, mine), (group_rows, 2 * mine), (TAIL, 2 * mine), (EDGE, 2 * mine), (TAIL, 2 * mine), (EDGE, 2 * mine))],
        (rows_of(mine, BF), pair(group_rows), pair(TAIL), pair(EDGE), pair(TAIL), pair(EDGE)),
        weight_pair(3 * mine) + [scratch(group_rows, 3 * mine), scratch(rows_cap, width), scratch(rows_cap, 3 * mine)],
        6,
    )(info, mod_own, mod_oth, whole_qkv)

    near_back, near_on = shift(tail, 1), shift(head, -1)
    gmlp_begun = spread_begin(copy_after(grad_mlp, (queries,)))
    fc1_piece = copy_after(plane_fc1, (near_back, near_on, *gmlp_begun[1:]))
    whole_fc1 = lax.all_gather(fc1_piece, "g", axis=0, tiled=True)
    gmlp_state = spread_next(gmlp_begun, (near_back, near_on, whole_out))
    gmlp_own, gmlp_oth = spread_end(gmlp_state)
    need_far = jnp.min(block_offsets[BLOCKS::BLOCKS] - block_offsets[:-1:BLOCKS]) < IMG + TXT
    far_back, far_on = if_needed(need_far, lambda a, b: (shift(a, 2), shift(b, -2)), edge, head_edge)
    sources = (far_back, near_back, pairs, near_on, far_on)
    source_specs = [whole(s.shape) for s in sources]

    tile_spec = pl.BlockSpec((CHUNK, mine), lambda t: (t, 0))
    log_spec = block((8, CHUNK))
    attended, attended_exact, logs, tops = stepped(
        attend_kernel,
        n_tiles,
        [SMEM, SMEM, tile_spec, *source_specs],
        (tile_spec, tile_spec, log_spec, kept((8, CHUNK))),
        (
            rows_of(mine, BF),
            rows_of(mine, F32),
            jax.ShapeDtypeStruct((n_tiles, 8, CHUNK), F32),
            jax.ShapeDtypeStruct((8, CHUNK), F32),
        ),
        [
            scratch(reach, mine),
            scratch(reach, mine),
            scratch(mine, reach),
            pltpu.VMEM((heads, mine, CHUNK), BF),
            pltpu.VMEM((heads, n_chunks, KEYS, CHUNK), F32),
            scratch(KEYS, heads * CHUNK),
            scratch(mine, CHUNK, F32),
            scratch(8 * heads, CHUNK, F32),
        ],
        1,
        (*gmlp_state[3:5], fc1_piece),
    )(chunks, seq_offsets, queries, *sources)

    def to_slots(n, first, rows, w, deps=(), time=10):
        return stepped(
            functools.partial(rows_to_slots_kernel, first),
            BLOCKS,
            [SMEM, whole(rows.shape), whole(w.shape)],
            (slot_block, slot_block),
            (slot(width), slot(width)),
            weight_pair(n) + [scratch(rows_cap, n), scratch(rows_cap, width)],
            time,
            deps,
        )(info, rows, w)

    branch_state = collect_next(collect_begin(core_sum(*to_slots(mine, 0, attended, whole_out, (), 1))), (whole_fc1,))
    branch, modulated_mlp = rows_kernel(
        middle_kernel, (F32, BF), (*parts_of(branch_state), my_tokens, image_mod, text_mod), 4, (gmlp_oth,)
    )
    mm_own, mm_oth = spread(modulated_mlp)
    fc_block = block((rows_cap, fc))
    hid, slope = stepped(
        mlp_up_kernel,
        BLOCKS,
        [SMEM, slot_block, slot_block, columns_from(width, fc, 0), columns_from(width, fc, 1)],
        (fc_block, fc_block),
        (full(fc), full(fc)),
        [scratch(rows_cap, width), scratch(rows_cap, fc, F32)],
        1,
    )(info, mm_own, mm_oth, whole_fc1, whole_fc1)

    def slot_sums(left, right, deps, time):
        return stepped(
            slot_sums_kernel,
            BLOCKS,
            [SMEM, slot_block, slot_block, fc_block],
            kept((width, 2 * fc)),
            jax.ShapeDtypeStruct((width, 2 * fc), BF),
            [scratch(width, fc, F32), scratch(width, fc, F32), scratch(rows_cap, width)],
            time,
            deps,
        )(info, *left, right)

    def row_sums(left, rows, deps=(), time=0.1):
        n = rows.shape[1]
        return stepped(
            row_sums_kernel,
            BLOCKS,
            [SMEM, slot_block, slot_block, whole(rows.shape)],
            kept((width, 2 * n)),
            jax.ShapeDtypeStruct((width, 2 * n), BF),
            [scratch(width, n, F32), scratch(width, n, F32), scratch(rows_cap, width), scratch(rows_cap, n)],
            time,
            deps,
        )(info, *left, rows)

    fc2_sums = slot_sums((gmlp_own, gmlp_oth), hid, (), 1)
    fc2_part = over_groups(fc2_sums)
    gm_own, gm_oth, gb = stepped(
        mlp_back_kernel,
        BLOCKS,
        [SMEM, slot_block, slot_block, fc_block] + [columns_from(width, fc, at) for at in (0, 1, 0, 1)],
        (slot_block, slot_block, fc_block),
        (slot(width), slot(width), full(fc)),
        [scratch(rows_cap, width), scratch(rows_cap, fc), scratch(rows_cap, width)],
        1,
        (fc2_sums,),
    )(info, gmlp_own, gmlp_oth, slope, whole_fc1, whole_fc1, whole_fc2, whole_fc2)

    gm_part = core_sum(gm_own, gm_oth)
    gm_state = collect_begin(gm_part)
    fc1_sums = slot_sums((mm_own, mm_oth), gb, gm_part, 12)
    fc1_part = over_groups(fc1_sums)
    gm_state = collect_next(gm_state, (fc1_sums,), 1)
    mlp_own, mlp_oth = stepped(
        slots_to_slots_kernel,
        BLOCKS,
        [SMEM, fc_block, columns_from(width, fc, 0), columns_from(width, fc, 1)],
        (slot_block, slot_block),
        (slot(width), slot(width)),
        [scratch(rows_cap, width)],
        25,
        gm_state[3:5],
    )(info, hid, whole_fc2, whole_fc2)
    grad_mod_mlp, grad_first, grad_branch = rows_kernel(
        turn_kernel,
        (F32, F32, BF),
        (*parts_of(gm_state), branch, my_tokens, my_cotangent, image_mod, text_mod),
        5,
        (mlp_own,),
    )
    gbr_begun = spread_begin(grad_branch)
    gbr_own, gbr_oth = spread_end(spread_next(gbr_begun, (fc2_part,)))
    grad_attended = stepped(
        functools.partial(back_project_kernel, 0),
        BLOCKS,
        [SMEM, slot_block, slot_block, whole(whole_out.shape)],
        kept((group_rows, mine)),
        rows_of(mine, BF),
        weight_pair(mine) + [scratch(rows_cap, width), scratch(rows_cap, mine)],
        1,
    )(info, gbr_own, gbr_oth, whole_out)

    mlp_part = core_sum(mlp_own, mlp_oth, (gbr_oth,), 3)
    mlp_state = collect_begin(mlp_part)
    dq, give_far_back, give_back, d_pairs, give_on, give_far_on = stepped(
        attend_back_kernel,
        n_tiles,
        [SMEM, SMEM, tile_spec, tile_spec, tile_spec, *source_specs, log_spec],
        (tile_spec, *(kept(s.shape) for s in sources)),
        (rows_of(mine, BF), pair(EDGE), pair(TAIL), pair(group_rows), pair(TAIL), pair(EDGE)),
        [
            scratch(reach, mine),
            scratch(reach, mine),
            scratch(mine, reach),
            scratch(heads * CHUNK, mine),
            scratch(heads * CHUNK, mine),
            pltpu.VMEM((heads, mine, CHUNK), BF),
            pltpu.VMEM((heads, mine, CHUNK), BF),
            pltpu.VMEM((heads, KEYS, CHUNK), F32),
            pltpu.VMEM((heads, KEYS, CHUNK), F32),
            scratch(KEYS, heads * CHUNK),
            scratch(KEYS, heads * CHUNK),
            scratch(mine, CHUNK, F32),
            scratch(reach, mine, F32),
            scratch(reach, mine, F32),
        ],
        1,
        (mlp_part[0],),
    )(chunks, seq_offsets, queries, grad_attended, attended_exact, *sources, logs)
    gave_back, gave_on = shift(give_back, -1), shift(give_on, 1)
    gave_far_back, gave_far_on = if_needed(
        need_far, lambda a, b: (shift(a, -2), shift(b, 2)), give_far_back, give_far_on
    )

    out_sums = row_sums((gbr_own, gbr_oth), attended, (dq,))
    out_part = over_groups(copy_after(out_sums, (gave_back, gave_on)))
    mlp_state = collect_next(mlp_state, (out_sums,), 1)
    pieces_of = lambda part, deps: pick_pieces(part.reshape(BLOCKS, share, -1), place, deps)
    grad_qkv = pl.pallas_call(
        after(gather_grads_kernel, 7, 2),
        out_shape=rows_of(3 * mine, BF),
        in_specs=[SMEM] + [VMEM] * 6 + [ANY] * 2,
        out_specs=VMEM,
        scratch_shapes=[scratch(group_rows, 2 * mine, F32)],
        compiler_params=pltpu.CompilerParams(vmem_limit_bytes=VMEM_LIMIT),
        cost_estimate=took_us(8),
    )(info, dq, d_pairs, gave_back, gave_on, gave_far_back, gave_far_on, out_sums, fc1_part)

    mod_sent = to_slots(3 * mine, 0, grad_qkv, whole_qkv, mlp_state[3:5], 0.1)
    qkv_sums = row_sums((mod_own, mod_oth), grad_qkv, (*mod_sent, *mlp_state[5:]), 14)
    qkv_part = over_groups(qkv_sums)
    mod_part = core_sum(*mod_sent, (qkv_sums,), 3)
    mod_state = collect_next(collect_begin(mod_part), mod_part[:1], 1)
    pair_f32 = lambda *shape: (jax.ShapeDtypeStruct(shape, F32),) * 2
    fc2_picked, fc1_picked = pieces_of(fc2_part, mod_state[3:5]), pieces_of(fc1_part, mod_state[3:5])
    out_picked = pieces_of(out_part, mod_state[3:5])
    fc2_got, fc1_got, out_got = swap_pieces(fc2_picked), swap_pieces(fc1_picked), swap_pieces(out_picked)
    tokens_grad_rows, mixed_rows, mod_sum = rows_kernel(
        leave_kernel,
        (F32, BF),
        (
            *parts_of(mod_state),
            *parts_of(mlp_state),
            grad_first,
            branch,
            grad_mod_mlp,
            my_tokens,
            my_cotangent,
            image_mod,
            text_mod,
        ),
        12,
        (fc2_picked[0], fc1_picked[0], out_picked[0]),
        (jax.ShapeDtypeStruct((2 * seq_count, 6, width), F32),),
        (scratch(half, width, F32), scratch(half, width, F32)),
    )
    mixed = both_halves(mixed_rows)
    qkv_got = swap_pieces(pieces_of(qkv_part, (mod_sum,)))
    fc2_outs = arrange(fc2_got, place, give_wide, pair_f32(share, BLOCKS * fc))
    fc1_outs = arrange(fc1_got, place, give_wide, pair_f32(share, BLOCKS * fc))
    out_outs = arrange(out_got, place, give_narrow, pair_f32(share, columns))
    qkv_outs = arrange(qkv_got, place, give_qkv, pair_f32(3, share, columns))
    mod_sum = mod_sum.reshape(2 * seq_count * 6, -1, share)
    mod_sum = jnp.swapaxes(mod_sum, 0, 1)
    mod_sum = mod_sum + over_core(mod_sum)
    head_top = jnp.max(tops[:heads], axis=1)
    spot = jnp.arange(BLOCKS)[:, None] == q
    head_top = jnp.where(spot, head_top[None, :], NEGATIVE).reshape(-1)
    n_heads = head_top.shape[0]
    head_top = jnp.pad(head_top, (0, -n_heads % share))[None, :]
    top_rows = -(-n_heads // share)
    head_top = jnp.broadcast_to(head_top.reshape(1, top_rows, share), (mod_sum.shape[0], top_rows, share))
    mod_sum = sums_of_shares(jnp.concatenate([mod_sum, head_top], axis=1), top_rows, g, q, qkv_got)
    head_max = mod_sum[-top_rows:].reshape(-1)[:n_heads]
    mod_sum = mod_sum[:-top_rows].reshape(2, seq_count, 6, share)
    root_factor = jnp.sqrt(clip_limits / jnp.maximum(head_max, clip_limits))
    column_scale = jnp.repeat(root_factor, HEAD)[None, None, :]
    clipped = tuple((w[:, :2, :].astype(F32) * column_scale).astype(BF) for w in (image_qkv, text_qkv))

    return (
        mixed,
        both_halves(tokens_grad_rows),
        mod_sum[0],
        mod_sum[1],
        *(jnp.swapaxes(part, 0, 1) for part in qkv_outs),
        *(part.T for part in out_outs),
        *fc1_outs,
        *(part.T for part in fc2_outs),
        head_max,
        *clipped,
    )


def solution(mesh):
    devices = mesh.devices
    split = Mesh(devices.reshape(devices.shape[0] // BLOCKS, 2, 2, devices.shape[1]), ("g", "y", "x", "c"))
    dp = ("g", "y", "x")
    placed = (
        P(dp, None),
        P(dp, None),
        P(),
        P(),
        P(),
        P(),
        P(dp, None, "c"),
        P(dp, None, "c"),
        P("c", dp),
        P("c", dp),
        P(dp, "c"),
        P(dp, "c"),
        P("c", dp),
        P("c", dp),
        P("c"),
    )
    return jax.shard_map(
        local,
        mesh=split,
        in_specs=placed,
        out_specs=(
            P(dp, None),
            P(dp, None),
            P(None, None, dp),
            P(None, None, dp),
            P(dp, None, "c"),
            P(dp, None, "c"),
            P("c", dp),
            P("c", dp),
            P(dp, "c"),
            P(dp, "c"),
            P("c", dp),
            P("c", dp),
            P("c"),
            P(dp, None, "c"),
            P(dp, None, "c"),
        ),
        check_vma=False,
    )
```
